32 devices in a mesh: batch: 2 (over y), branch: 2 (over core), tensor: 8 (over z, x).
Axes of the slice: x: 2, y: 2, z: 4, core: 2. Of those that a mesh axis runs over, the one named last changes fastest.
Arguments:
- tokens: bfloat16 [2, 8, 1024, 2048], P(None, ('batch', 'branch'), 'tensor'), may hold values from -6 to 6
- cotangent: bfloat16 [2, 8, 1024, 2048], P(None, ('batch', 'branch'), 'tensor'), may hold values from -6 to 6
- segments: int32 [2, 8, 1024], P(None, ('batch', 'branch')), may hold values from 0 to 3, as said below
- positions: int32 [2, 8, 1024], P(None, ('batch', 'branch')), may hold values from 0 to 1023, as said below
- ln_gain: float32 [2048], replicated, may hold values from 0.5 to 1.5
- ln_bias: float32 [2048], replicated, may hold values from -1.25 to 1.25
- qkv_weight: bfloat16 [2048, 3, 2048], P(('batch', 'branch'), None, 'tensor'), may hold values from -0.125 to 0.125
- qkv_bias: float32 [3, 2048], P(None, 'tensor'), may hold values from -1.25 to 1.25
- dense_weight: bfloat16 [2048, 2048], P('tensor', ('batch', 'branch')), may hold values from -0.5 to 0.5
- dense_bias: float32 [2048], replicated, may hold values from -1.75 to 1.75
- up_weight: bfloat16 [2048, 8192], P(('batch', 'branch'), 'tensor'), may hold values from -0.125 to 0.125
- up_bias: float32 [8192], P('tensor'), may hold values from -1.75 to 1.75
- down_weight: bfloat16 [8192, 2048], P('tensor', ('batch', 'branch')), may hold values from -0.0625 to 0.0625
- down_bias: float32 [2048], replicated, may hold values from -1.75 to 1.75
Outputs:
- mixed: bfloat16 [2, 8, 1024, 2048], P(None, ('batch', 'branch'), 'tensor')
- tokens_grad: float32 [2, 8, 1024, 2048], P(None, ('batch', 'branch'), 'tensor')
- ln_gain_grad: float32 [2048], replicated
- ln_bias_grad: float32 [2048], replicated
- qkv_weight_grad: float32 [2048, 3, 2048], P(('batch', 'branch'), None, 'tensor')
- qkv_bias_grad: float32 [3, 2048], P(None, 'tensor')
- dense_weight_grad: float32 [2048, 2048], P('tensor', ('batch', 'branch'))
- dense_bias_grad: float32 [2048], replicated
- up_weight_grad: float32 [2048, 8192], P(('batch', 'branch'), 'tensor')
- up_bias_grad: float32 [8192], P('tensor')
- down_weight_grad: float32 [8192, 2048], P('tensor', ('batch', 'branch'))
- down_bias_grad: float32 [2048], replicated
The draws below stay inside these ranges and needn't reach their ends.
Inputs may be any that keep to these rules, and one draw needn't show every extreme that they name: `segments`: each sequence holds four documents numbered 0 to 3 in order, none empty. Within a document positions rise by one from token to token; the first document of each sequence starts at 0; the last token of each sequence has position 1023.
All inputs are finite; a program needn't handle non-finite values.
Results may differ from the reference program's by a relative error of at most 0.012.
Values may be sent and summed in bfloat16 or wider, within the bound.
No kernel may reach another device: no remote copies, remote signals or barrier semaphores. Data moves between devices by JAX's collectives and lax.ppermute only.
A program may use at most 384 MiB of HBM per device.

```python
import jax
import jax.numpy as jnp
from jax import lax

D = 2048
HEADS = 32
HEAD_DIM = 64
ROT = 32
FF = 8192
MB = 2
L = 1024
NSEQ = 8
SHARD_ROWS = 128


def document_layout(key):
    short_key, long_key, offset_key = jax.random.split(key, 3)
    short_len = jax.random.randint(short_key, (MB, NSEQ, 3), 1, 1 + SHARD_ROWS // 4)
    long_slot = jax.random.randint(long_key, (MB, NSEQ, 1), 0, 4)
    slot_ids = jnp.arange(4, dtype=jnp.int32)
    padded = jnp.concatenate([short_len, short_len[..., :1]], axis=-1)
    shifted = jnp.concatenate([short_len[..., :1], short_len], axis=-1)
    short_at = jnp.where(slot_ids < long_slot, padded, shifted)
    long_len = L - jnp.sum(short_len, -1, keepdims=True)
    lengths = jnp.where(slot_ids == long_slot, long_len, short_at).astype(jnp.int32)
    doc_ends = jnp.cumsum(lengths, -1)
    starts = doc_ends - lengths
    token_place = jnp.arange(L, dtype=jnp.int32)
    doc_ids = jnp.sum((token_place[None, None, :, None] >= doc_ends[:, :, None, :3]).astype(jnp.int32), -1)
    offsets = jax.random.randint(offset_key, (MB, NSEQ, 4), 0, L - lengths + 1)
    offsets = jnp.where(slot_ids == 0, 0, offsets)
    offsets = jnp.where(slot_ids == 3, L - lengths, offsets)
    one_hot = (doc_ids[..., None] == slot_ids).astype(jnp.int32)
    positions = jnp.sum(one_hot * (offsets - starts)[:, :, None, :], -1) + token_place
    return (doc_ids.astype(jnp.int32), positions.astype(jnp.int32))


def draw_segments(key, part):
    return document_layout(key)[0]


def draw_positions(key, part):
    return document_layout(key)[1]


def shard_levels(key, extent, shards, smallest, top_value):
    loudness, own = 1.0, jax.random.fold_in(key, 6)
    for axis_at, shards_of in shards:
        steps = jnp.exp(jax.random.uniform(jax.random.fold_in(own, axis_at), (shards_of,), jnp.float32, smallest / len(shards), top_value / len(shards)))
        loudness = loudness * jnp.repeat(steps, extent[axis_at] // shards_of).reshape([-1 if axis == axis_at else 1 for axis in range(len(extent))])
    return loudness


def gaussian(key, shape, scale, most, pieces=(), kind=jnp.bfloat16):
    values = scale * jax.random.normal(key, shape, jnp.float32)
    if pieces:
        values = values * shard_levels(key, shape, pieces, -0.22, 0.18)
    return jnp.clip(values, -most, most).astype(kind)


def setup_inputs(seed: int = 0) -> dict:
    arg_keys = jax.random.split(jax.random.key(seed), 15)
    return {
        "tokens": gaussian(arg_keys[0], (MB, NSEQ, L, D), 1.0, 6.0, ((1, 4), (2, 8))),
        "cotangent": gaussian(arg_keys[1], (MB, NSEQ, L, D), 1.0, 6.0, ((1, 4), (2, 8))),
        "segments": draw_segments(jax.random.fold_in(arg_keys[14], 71), 0),
        "positions": draw_positions(jax.random.fold_in(arg_keys[14], 71), 0),
        "ln_gain": jnp.clip(1.0 + 0.1 * jax.random.normal(arg_keys[4], (D,), jnp.float32), 0.5, 1.5),
        "ln_bias": gaussian(arg_keys[5], (D,), 0.2, 1.25, (), jnp.float32),
        "qkv_weight": gaussian(arg_keys[6], (D, 3, D), D ** -0.5, 0.125, ((0, 4), (2, 8))),
        "qkv_bias": gaussian(arg_keys[7], (3, D), 0.2, 1.25, ((1, 8),), jnp.float32),
        "dense_weight": gaussian(arg_keys[8], (D, D), (D // 16) ** -0.5, 0.5, ((0, 8), (1, 4))),
        "dense_bias": gaussian(arg_keys[9], (D,), 0.3, 1.75, (), jnp.float32),
        "up_weight": gaussian(arg_keys[10], (D, FF), D ** -0.5, 0.125, ((0, 4), (1, 8))),
        "up_bias": gaussian(arg_keys[11], (FF,), 0.3, 1.75, ((0, 8),), jnp.float32),
        "down_weight": gaussian(arg_keys[12], (FF, D), FF ** -0.5, 0.0625, ((0, 8), (1, 4))),
        "down_bias": gaussian(arg_keys[13], (D,), 0.3, 1.75, (), jnp.float32),
    }


@jax.custom_vjp
def low(v):
    return lax.optimization_barrier(v.astype(jnp.bfloat16)).astype(jnp.float32)

@jax.custom_vjp
def low_back(v):
    return v

def low_keep(v):
    return (low(v), None)

def low_pass(kept, grad):
    return (grad,)

def back_keep(v):
    return (v, None)

def back_low(kept, grad):
    return (low(grad),)
low.defvjp(low_keep, low_pass)
low_back.defvjp(back_keep, back_low)
eps_norm = 1e-05
rope_base = 10000.0
masked_score = -1e+30
highest = lax.Precision.HIGHEST

def rope_tables(token_place):
    half_dims = ROT // 2
    exponent = jnp.arange(half_dims, dtype=jnp.float32) * (2.0 / ROT)
    inverse = rope_base ** (-exponent)
    angles = token_place.astype(jnp.float32)[..., None] * inverse
    return (jnp.cos(angles), jnp.sin(angles))

def rotate(values, cosine, sine_table):
    half_dims = ROT // 2
    lower_half = values[..., :half_dims]
    upper_half = values[..., half_dims:ROT]
    cos_wide = cosine[..., None, :]
    sin_wide = sine_table[..., None, :]
    return jnp.concatenate([lower_half * cos_wide - upper_half * sin_wide, upper_half * cos_wide + lower_half * sin_wide, values[..., ROT:]], axis=-1)

def attend(queries, key_heads, value_heads, segment):
    block_rows = min(512, L)
    query_blocks = queries.reshape(L // block_rows, block_rows, HEADS, HEAD_DIM)
    row_index = jnp.arange(L, dtype=jnp.int32).reshape(L // block_rows, block_rows)
    seg_blocks = segment.reshape(L // block_rows, block_rows)
    columns = jnp.arange(L, dtype=jnp.int32)

    def per_block(inputs):
        query_block, row_ids, seg_ids = inputs
        scores = jnp.einsum('qhe,khe->hqk', query_block, key_heads, precision=highest) * HEAD_DIM ** (-0.5)
        allowed = (columns[None, :] <= row_ids[:, None]) & (seg_ids[:, None] == segment[None, :])
        scores = low_back(jnp.where(allowed[None], scores, masked_score))
        row_max = lax.optimization_barrier(jnp.max(scores, -1, keepdims=True))
        exponent = jnp.exp(scores - row_max)
        probs_low = low(exponent / lax.optimization_barrier(jnp.sum(exponent, -1, keepdims=True)))
        return jnp.einsum('hqk,khe->qhe', probs_low, value_heads, precision=highest)
    blocks = lax.map(jax.checkpoint(per_block), (query_blocks, row_index, seg_blocks))
    return blocks.reshape(L, HEADS, HEAD_DIM)

def layer(params, tokens_seq, segment, token_place):
    ln_gain, ln_bias, qkv_weight, qkv_bias, dense_weight, dense_bias, up_weight, up_bias, down_weight, down_bias = params
    row_mean = lax.optimization_barrier(jnp.mean(tokens_seq, -1, keepdims=True))
    centered = tokens_seq - row_mean
    variance = lax.optimization_barrier(jnp.mean(centered * centered, -1, keepdims=True))
    normed = low(centered * lax.rsqrt(variance + eps_norm) * ln_gain + ln_bias)
    projected = jnp.einsum('ld,dce->lce', normed, qkv_weight, precision=highest) + qkv_bias
    projected = low_back(projected)
    cosine, sine_table = rope_tables(token_place)
    queries = low(rotate(projected[:, 0].reshape(L, HEADS, HEAD_DIM), cosine, sine_table))
    key_heads = low(rotate(projected[:, 1].reshape(L, HEADS, HEAD_DIM), cosine, sine_table))
    value_heads = low(projected[:, 2].reshape(L, HEADS, HEAD_DIM))
    attn_out = attend(queries, key_heads, value_heads, segment)
    attn_out = low(low_back(attn_out)).reshape(L, D)
    hidden_pre = low_back(jnp.dot(normed, up_weight, precision=highest) + up_bias)
    activated = low(jax.nn.gelu(hidden_pre, approximate=True))
    return tokens_seq + jnp.dot(attn_out, dense_weight, precision=highest) + dense_bias + jnp.dot(activated, down_weight, precision=highest) + down_bias

def reference(tokens, cotangent, segments, positions, ln_gain, ln_bias, qkv_weight, qkv_bias, dense_weight, dense_bias, up_weight, up_bias, down_weight, down_bias):
    params = tuple((item.astype(jnp.float32) for item in (ln_gain, ln_bias, qkv_weight, qkv_bias, dense_weight, dense_bias, up_weight, up_bias, down_weight, down_bias)))
    flat_tokens = tokens.astype(jnp.float32).reshape(MB * NSEQ, L, D)
    flat_grads = cotangent.astype(jnp.float32).reshape(MB * NSEQ, L, D)
    flat_segments = segments.reshape(MB * NSEQ, L).astype(jnp.int32)
    flat_positions = positions.reshape(MB * NSEQ, L).astype(jnp.int32)
    zero_grads = jax.tree.map(jnp.zeros_like, params)

    def per_sequence(running, inputs):
        tokens_seq, grad_seq, segment, token_place = inputs

        def apply_layer(weights, values):
            return layer(weights, values, segment, token_place)
        output, pull_back = jax.vjp(apply_layer, params, tokens_seq)
        param_grads, token_grads = pull_back(grad_seq)
        running = jax.tree.map(jnp.add, running, param_grads)
        return (running, (output.astype(jnp.bfloat16), token_grads))
    totals, (outputs, token_grads) = lax.scan(per_sequence, zero_grads, (flat_tokens, flat_grads, flat_segments, flat_positions))
    mixed = outputs.reshape(MB, NSEQ, L, D)
    tokens_grad = token_grads.reshape(MB, NSEQ, L, D)
    return (mixed, tokens_grad, totals[0], totals[1], totals[2], totals[3], totals[4], totals[5], totals[6], totals[7], totals[8], totals[9])
```

```python
from functools import partial

import jax
import jax.numpy as jnp
from jax import lax
from jax.experimental import pallas as pl
from jax.experimental.pallas import tpu as pltpu
from jax.sharding import Mesh
from jax.sharding import PartitionSpec as P

HEAD_DIM = 64
ROT = 32
LANES = 128
VMEM = 60 * 2**20

eps_norm = 1e-05
rope_base = 10000.0
masked_score = -1e30
f32 = jnp.float32
bf16 = jnp.bfloat16

NN = (((1,), (0,)), ((), ()))
NT = (((1,), (1,)), ((), ()))
TN = (((0,), (0,)), ((), ()))


def mm(a, b, dims=NN):
    return lax.dot_general(a, b, dims, preferred_element_type=f32)


def rope_tables(token_place):
    full_len = token_place.shape[0]
    half = ROT // 2
    inverse = rope_base ** (-(jnp.arange(half, dtype=f32) * (2.0 / ROT)))
    angles = token_place.astype(f32)[:, None] * inverse
    c, s = jnp.cos(angles), jnp.sin(angles)
    rest = (full_len, HEAD_DIM - ROT)
    zero_half = jnp.zeros((full_len, half), f32)
    cos = jnp.concatenate([c, c, jnp.ones(rest, f32)], 1)
    sa = jnp.concatenate([-s, zero_half, jnp.zeros(rest, f32)], 1)
    sb = jnp.concatenate([zero_half, s, jnp.zeros(rest, f32)], 1)
    return tuple(jnp.tile(t, (1, LANES // HEAD_DIM)) for t in (cos, sa, sb))


def attn_kernel(
    q_ref, k_ref, v_ref, qb_ref, kb_ref, vb_ref, cos_ref, sa_ref, sb_ref, ga_ref, segr_ref, segc_ref,
    out_ref, dp_ref, db_ref, dk_acc, dv_acc,
):
    full_len = q_ref.shape[0]
    size = min(256, full_len)
    half = ROT // 2
    heads = LANES // HEAD_DIM
    cos, sa, sb = cos_ref[...], sa_ref[...], sb_ref[...]

    def rope(x):
        return x * cos + pltpu.roll(x, LANES - half, 1) * sa + pltpu.roll(x, half, 1) * sb

    def unrope(g):
        return g * cos + pltpu.roll(g * sa, half, 1) + pltpu.roll(g * sb, LANES - half, 1)

    lane = lax.broadcasted_iota(jnp.int32, (1, LANES), 1)
    q = (rope(q_ref[...] + qb_ref[...]) * (HEAD_DIM**-0.5)).astype(bf16)
    k = rope(k_ref[...] + kb_ref[...]).astype(bf16)
    v = (v_ref[...] + vb_ref[...]).astype(bf16)
    do = ga_ref[...]
    k_t = k.astype(f32).T.astype(bf16)
    v_t = v.astype(f32).T.astype(bf16)
    do_t = do.astype(f32).T
    tri = lax.broadcasted_iota(jnp.int32, (size, size), 0) <= lax.broadcasted_iota(jnp.int32, (size, size), 1)
    zero = jnp.zeros((), bf16)
    dq_blocks = []
    for j in range(full_len // size):
        cols = slice(j * size, (j + 1) * size)
        seg_q = segr_ref[:, cols]
        out_rows, dq_rows, queries, grads = [], [], [], []
        low = [[None] * heads for _ in range(j + 1)]
        gs = [[None] * heads for _ in range(j + 1)]
        for h in range(heads):
            mine = (lane >= h * HEAD_DIM) & (lane < (h + 1) * HEAD_DIM)
            span = slice(h * HEAD_DIM, (h + 1) * HEAD_DIM)
            qh = jnp.where(mine, q[cols], zero)
            gh = jnp.where(mine, do[cols], zero)
            queries.append(qh)
            grads.append(gh)
            tiles, top, total, out, dq = [], None, None, None, None
            for i in range(j + 1):
                rows = slice(i * size, (i + 1) * size)
                ok = segc_ref[rows] == seg_q
                if i == j:
                    ok = ok & tri
                s = jnp.where(ok, mm(k[rows], qh, NT), masked_score)
                m = jnp.max(s, 0, keepdims=True)
                top = m if top is None else jnp.maximum(top, m)
                tiles.append(s)
            for i in range(j + 1):
                tiles[i] = jnp.exp(tiles[i] - top)
                t = jnp.sum(tiles[i], 0, keepdims=True)
                total = t if total is None else total + t
            inverse = 1.0 / total
            for i in range(j + 1):
                tiles[i] = tiles[i] * inverse
                low[i][h] = tiles[i].astype(bf16)
                t = mm(v_t[span, i * size : (i + 1) * size], low[i][h])
                out = t if out is None else out + t
            inner = jnp.sum(out * do_t[span, cols], 0, keepdims=True)
            for i in range(j + 1):
                dprob = mm(v[i * size : (i + 1) * size], gh, NT)
                gs[i][h] = (tiles[i] * (dprob - inner)).astype(bf16)
                t = mm(k_t[span, i * size : (i + 1) * size], gs[i][h])
                dq = t if dq is None else dq + t
            out_rows.append(out)
            dq_rows.append(dq)
        for i in range(j + 1):
            rows = slice(i * size, (i + 1) * size)
            dv = sum(mm(low[i][h], grads[h]) for h in range(heads))
            dk = sum(mm(gs[i][h], queries[h]) for h in range(heads))
            if i == j:
                dv_acc[rows] = dv
                dk_acc[rows] = dk
            else:
                dv_acc[rows] += dv
                dk_acc[rows] += dk
        out_ref[cols] = jnp.concatenate(out_rows, 0).T.astype(bf16)
        dq_blocks.append((jnp.concatenate(dq_rows, 0) * (HEAD_DIM**-0.5)).T)
    dq = unrope(jnp.concatenate(dq_blocks, 0)).astype(bf16)
    dk = unrope(dk_acc[...]).astype(bf16)
    dv = dv_acc[...].astype(bf16)
    for part, g in enumerate((dq, dk, dv)):
        dp_ref[part] = g
        db_ref[part : part + 1] = jnp.sum(g.astype(f32), 0, keepdims=True)


def attention(proj, bias, tables, grad_attn, segment):
    full_len, wide = proj.shape
    width = wide // 3
    pairs = width // LANES
    bias = bias.reshape(1, wide)

    def part(c):
        return pl.BlockSpec((full_len, LANES), lambda p: (0, c * pairs + p))

    def bias_part(c):
        return pl.BlockSpec((1, LANES), lambda p: (0, c * pairs + p))

    def whole(*shape):
        return pl.BlockSpec(shape, lambda p: (0, 0))

    table = whole(full_len, LANES)
    cols = pl.BlockSpec((full_len, LANES), lambda p: (0, p))
    return pl.pallas_call(
        attn_kernel,
        grid=(pairs,),
        in_specs=[part(0), part(1), part(2), bias_part(0), bias_part(1), bias_part(2), table, table, table, cols,
                  whole(1, full_len), whole(full_len, 1)],
        out_specs=[cols, pl.BlockSpec((3, full_len, LANES), lambda p: (0, 0, p)), pl.BlockSpec((8, LANES), lambda p: (0, p))],
        out_shape=[
            jax.ShapeDtypeStruct((full_len, width), bf16),
            jax.ShapeDtypeStruct((3, full_len, width), bf16),
            jax.ShapeDtypeStruct((8, width), f32),
        ],
        scratch_shapes=[pltpu.VMEM((full_len, LANES), f32), pltpu.VMEM((full_len, LANES), f32)],
        compiler_params=pltpu.CompilerParams(vmem_limit_bytes=VMEM),
        name="attention",
    )(proj, proj, proj, bias, bias, bias, *tables, grad_attn, segment.reshape(1, -1), segment.reshape(-1, 1))


def mlp_kernel(n_ref, c_ref, up_ref, down_ref, bias_ref, act_ref, pre_ref, sum_ref):
    rows = n_ref.shape[0]
    step = min(256, rows)
    k0 = 0.7978845608028654
    k1 = k0 * 0.044715
    total = None
    for i in range(rows // step):
        at = slice(i * step, (i + 1) * step)
        v = mm(n_ref[at], up_ref[...]) + bias_ref[...]
        g = mm(c_ref[at], down_ref[...], NT)
        v2 = v * v
        t = jnp.tanh(v * (k0 + k1 * v2))
        h = 0.5 * t + 0.5
        act_ref[at] = (v * h).astype(bf16)
        slope = h + v * (1.0 - t * t) * (0.5 * k0 + 1.5 * k1 * v2)
        p = (g * slope).astype(bf16)
        pre_ref[at] = p
        s = jnp.sum(p.astype(f32), 0, keepdims=True)
        total = s if total is None else total + s
    sum_ref[...] = jnp.broadcast_to(total, sum_ref.shape)


def mlp(n, c, up, down, bias):
    rows, depth = n.shape
    hidden = up.shape[1]
    br, bh = min(1024, rows), min(512, hidden)
    row = pl.BlockSpec((br, depth), lambda j, i: (i, 0))
    out = pl.BlockSpec((br, bh), lambda j, i: (i, j))
    act, pre, sums = pl.pallas_call(
        mlp_kernel,
        grid=(hidden // bh, rows // br),
        in_specs=[row, row, pl.BlockSpec((depth, bh), lambda j, i: (0, j)), pl.BlockSpec((bh, depth), lambda j, i: (j, 0)),
                  pl.BlockSpec((1, bh), lambda j, i: (0, j))],
        out_specs=[out, out, pl.BlockSpec((8, bh), lambda j, i: (i, j))],
        out_shape=[
            jax.ShapeDtypeStruct((rows, hidden), bf16),
            jax.ShapeDtypeStruct((rows, hidden), bf16),
            jax.ShapeDtypeStruct((rows // br * 8, hidden), f32),
        ],
        compiler_params=pltpu.CompilerParams(vmem_limit_bytes=VMEM),
        name="mlp",
    )(n, c, up, down, bias.reshape(1, hidden))
    return act, pre, jnp.sum(sums.reshape(-1, 8, hidden)[:, 0], 0)


def mixed_kernel(act_ref, attn_ref, down_ref, dense_ref, out_ref):
    rows = act_ref.shape[0]
    step = min(512, rows)
    for i in range(rows // step):
        at = slice(i * step, (i + 1) * step)
        out_ref[at] = (mm(act_ref[at], down_ref[...]) + mm(attn_ref[at], dense_ref[...])).astype(bf16)


def mixed_part(act, attn, down, dense):
    rows, hidden = act.shape
    width = attn.shape[1]
    depth = down.shape[1]
    br, bn = min(1024, rows), min(1024, depth)
    return pl.pallas_call(
        mixed_kernel,
        grid=(depth // bn, rows // br),
        in_specs=[pl.BlockSpec((br, hidden), lambda j, i: (i, 0)), pl.BlockSpec((br, width), lambda j, i: (i, 0)),
                  pl.BlockSpec((hidden, bn), lambda j, i: (0, j)), pl.BlockSpec((width, bn), lambda j, i: (0, j))],
        out_specs=pl.BlockSpec((br, bn), lambda j, i: (i, j)),
        out_shape=jax.ShapeDtypeStruct((rows, depth), bf16),
        compiler_params=pltpu.CompilerParams(vmem_limit_bytes=VMEM),
        name="mixed_part",
    )(act, attn, down, dense)


def back_kernel(pre_ref, dp_ref, up_ref, qkv_ref, out_ref):
    rows = pre_ref.shape[0]
    step = min(512, rows)
    for i in range(rows // step):
        at = slice(i * step, (i + 1) * step)
        total = mm(pre_ref[at], up_ref[...], NT)
        for c in range(3):
            total = total + mm(dp_ref[c, at], qkv_ref[c], NT)
        out_ref[at] = total.astype(bf16)


def back_part(pre, dp, up, qkv):
    rows, hidden = pre.shape
    width = dp.shape[2]
    depth = up.shape[0]
    br, bn = min(1024, rows), min(1024, depth)
    return pl.pallas_call(
        back_kernel,
        grid=(depth // bn, rows // br),
        in_specs=[pl.BlockSpec((br, hidden), lambda j, i: (i, 0)), pl.BlockSpec((3, br, width), lambda j, i: (0, i, 0)),
                  pl.BlockSpec((bn, hidden), lambda j, i: (j, 0)), pl.BlockSpec((3, bn, width), lambda j, i: (0, j, 0))],
        out_specs=pl.BlockSpec((br, bn), lambda j, i: (i, j)),
        out_shape=jax.ShapeDtypeStruct((rows, depth), bf16),
        compiler_params=pltpu.CompilerParams(vmem_limit_bytes=VMEM),
        name="back_part",
    )(pre, dp, up, qkv)


def weight_grad(x, y, split_rows, split_cols):
    rows, m = x.shape
    n = y.shape[1]
    bm, bn = m // split_rows, n // split_cols
    tile = min(bn, 512)

    def kernel(x_ref, y_ref, out_ref):
        out_ref[...] = mm(x_ref[...], y_ref[...], TN).astype(bf16).reshape(out_ref.shape)

    return pl.pallas_call(
        kernel,
        grid=(n // tile,),
        in_specs=[pl.BlockSpec((rows, m), lambda j: (0, 0), pipeline_mode=pl.Buffered(1)), pl.BlockSpec((rows, tile), lambda j: (0, j))],
        out_specs=pl.BlockSpec((split_rows, 1, bm, tile), lambda j: (0, j // (bn // tile), 0, j % (bn // tile))),
        out_shape=jax.ShapeDtypeStruct((split_rows, split_cols, bm, bn), bf16),
        compiler_params=pltpu.CompilerParams(vmem_limit_bytes=VMEM),
        name="weight_grad",
    )(x, y)


def body(
    tokens,
    cotangent,
    segments,
    positions,
    ln_gain,
    ln_bias,
    qkv_weight,
    qkv_bias,
    dense_weight,
    dense_bias,
    up_weight,
    up_bias,
    down_weight,
    down_bias,
):
    micros, seqs, shard, depth = tokens.shape
    full_len = segments.shape[2]
    parts, width = qkv_weight.shape[1:]
    hidden = up_weight.shape[1]
    quarter = qkv_weight.shape[0]
    quarters = depth // quarter
    fold = ("batch", "branch")
    mine = lax.axis_index("near")
    first = mine == 0
    swap = [(0, 1), (1, 0)]

    def to_group(a):
        got = lax.ppermute(jnp.where(first, a[1], a[0]), "near", swap)
        kept = jnp.where(first, a[0], a[1])
        return jnp.concatenate([jnp.where(first, kept, got), jnp.where(first, got, kept)], 1)

    def from_group(a):
        lo, hi = a[:, :shard], a[:, shard:]
        got = lax.ppermute(jnp.where(first, hi, lo), "near", swap)
        kept = jnp.where(first, lo, hi)
        return jnp.stack([jnp.where(first, kept, got), jnp.where(first, got, kept)], 0)

    cot_group = to_group(cotangent)
    residual = tokens.astype(f32)
    centered = residual - jnp.mean(residual, -1, keepdims=True)
    scale = lax.rsqrt(jnp.mean(centered * centered, -1, keepdims=True) + eps_norm)
    unit = centered * scale
    normed = (unit * ln_gain + ln_bias).astype(bf16)
    normed_group = to_group(normed)

    spread = ("near",) + fold
    qkv_all = lax.all_gather(qkv_weight.transpose(1, 0, 2), spread, axis=0, tiled=False)
    up_all = lax.all_gather(up_weight, spread, axis=0, tiled=False)
    down_all = lax.all_gather(down_weight, spread, axis=0, tiled=False)
    dense_all = lax.all_gather(dense_weight, spread, axis=0, tiled=False)
    qkv = qkv_all.reshape(2, quarters, parts, quarter, width).transpose(2, 1, 3, 0, 4).reshape(parts, depth, 2 * width)
    up = up_all.reshape(2, depth, hidden).transpose(1, 0, 2).reshape(depth, 2 * hidden)
    down = down_all.reshape(2, quarters, hidden, quarter).transpose(0, 2, 1, 3).reshape(2 * hidden, depth)
    dense = dense_all.reshape(2, quarters, width, quarter).transpose(0, 2, 1, 3).reshape(2 * width, depth)
    bias_qkv = lax.all_gather(qkv_bias, "near", axis=1, tiled=True)
    bias_up = lax.all_gather(up_bias, "near", axis=0, tiled=True)
    segment = jnp.where(first, segments[0], segments[1])
    place = jnp.where(first, positions[0], positions[1])

    rows_n, rows_c, acts, pres, attns, dps = [], [], [], [], [], []
    mixed_sums, back_sums = [], []
    sum_qkv, sum_up = 0.0, 0.0
    for s in range(seqs):
        n = lax.all_gather(normed_group[s], "line", axis=0, tiled=True)
        c = lax.all_gather(cot_group[s], "line", axis=0, tiled=True)
        proj = jnp.concatenate([mm(n, qkv[p]) for p in range(parts)], 1)
        grad_attn = mm(c, dense, NT).astype(bf16)
        attn, dp, db = attention(proj, bias_qkv, rope_tables(place[s]), grad_attn, segment[s])
        act, pre, up_sum = mlp(n, c, up, down, bias_up)
        mixed_sums.append(lax.psum_scatter(mixed_part(act, attn, down, dense), "line", scatter_dimension=0, tiled=True))
        back_sums.append(lax.psum_scatter(back_part(pre, dp, up, qkv), "line", scatter_dimension=0, tiled=True))
        sum_qkv = sum_qkv + db[:parts]
        sum_up = sum_up + up_sum
        rows_n.append(n)
        rows_c.append(c)
        acts.append(act)
        pres.append(pre)
        attns.append(attn)
        dps.append(dp)
    rows_n, rows_c, acts, pres, attns = (jnp.concatenate(a, 0) for a in (rows_n, rows_c, acts, pres, attns))
    dps = jnp.concatenate(dps, 1)

    def scatter(g):
        return lax.psum_scatter(g.reshape(2 * quarters, *g.shape[2:]), spread, scatter_dimension=0, tiled=False)

    grad_down = scatter(weight_grad(acts, rows_c, 2, quarters)).astype(f32)
    grad_up = weight_grad(rows_n, pres, quarters, 2)
    grad_up = scatter(grad_up.transpose(1, 0, 2, 3)).astype(f32)
    grad_dense = scatter(weight_grad(attns, rows_c, 2, quarters)).astype(f32)
    grad_qkv = jnp.stack([weight_grad(rows_n, dps[p], quarters, 1)[:, 0] for p in range(parts)], 1)
    grad_qkv = grad_qkv.reshape(quarters, parts, quarter, 2, width).transpose(3, 0, 1, 2, 4)
    grad_qkv = scatter(grad_qkv).transpose(1, 0, 2).astype(f32)

    summed = from_group(jnp.stack(mixed_sums, 0))
    mixed = (residual + summed.astype(f32) + dense_bias + down_bias).astype(bf16)
    grad_normed = from_group(jnp.stack(back_sums, 0)).astype(f32)
    w = grad_normed * ln_gain
    tokens_grad = cotangent.astype(f32) + scale * (
        w - jnp.mean(w, -1, keepdims=True) - unit * jnp.mean(w * unit, -1, keepdims=True)
    )
    everyone = fold + ("line", "near")
    gain_grad, shift_grad, out_bias_grad = lax.psum(
        (
            jnp.sum(grad_normed * unit, (0, 1, 2)),
            jnp.sum(grad_normed, (0, 1, 2)),
            jnp.sum(cotangent, (0, 1, 2), dtype=f32),
        ),
        everyone,
    )
    bias_sums = lax.psum((sum_qkv, sum_up), spread)
    qkv_bias_grad = lax.dynamic_slice_in_dim(bias_sums[0], mine * width, width, 1)
    up_bias_grad = lax.dynamic_slice_in_dim(bias_sums[1], mine * hidden, hidden, 0)
    return (
        mixed,
        tokens_grad,
        gain_grad,
        shift_grad,
        grad_qkv,
        qkv_bias_grad,
        grad_dense,
        out_bias_grad,
        grad_up,
        up_bias_grad,
        grad_down,
        out_bias_grad,
    )


def solution(mesh):
    batch, branch, tensor = (mesh.shape[a] for a in ("batch", "branch", "tensor"))
    inner = Mesh(mesh.devices.reshape(batch, branch, tensor // 2, 2), ("batch", "branch", "line", "near"))
    fold = ("batch", "branch")
    tensor = ("line", "near")
    rows = P(None, fold, tensor, None)
    first = P(fold, None, tensor)
    weights = (first, P(None, tensor), P(tensor, fold), P(), P(fold, tensor), P(tensor), P(tensor, fold), P())
    return jax.shard_map(
        body,
        mesh=inner,
        in_specs=(rows, rows, P(None, fold, None), P(None, fold, None), P(), P(), *weights),
        out_specs=(rows, rows, P(), P(), *weights),
        check_vma=False,
    )
```

```python
from functools import partial

import jax
import jax.numpy as jnp
from jax import lax
from jax.experimental import pallas as pl
from jax.experimental.pallas import tpu as pltpu
from jax.sharding import Mesh
from jax.sharding import PartitionSpec as P

HEAD_DIM = 64
ROT = 32
LANES = 128
VMEM = 60 * 2**20
COST = {"attention": 100, "attention_grad": 23, "mlp_act": 17, "mlp_pre": 14, "mixed_part": 16, "back_part": 22, "weight_grad": 100,
        "heads_grad": 28, "project": 9, "line_step": 3, "assemble": 8, "assemble_heads": 14}


def cost(units):
    return pl.CostEstimate(flops=units * 250000000 + 1, bytes_accessed=units * 250000 + 1, transcendentals=0)


eps_norm = 1e-05
rope_base = 10000.0
masked_score = -1e30
f32 = jnp.float32
bf16 = jnp.bfloat16

NN = (((1,), (0,)), ((), ()))
NT = (((1,), (1,)), ((), ()))
TN = (((0,), (0,)), ((), ()))


def mm(a, b, dims=NN):
    return lax.dot_general(a, b, dims, preferred_element_type=f32)


def call(kernel, deps, args, *, grid, in_specs, out_specs, out_shape, name, scratch=(), prefetch=0):
    deps = list(deps)
    inputs = prefetch + len(in_specs)

    def run(*refs):
        kernel(*refs[:inputs], *refs[inputs + len(deps) :])

    spec = pltpu.PrefetchScalarGridSpec(
        num_scalar_prefetch=prefetch,
        grid=grid,
        in_specs=list(in_specs) + [pl.BlockSpec(memory_space=pl.ANY)] * len(deps),
        out_specs=out_specs,
        scratch_shapes=list(scratch),
    )
    return pl.pallas_call(
        run,
        grid_spec=spec,
        out_shape=out_shape,
        compiler_params=pltpu.CompilerParams(vmem_limit_bytes=VMEM),
        cost_estimate=cost(COST[name]),
        name=name,
    )(*args, *deps)


def tie(a, *deps, units=0):
    return pl.pallas_call(
        lambda *refs: None,
        in_specs=[pl.BlockSpec(memory_space=pl.ANY)] * (1 + len(deps)),
        out_specs=pl.BlockSpec(memory_space=pl.ANY),
        out_shape=jax.ShapeDtypeStruct(a.shape, a.dtype),
        input_output_aliases={0: 0},
        cost_estimate=cost(units),
        name="tie",
    )(a, *deps)


def project_kernel(a_ref, w_ref, out_ref):
    rows = a_ref.shape[0]
    step = min(512, rows)
    for i in range(rows // step):
        at = slice(i * step, (i + 1) * step)
        out_ref[at] = mm(a_ref[at], w_ref[...]).astype(out_ref.dtype)


def project(a, w, dtype, deps=()):
    rows, depth = a.shape
    cols = w.shape[1]
    bn = 256 if cols % 256 == 0 else 128
    return call(
        project_kernel,
        deps,
        (a, w),
        grid=(cols // bn,),
        in_specs=[pl.BlockSpec((rows, depth), lambda j: (0, 0)), pl.BlockSpec((depth, bn), lambda j: (0, j))],
        out_specs=pl.BlockSpec((rows, bn), lambda j: (0, j)),
        out_shape=jax.ShapeDtypeStruct((rows, cols), dtype),
        name="project",
    )


def rope_tables(token_place):
    full_len = token_place.shape[0]
    half = ROT // 2
    inverse = rope_base ** (-(jnp.arange(half, dtype=f32) * (2.0 / ROT)))
    angles = token_place.astype(f32)[:, None] * inverse
    c, s = jnp.cos(angles), jnp.sin(angles)
    rest = (full_len, HEAD_DIM - ROT)
    zero_half = jnp.zeros((full_len, half), f32)
    cos = jnp.concatenate([c, c, jnp.ones(rest, f32)], 1)
    sa = jnp.concatenate([-s, zero_half, jnp.zeros(rest, f32)], 1)
    sb = jnp.concatenate([zero_half, s, jnp.zeros(rest, f32)], 1)
    return tuple(jnp.tile(t, (1, LANES // HEAD_DIM)) for t in (cos, sa, sb))


def attn_kernel(
    q_ref, k_ref, v_ref, qb_ref, kb_ref, vb_ref, cos_ref, sa_ref, sb_ref, segr_ref, segc_ref, out_ref, keep_ref, log_ref
):
    full_len = q_ref.shape[0]
    size = min(256, full_len)
    half = ROT // 2
    heads = LANES // HEAD_DIM
    cos, sa, sb = cos_ref[...], sa_ref[...], sb_ref[...]

    def rope(x):
        return x * cos + pltpu.roll(x, LANES - half, 1) * sa + pltpu.roll(x, half, 1) * sb

    lane = lax.broadcasted_iota(jnp.int32, (1, LANES), 1)
    q = (rope(q_ref[...] + qb_ref[...]) * (HEAD_DIM**-0.5)).astype(bf16)
    k = rope(k_ref[...] + kb_ref[...]).astype(bf16)
    v = (v_ref[...] + vb_ref[...]).astype(bf16)
    keep_ref[0] = q
    keep_ref[1] = k
    keep_ref[2] = v
    v_t = v.astype(f32).T.astype(bf16)
    tri = lax.broadcasted_iota(jnp.int32, (size, size), 0) <= lax.broadcasted_iota(jnp.int32, (size, size), 1)
    zero = jnp.zeros((), bf16)
    for j in range(full_len // size):
        cols = slice(j * size, (j + 1) * size)
        seg_q = segr_ref[:, cols]
        out_rows = []
        for h in range(heads):
            mine = (lane >= h * HEAD_DIM) & (lane < (h + 1) * HEAD_DIM)
            span = slice(h * HEAD_DIM, (h + 1) * HEAD_DIM)
            qh = jnp.where(mine, q[cols], zero)
            tiles, top, total, out = [], None, None, None
            for i in range(j + 1):
                rows = slice(i * size, (i + 1) * size)
                ok = segc_ref[rows] == seg_q
                if i == j:
                    ok = ok & tri
                s = jnp.where(ok, mm(k[rows], qh, NT), masked_score)
                m = jnp.max(s, 0, keepdims=True)
                top = m if top is None else jnp.maximum(top, m)
                tiles.append(s)
            for i in range(j + 1):
                e = jnp.exp(tiles[i] - top)
                t = jnp.sum(e, 0, keepdims=True)
                total = t if total is None else total + t
                t = mm(v_t[span, i * size : (i + 1) * size], e.astype(bf16))
                out = t if out is None else out + t
            out_rows.append(out * (1.0 / total))
            log_ref[h : h + 1, cols] = top + jnp.log(total)
        out_ref[cols] = jnp.concatenate(out_rows, 0).T.astype(bf16)


def attention(proj, bias, tables, segment, deps=()):
    full_len, wide = proj.shape
    width = wide // 3
    pairs = width // LANES
    bias = bias.reshape(1, wide)

    def part(c):
        return pl.BlockSpec((full_len, LANES), lambda p: (0, c * pairs + p))

    def bias_part(c):
        return pl.BlockSpec((1, LANES), lambda p: (0, c * pairs + p))

    def whole(*shape):
        return pl.BlockSpec(shape, lambda p: (0, 0))

    table = whole(full_len, LANES)
    return call(
        attn_kernel,
        deps,
        (proj, proj, proj, bias, bias, bias, *tables, segment.reshape(1, -1), segment.reshape(-1, 1)),
        grid=(pairs,),
        in_specs=[part(0), part(1), part(2), bias_part(0), bias_part(1), bias_part(2), table, table, table,
                  whole(1, full_len), whole(full_len, 1)],
        out_specs=[
            pl.BlockSpec((full_len, LANES), lambda p: (0, p)),
            pl.BlockSpec((3, full_len, LANES), lambda p: (0, 0, p)),
            pl.BlockSpec((8, full_len), lambda p: (p, 0)),
        ],
        out_shape=[
            jax.ShapeDtypeStruct((full_len, width), bf16),
            jax.ShapeDtypeStruct((3, full_len, width), bf16),
            jax.ShapeDtypeStruct((8 * pairs, full_len), f32),
        ],
        name="attention",
    )


def attn_grad_kernel(
    keep_ref, log_ref, ao_ref, ga_ref, cos_ref, sa_ref, sb_ref, segr_ref, segc_ref, dp_ref, db_ref, dk_acc, dv_acc
):
    full_len = ao_ref.shape[0]
    size = min(256, full_len)
    half = ROT // 2
    heads = LANES // HEAD_DIM
    cos, sa, sb = cos_ref[...], sa_ref[...], sb_ref[...]

    def unrope(g):
        return g * cos + pltpu.roll(g * sa, half, 1) + pltpu.roll(g * sb, LANES - half, 1)

    lane = lax.broadcasted_iota(jnp.int32, (1, LANES), 1)
    q, k, v, do = keep_ref[0], keep_ref[1], keep_ref[2], ga_ref[...]
    k_t = k.astype(f32).T.astype(bf16)
    inner_t = (do.astype(f32) * ao_ref[...].astype(f32)).T
    tri = lax.broadcasted_iota(jnp.int32, (size, size), 0) <= lax.broadcasted_iota(jnp.int32, (size, size), 1)
    zero = jnp.zeros((), bf16)
    dq_blocks = []
    for j in range(full_len // size):
        cols = slice(j * size, (j + 1) * size)
        seg_q = segr_ref[:, cols]
        spans, masks, queries, grads, logs, inners = [], [], [], [], [], []
        for h in range(heads):
            mine = (lane >= h * HEAD_DIM) & (lane < (h + 1) * HEAD_DIM)
            spans.append(slice(h * HEAD_DIM, (h + 1) * HEAD_DIM))
            queries.append(jnp.where(mine, q[cols], zero))
            grads.append(jnp.where(mine, do[cols], zero))
            logs.append(log_ref[h : h + 1, cols])
            inners.append(jnp.sum(inner_t[spans[h], cols], 0, keepdims=True))
        dq = [None] * heads
        for i in range(j + 1):
            rows = slice(i * size, (i + 1) * size)
            ok = segc_ref[rows] == seg_q
            if i == j:
                ok = ok & tri
            dv = dk = None
            for h in range(heads):
                p = jnp.exp(jnp.where(ok, mm(k[rows], queries[h], NT) - logs[h], masked_score))
                g = (p * (mm(v[rows], grads[h], NT) - inners[h])).astype(bf16)
                t = mm(p.astype(bf16), grads[h])
                dv = t if dv is None else dv + t
                t = mm(g, queries[h])
                dk = t if dk is None else dk + t
                t = mm(k_t[spans[h], rows], g)
                dq[h] = t if dq[h] is None else dq[h] + t
            if i == j:
                dv_acc[rows] = dv
                dk_acc[rows] = dk
            else:
                dv_acc[rows] += dv
                dk_acc[rows] += dk
        dq_blocks.append((jnp.concatenate(dq, 0) * (HEAD_DIM**-0.5)).T)
    dq = unrope(jnp.concatenate(dq_blocks, 0)).astype(bf16)
    dk = unrope(dk_acc[...]).astype(bf16)
    dv = dv_acc[...].astype(bf16)
    for part, g in enumerate((dq, dk, dv)):
        dp_ref[part] = g
        db_ref[part : part + 1] = jnp.sum(g.astype(f32), 0, keepdims=True)


def attention_grad(keep, logs, attn, grad_attn, tables, segment, deps=()):
    _, full_len, width = keep.shape

    def whole(*shape):
        return pl.BlockSpec(shape, lambda p: (0, 0))

    table = whole(full_len, LANES)
    cols = pl.BlockSpec((full_len, LANES), lambda p: (0, p))
    three = pl.BlockSpec((3, full_len, LANES), lambda p: (0, 0, p))
    return call(
        attn_grad_kernel,
        deps,
        (keep, logs, attn, grad_attn, *tables, segment.reshape(1, -1), segment.reshape(-1, 1)),
        grid=(width // LANES,),
        in_specs=[three, pl.BlockSpec((8, full_len), lambda p: (p, 0)), cols, cols, table, table, table,
                  whole(1, full_len), whole(full_len, 1)],
        out_specs=[three, pl.BlockSpec((8, LANES), lambda p: (0, p))],
        out_shape=[jax.ShapeDtypeStruct((3, full_len, width), bf16), jax.ShapeDtypeStruct((8, width), f32)],
        scratch=[pltpu.VMEM((full_len, LANES), f32), pltpu.VMEM((full_len, LANES), f32)],
        name="attention_grad",
    )


def act_kernel(n_ref, up_ref, bias_ref, act_ref, slope_ref):
    rows = n_ref.shape[0]
    step = min(256, rows)
    k0 = 0.7978845608028654
    k1 = k0 * 0.044715
    for i in range(rows // step):
        at = slice(i * step, (i + 1) * step)
        v = mm(n_ref[at], up_ref[...]) + bias_ref[...]
        v2 = v * v
        t = jnp.tanh(v * (k0 + k1 * v2))
        h = 0.5 * t + 0.5
        act_ref[at] = (v * h).astype(bf16)
        slope_ref[at] = (h + v * (1.0 - t * t) * (0.5 * k0 + 1.5 * k1 * v2)).astype(bf16)


def mlp_act(n, up, bias, deps=()):
    rows, depth = n.shape
    near, _, hidden = up.shape
    br, bh = min(1024, rows), min(512, hidden)
    per = hidden // bh
    out = pl.BlockSpec((br, bh), lambda j, i: (i, j))
    shape = jax.ShapeDtypeStruct((rows, near * hidden), bf16)
    return call(
        act_kernel,
        deps,
        (n, up, bias.reshape(1, -1)),
        grid=(near * per, rows // br),
        in_specs=[pl.BlockSpec((br, depth), lambda j, i: (i, 0)),
                  pl.BlockSpec((None, depth, bh), lambda j, i: (j // per, 0, j % per)),
                  pl.BlockSpec((1, bh), lambda j, i: (0, j))],
        out_specs=[out, out],
        out_shape=[shape, shape],
        name="mlp_act",
    )


def pre_kernel(c_ref, down_ref, slope_ref, pre_ref, sum_ref):
    rows = c_ref.shape[0]
    step = min(256, rows)
    total = None
    for i in range(rows // step):
        at = slice(i * step, (i + 1) * step)
        p = (mm(c_ref[at], down_ref[...]) * slope_ref[at].astype(f32)).astype(bf16)
        pre_ref[at] = p
        s = jnp.sum(p.astype(f32), 0, keepdims=True)
        total = s if total is None else total + s
    sum_ref[...] = jnp.broadcast_to(total, sum_ref.shape)


def mlp_pre(c, down_t, slope, deps=()):
    rows, depth = c.shape
    near, _, hidden = down_t.shape
    br, bh = min(1024, rows), min(512, hidden)
    per = hidden // bh
    out = pl.BlockSpec((br, bh), lambda j, i: (i, j))
    pre, sums = call(
        pre_kernel,
        deps,
        (c, down_t, slope),
        grid=(near * per, rows // br),
        in_specs=[pl.BlockSpec((br, depth), lambda j, i: (i, 0)),
                  pl.BlockSpec((None, depth, bh), lambda j, i: (j // per, 0, j % per)), out],
        out_specs=[out, pl.BlockSpec((8, bh), lambda j, i: (i, j))],
        out_shape=[
            jax.ShapeDtypeStruct((rows, near * hidden), bf16),
            jax.ShapeDtypeStruct((rows // br * 8, near * hidden), f32),
        ],
        name="mlp_pre",
    )
    return pre, jnp.sum(sums.reshape(-1, 8, near * hidden)[:, 0], 0)


def mixed_kernel(act_ref, attn_ref, down_ref, dense_ref, out_ref):
    rows = act_ref.shape[0]
    near, _, hidden = down_ref.shape
    step = min(512, rows)
    for i in range(rows // step):
        at = slice(i * step, (i + 1) * step)
        total = mm(attn_ref[at], dense_ref[...], NT)
        for r in range(near):
            total = total + mm(act_ref[at, r * hidden : (r + 1) * hidden], down_ref[r], NT)
        out_ref[at] = total.astype(bf16)


def mixed_part(act, attn, down_t, dense_t, deps=()):
    rows = act.shape[0]
    width = attn.shape[1]
    near, depth, hidden = down_t.shape
    br, bn = min(1024, rows), min(512, depth)
    return call(
        mixed_kernel,
        deps,
        (act, attn, down_t, dense_t),
        grid=(depth // bn, rows // br),
        in_specs=[pl.BlockSpec((br, near * hidden), lambda j, i: (i, 0)), pl.BlockSpec((br, width), lambda j, i: (i, 0)),
                  pl.BlockSpec((near, bn, hidden), lambda j, i: (0, j, 0)), pl.BlockSpec((bn, width), lambda j, i: (j, 0))],
        out_specs=pl.BlockSpec((br, bn), lambda j, i: (i, j)),
        out_shape=jax.ShapeDtypeStruct((rows, depth), bf16),
        name="mixed_part",
    )


def back_kernel(pre_ref, dp_ref, up_ref, qkv_ref, n_ref, out_ref, sum_ref):
    rows = pre_ref.shape[0]
    near, _, hidden = up_ref.shape
    parts, _, width = dp_ref.shape
    step = min(512, rows)
    plain = scaled = None
    for i in range(rows // step):
        at = slice(i * step, (i + 1) * step)
        total = None
        for r in range(near):
            t = mm(pre_ref[at, r * hidden : (r + 1) * hidden], up_ref[r], NT)
            total = t if total is None else total + t
        for c in range(parts):
            total = total + mm(dp_ref[c, at], qkv_ref[:, c * width : (c + 1) * width], NT)
        out_ref[at] = total.astype(bf16)
        a = jnp.sum(total, 0, keepdims=True)
        b = jnp.sum(total * n_ref[at].astype(f32), 0, keepdims=True)
        plain = a if plain is None else plain + a
        scaled = b if scaled is None else scaled + b
    sum_ref[0:1] = plain
    sum_ref[1:2] = scaled


def back_part(pre, dp, up, qkv, n, deps=()):
    rows = pre.shape[0]
    parts, _, width = dp.shape
    near, depth, hidden = up.shape
    br, bn = min(1024, rows), min(512, depth)
    out, sums = call(
        back_kernel,
        deps,
        (pre, dp, up, qkv, n),
        grid=(depth // bn, rows // br),
        in_specs=[pl.BlockSpec((br, near * hidden), lambda j, i: (i, 0)), pl.BlockSpec((parts, br, width), lambda j, i: (0, i, 0)),
                  pl.BlockSpec((near, bn, hidden), lambda j, i: (0, j, 0)), pl.BlockSpec((bn, parts * width), lambda j, i: (j, 0)),
                  pl.BlockSpec((br, bn), lambda j, i: (i, j))],
        out_specs=[pl.BlockSpec((br, bn), lambda j, i: (i, j)), pl.BlockSpec((8, bn), lambda j, i: (i, j))],
        out_shape=[jax.ShapeDtypeStruct((rows, depth), bf16), jax.ShapeDtypeStruct((rows // br * 8, depth), f32)],
        name="back_part",
    )
    return out, jnp.sum(sums.reshape(-1, 8, depth)[:, :2], 0)


def store_quarters(at_ref, total, held, keep_ref, send_ref):
    held[...] = total.astype(bf16)
    rows = held.shape[0] // 4
    y, core = at_ref[0], at_ref[1]
    for d in range(2):
        row = 2 * (1 - y if d else y)
        keep_ref[d] = held[pl.ds(pl.multiple_of((row + core) * rows, rows), rows)]
        send_ref[d] = held[pl.ds(pl.multiple_of((row + 1 - core) * rows, rows), rows)]


def weight_grad(at, xs, ys, deps=()):
    rows, m = xs[0].shape
    hidden = ys[0].shape[1] // 2
    tile = min(hidden, 512)
    per = hidden // tile
    count = len(xs)

    def kernel(at_ref, *refs):
        total = None
        for x, y in zip(refs[:count], refs[count : 2 * count], strict=True):
            t = mm(x[...], y[...], TN)
            total = t if total is None else total + t
        keep_ref, send_ref, held = refs[2 * count :]
        store_quarters(at_ref, total, held, keep_ref, send_ref)

    x_spec = pl.BlockSpec((rows, m), lambda j, at: (0, 0), pipeline_mode=pl.Buffered(1))
    y_spec = pl.BlockSpec((rows, tile), lambda j, at: (0, j))
    out = pl.BlockSpec((None, 2, m // 4, tile), lambda j, at: (j // per, 0, 0, j % per))
    shape = jax.ShapeDtypeStruct((2, 2, m // 4, hidden), bf16)
    return call(
        kernel,
        deps,
        (at, *xs, *ys),
        grid=(2 * per,),
        in_specs=[x_spec] * count + [y_spec] * count,
        out_specs=[out, out],
        out_shape=[shape, shape],
        scratch=[pltpu.VMEM((m, tile), bf16)],
        prefetch=1,
        name="weight_grad",
    )


def heads_grad(at, ns, dps, cs, attns, deps=()):
    parts, rows, wide = dps[0].shape
    m = ns[0].shape[1]
    width = wide // 2
    count = len(ns)
    out_cols = (parts + 1) * width
    if width % LANES:
        blocks = [sum(mm(n, dp[c], TN) for n, dp in zip(ns, dps, strict=True)) for c in range(parts)]
        blocks.append(sum(mm(c, a, TN) for c, a in zip(cs, attns, strict=True)))
        g = jnp.stack([jnp.concatenate([b[:, r * width : (r + 1) * width] for b in blocks], 1) for r in range(2)], 0)
        g = g.astype(bf16).reshape(2, 2, 2, m // 4, out_cols)
        g = jnp.where(at[0] == 0, g, g[:, ::-1])
        return jnp.where(at[1] == 0, g[:, :, 0], g[:, :, 1]), jnp.where(at[1] == 0, g[:, :, 1], g[:, :, 0])

    def kernel(at_ref, *refs):
        n_refs, dp_refs, c_refs, a_refs = (refs[i * count : (i + 1) * count] for i in range(4))
        keep_ref, send_ref, held = refs[4 * count :]
        part = pl.program_id(0)

        def store(total):
            for d in range(2):
                store_quarters(at_ref, total[:, d * width : (d + 1) * width], held, keep_ref.at[d], send_ref.at[d])

        @pl.when(part < parts)
        def _():
            store(sum(mm(n[...], d[...], TN) for n, d in zip(n_refs, dp_refs, strict=True)))

        @pl.when(part == parts)
        def _():
            store(sum(mm(c[...], a[...], TN) for c, a in zip(c_refs, a_refs, strict=True)))

    x_spec = pl.BlockSpec((rows, m), lambda p, at: (0, 0), pipeline_mode=pl.Buffered(1))
    dp_spec = pl.BlockSpec((None, rows, wide), lambda p, at: (jnp.minimum(p, parts - 1), 0, 0))
    a_spec = pl.BlockSpec((rows, wide), lambda p, at: (0, 0))
    out = pl.BlockSpec((2, 2, m // 4, width), lambda p, at: (0, 0, 0, p))
    shape = jax.ShapeDtypeStruct((2, 2, m // 4, out_cols), bf16)
    return call(
        kernel,
        deps,
        (at, *ns, *dps, *cs, *attns),
        grid=(parts + 1,),
        in_specs=[x_spec] * count + [dp_spec] * count + [x_spec] * count + [a_spec] * count,
        out_specs=[out, out],
        out_shape=[shape, shape],
        scratch=[pltpu.VMEM((m, width), bf16)],
        prefetch=1,
        name="heads_grad",
    )


SWAP = [(0, 1), (1, 0)]
FOLD = ("batch", "branch")


def flip(a, axis):
    return lax.ppermute(a, axis, SWAP)


def pick(a, index, axis=0):
    return lax.dynamic_index_in_dim(a, index, axis, keepdims=False)


def block_row(at_ref, k):
    y, core = at_ref[0], at_ref[1]
    chip, other = k // 2, k % 2
    return chip % 2, 2 * (1 - y if chip // 2 else y) + (1 - core if other else core)


def assemble(blocks, at, deps=()):
    rows, cols = blocks[0].shape
    tile = 256 if cols % 256 == 0 else cols

    def kernel(at_ref, *refs):
        for k in range(8):
            d, row = block_row(at_ref, k)
            refs[8][d, pl.ds(pl.multiple_of(row * rows, rows), rows)] = refs[k][...]

    return call(
        kernel,
        deps,
        (at, *blocks),
        grid=(cols // tile,),
        in_specs=[pl.BlockSpec((rows, tile), lambda j, at: (0, j))] * 8,
        out_specs=pl.BlockSpec((2, 4 * rows, tile), lambda j, at: (0, 0, j)),
        out_shape=jax.ShapeDtypeStruct((2, 4 * rows, cols), blocks[0].dtype),
        prefetch=1,
        name="assemble",
    )


def assemble_heads(blocks, at, parts, width):
    rows, cols = blocks[0].shape
    hidden = cols - (parts + 1) * width
    if width % LANES:
        w = assemble(blocks, at)
        columns = [w[r, :, c * width : (c + 1) * width] for c in range(parts + 1) for r in range(2)]
        return jnp.concatenate(columns[: 2 * parts], 1), jnp.concatenate(columns[2 * parts :], 1), w[:, :, cols - hidden :]

    def kernel(at_ref, *refs):
        qkv_ref, dense_ref, up_ref = refs[8:]
        j = pl.program_id(0)
        for k in range(8):
            d, row = block_row(at_ref, k)
            at = pl.ds(pl.multiple_of(row * rows, rows), rows)
            for d_k in range(2):
                if d_k != d:
                    continue

                @pl.when(j < parts)
                def _():
                    qkv_ref[at, d_k * width : (d_k + 1) * width] = refs[k][...]

                @pl.when(j == parts)
                def _():
                    dense_ref[at, d_k * width : (d_k + 1) * width] = refs[k][...]

                @pl.when(j > parts)
                def _():
                    up_ref[d_k, at] = refs[k][...]

    depth = 4 * rows
    return call(
        kernel,
        (),
        (at, *blocks),
        grid=(cols // width,),
        in_specs=[pl.BlockSpec((rows, width), lambda j, at: (0, j))] * 8,
        out_specs=[
            pl.BlockSpec((depth, 2 * width), lambda j, at: (0, jnp.minimum(j, parts - 1))),
            pl.BlockSpec((depth, 2 * width), lambda j, at: (0, 0)),
            pl.BlockSpec((2, depth, width), lambda j, at: (0, 0, jnp.maximum(j - parts - 1, 0))),
        ],
        out_shape=[
            jax.ShapeDtypeStruct((depth, 2 * parts * width), bf16),
            jax.ShapeDtypeStruct((depth, 2 * width), bf16),
            jax.ShapeDtypeStruct((2, depth, hidden), bf16),
        ],
        prefetch=1,
        name="assemble_heads",
    )


class Gather:
    def __init__(self, w):
        self.w = w
        self.half = w.shape[0] // 2
        self.blocks = [w, flip(w, "branch")]

    def first(self, *deps):
        w = tie(self.w, *deps) if deps else self.w
        self.x, self.y = flip(w, "near"), flip(w, "batch")

    def second(self, *deps):
        if deps:
            self.x, self.y = (tie(a, *deps) for a in (self.x, self.y))
        self.halves = self.y[: self.half], self.x[self.half :]
        self.corner = flip(self.halves[0], "near"), flip(self.halves[1], "batch")

    def third(self):
        for b in (self.x, self.y, jnp.concatenate(self.corner, 0)):
            self.blocks += [b, flip(b, "branch")]
        return self.blocks


class Scatter:
    def __init__(self, keep, send):
        self.keep, self.got = keep, flip(send, "branch")
        self.half = keep.shape[2] // 2

    def first(self, *deps):
        g = (tie(self.keep, *deps) if deps else self.keep) + self.got
        corner = g[1, 1]
        self.own, self.to_y, self.to_x = g[0, 0], g[0, 1], g[1, 0]
        self.got = flip(corner[: self.half], "near"), flip(corner[self.half :], "batch")
        return (self.own,)

    def second(self, *deps):
        h = self.half
        got = tuple(tie(a, *deps) for a in self.got) if deps else self.got
        to_y = jnp.concatenate([self.to_y[:h] + got[0], self.to_y[h:]], 0)
        to_x = jnp.concatenate([self.to_x[:h], self.to_x[h:] + got[1]], 0)
        self.got = flip(to_x, "near"), flip(to_y, "batch")
        return to_x, to_y

    def result(self):
        return self.own.astype(f32) + self.got[0].astype(f32) + self.got[1].astype(f32)


def body(
    line_size,
    tokens,
    cotangent,
    segments,
    positions,
    ln_gain,
    ln_bias,
    qkv_weight,
    qkv_bias,
    dense_weight,
    dense_bias,
    up_weight,
    up_bias,
    down_weight,
    down_bias,
):
    micros, seqs, shard, depth = tokens.shape
    full_len = segments.shape[2]
    quarter, parts, width = qkv_weight.shape
    hidden = up_weight.shape[1]
    x, y, core, z = (lax.axis_index(a) for a in ("near", "batch", "branch", "line"))
    first = x == 0

    def to_group(a, start=(), end=()):
        send = jnp.where(first, a[1], a[0])
        got = flip(tie(send, *start) if start else send, "near")
        kept = jnp.where(first, a[0], a[1])
        got = tie(got, *end) if end else got
        return jnp.concatenate([jnp.where(first, kept, got), jnp.where(first, got, kept)], 0)

    def from_group(a, end=()):
        lo, hi = a[:shard], a[shard:]
        got = flip(jnp.where(first, hi, lo), "near")
        got = tie(got, *end) if end else got
        kept = jnp.where(first, lo, hi)
        return jnp.where(first, kept, got), jnp.where(first, got, kept)

    at = jnp.stack([y, core]).astype(jnp.int32)

    units, scales, groups_n, groups_c = [], [], [], []
    for s in range(seqs):
        r = tokens[:, s].astype(f32)
        centered = r - jnp.mean(r, -1, keepdims=True)
        scales.append(lax.rsqrt(jnp.mean(centered * centered, -1, keepdims=True) + eps_norm))
        units.append(centered * scales[s])

    def normed(s):
        return (units[s] * ln_gain + ln_bias).astype(bf16)

    def gather_rows(group):
        return lax.all_gather(group, "line", axis=0, tiled=True)

    n_0 = to_group(normed(0))
    early = Gather(jnp.concatenate([qkv_weight.reshape(quarter, parts * width), dense_weight.T, up_weight], 1))
    late = Gather(down_weight.T)
    early.first(n_0)
    early.second()
    late.first(*early.corner)
    qkv, dense_t, up = assemble_heads(early.third(), at, parts, width)
    c_0 = to_group(cotangent[:, 0], early.corner, (dense_t,))
    rows_n, rows_c = [gather_rows(n_0)], [gather_rows(c_0)]
    late.second(dense_t)
    bias_qkv = jnp.concatenate([qkv_bias, flip(qkv_bias, "near")], 1)
    bias_up = jnp.concatenate([up_bias, flip(up_bias, "near")], 0)
    segment = jnp.where(first, segments[0], segments[1])
    place = jnp.where(first, positions[0], positions[1])
    tables = [rope_tables(place[s]) for s in range(seqs)]

    def scatter_rows(part):
        return lax.psum_scatter(part, "line", scatter_dimension=0, tiled=True)

    proj = project(rows_n[0], qkv, f32, (c_0,))
    n_1 = to_group(normed(1), (proj,), (proj,))
    rows_n.append(gather_rows(n_1))
    attn_0, keep, log = attention(proj, bias_qkv, tables[0], segment[0], (n_1,))
    late.second(attn_0)
    c_1 = to_group(cotangent[:, 1], (attn_0,), (attn_0,))
    rows_c.append(gather_rows(c_1))
    act_0, slope = mlp_act(rows_n[0], up, bias_up, (*late.halves, c_1))
    down_t = assemble(late.third(), at, (act_0,))
    part = mixed_part(act_0, attn_0, down_t, dense_t)
    mixed_0 = scatter_rows(part)
    grad_attn = project(rows_c[0], dense_t, bf16, (part,))
    dp_0, db_0 = attention_grad(keep, log, attn_0, grad_attn, tables[0], segment[0])
    pre_0, up_0 = mlp_pre(rows_c[0], down_t, slope, (dp_0,))
    part, back_0 = back_part(pre_0, dp_0, up, qkv, rows_n[0])
    back_sum_0 = scatter_rows(part)
    proj = project(rows_n[1], qkv, f32, (part,))
    attn_1, keep, log = attention(proj, bias_qkv, tables[1], segment[1])
    act_1, slope = mlp_act(rows_n[1], up, bias_up, (attn_1,))
    part = mixed_part(act_1, attn_1, down_t, dense_t)
    mixed_1 = scatter_rows(part)
    grad_attn = project(rows_c[1], dense_t, bf16, (part,))
    dp_1, db_1 = attention_grad(keep, log, attn_1, grad_attn, tables[1], segment[1])
    pre_1, up_1 = mlp_pre(rows_c[1], down_t, slope, (dp_1,))
    part, back_1 = back_part(pre_1, dp_1, up, qkv, rows_n[1])
    back_sum_1 = scatter_rows(part)
    grad_up = Scatter(*weight_grad(at, rows_n, (pre_0, pre_1), (part,)))
    grad_down = Scatter(*weight_grad(at, rows_c, (act_0, act_1), (grad_up.keep,)))
    mixed_0 = from_group(tie(mixed_0, grad_up.keep), (grad_down.keep,))
    sends = (*grad_up.first(grad_down.keep), *mixed_0)
    sum_qkv = (db_0 + db_1)[:parts].reshape(parts, 2, width)
    sum_up = (up_0 + up_1).reshape(2, hidden)
    out_bias = jnp.sum(cotangent, (0, 1, 2), dtype=f32)
    own, other = (jnp.concatenate([sum_qkv[:, d].reshape(-1), sum_up[d]]) for d in range(2))
    rest = jnp.concatenate([(back_0 + back_1).reshape(-1), out_bias])
    size = own.shape[0]
    sums = jnp.concatenate([other, rest])
    got = flip(sums, "near")
    sends = (*sends, sums)
    grad_heads = Scatter(*heads_grad(at, rows_n, (dp_0, dp_1), rows_c, (attn_0, attn_1), sends))
    done = grad_heads.keep
    got = tie(got, done)
    sends = (*grad_up.second(done), *grad_down.first(done))
    sums = tie(jnp.concatenate([own, rest]) + got, *sends)
    sums = sums + flip(sums, "batch")
    sends = (*grad_down.second(), *grad_heads.first(sums))
    back_sum_0 = from_group(tie(back_sum_0, *sends))
    sums = tie(sums, *sends)
    sums = sums + flip(sums, "branch")
    sends = grad_heads.second(sums)
    bias_sums, rest = sums[:size], sums[size:]
    reach = 1
    while reach < line_size:
        rest = rest + lax.ppermute(rest, "line", [(i, i ^ reach) for i in range(line_size)])
        reach *= 2
    rest = rest.reshape(3, depth)
    shift_grad = rest[0]
    gain_grad = (rest[1] - ln_bias * shift_grad) / ln_gain
    grad_up = grad_up.result()
    grad_down = grad_down.result().T
    grad_heads = grad_heads.result()
    grad_qkv = grad_heads[:, : parts * width].reshape(quarter, parts, width)
    grad_dense = grad_heads[:, parts * width :].T

    mixed, tokens_grad = [], []
    mixed_1 = from_group(tie(mixed_1, grad_qkv, grad_dense, grad_up, grad_down))
    back_sum_1 = from_group(tie(back_sum_1, *mixed_1))
    for s, (m, g) in enumerate(((mixed_0, back_sum_0), (mixed_1, back_sum_1))):
        mixed.append((tokens[:, s].astype(f32) + jnp.stack(m, 0).astype(f32) + dense_bias + down_bias).astype(bf16))
        w = jnp.stack(g, 0).astype(f32) * ln_gain
        u = units[s]
        tokens_grad.append(
            cotangent[:, s].astype(f32)
            + scales[s] * (w - jnp.mean(w, -1, keepdims=True) - u * jnp.mean(w * u, -1, keepdims=True))
        )

    return (
        jnp.stack(mixed, 1),
        jnp.stack(tokens_grad, 1),
        gain_grad,
        shift_grad,
        grad_qkv,
        bias_sums[: parts * width].reshape(parts, width),
        grad_dense,
        rest[2],
        grad_up,
        bias_sums[parts * width :],
        grad_down,
        rest[2],
    )


def solution(mesh):
    batch, branch, tensor = (mesh.shape[a] for a in ("batch", "branch", "tensor"))
    inner = Mesh(mesh.devices.reshape(batch, branch, tensor // 2, 2), ("batch", "branch", "line", "near"))
    tensor = ("line", "near")
    rows = P(None, FOLD, tensor, None)
    first = P(FOLD, None, tensor)
    weights = (first, P(None, tensor), P(tensor, FOLD), P(), P(FOLD, tensor), P(tensor), P(tensor, FOLD), P())
    return jax.shard_map(
        partial(body, inner.shape["line"]),
        mesh=inner,
        in_specs=(rows, rows, P(None, FOLD, None), P(None, FOLD, None), P(), P(), *weights),
        out_specs=(rows, rows, P(), P(), *weights),
        check_vma=False,
    )
```

```python
from functools import partial

import jax
import jax.numpy as jnp
from jax import lax
from jax.experimental import pallas as pl
from jax.experimental.pallas import tpu as pltpu
from jax.sharding import Mesh
from jax.sharding import PartitionSpec as P

HEAD_DIM = 64
ROT = 32
LANES = 128
VMEM = 60 * 2**20
COST = {"attention": 100, "attention_grad": 100, "mlp_act": 100, "mlp_pre": 60, "mixed_part": 60, "back_part": 100,
        "weight_grad": 100, "heads_grad": 100, "project": 50, "assemble": 8, "assemble_heads": 14}


def cost(units):
    return pl.CostEstimate(flops=units * 250000000 + 1, bytes_accessed=units * 250000 + 1, transcendentals=0)


eps_norm = 1e-05
rope_base = 10000.0
masked_score = -1e30
f32 = jnp.float32
bf16 = jnp.bfloat16

NN = (((1,), (0,)), ((), ()))
NT = (((1,), (1,)), ((), ()))
TN = (((0,), (0,)), ((), ()))


def mm(a, b, dims=NN):
    return lax.dot_general(a, b, dims, preferred_element_type=f32)


def call(kernel, deps, args, *, grid, in_specs, out_specs, out_shape, name, scratch=(), prefetch=0):
    deps = list(deps)
    inputs = prefetch + len(in_specs)

    def run(*refs):
        kernel(*refs[:inputs], *refs[inputs + len(deps) :])

    spec = pltpu.PrefetchScalarGridSpec(
        num_scalar_prefetch=prefetch,
        grid=grid,
        in_specs=list(in_specs) + [pl.BlockSpec(memory_space=pl.ANY)] * len(deps),
        out_specs=out_specs,
        scratch_shapes=list(scratch),
    )
    return pl.pallas_call(
        run,
        grid_spec=spec,
        out_shape=out_shape,
        compiler_params=pltpu.CompilerParams(vmem_limit_bytes=VMEM),
        cost_estimate=cost(COST[name]),
        name=name,
    )(*args, *deps)


def tie(a, *deps, units=0):
    return pl.pallas_call(
        lambda *refs: None,
        in_specs=[pl.BlockSpec(memory_space=pl.ANY)] * (1 + len(deps)),
        out_specs=pl.BlockSpec(memory_space=pl.ANY),
        out_shape=jax.ShapeDtypeStruct(a.shape, a.dtype),
        input_output_aliases={0: 0},
        cost_estimate=cost(units),
        name="tie",
    )(a, *deps)


def project_kernel(a_ref, w_ref, out_ref):
    rows = a_ref.shape[0]
    step = min(512, rows)
    for i in range(rows // step):
        at = slice(i * step, (i + 1) * step)
        out_ref[at] = mm(a_ref[at], w_ref[...]).astype(out_ref.dtype)


def project(a, w, dtype, deps=()):
    rows, depth = a.shape
    cols = w.shape[1]
    bn = 256 if cols % 256 == 0 else 128
    return call(
        project_kernel,
        deps,
        (a, w),
        grid=(cols // bn,),
        in_specs=[pl.BlockSpec((rows, depth), lambda j: (0, 0)), pl.BlockSpec((depth, bn), lambda j: (0, j))],
        out_specs=pl.BlockSpec((rows, bn), lambda j: (0, j)),
        out_shape=jax.ShapeDtypeStruct((rows, cols), dtype),
        name="project",
    )


def rope_tables(token_place):
    full_len = token_place.shape[0]
    half = ROT // 2
    inverse = rope_base ** (-(jnp.arange(half, dtype=f32) * (2.0 / ROT)))
    angles = token_place.astype(f32)[:, None] * inverse
    c, s = jnp.cos(angles), jnp.sin(angles)
    rest = (full_len, HEAD_DIM - ROT)
    zero_half = jnp.zeros((full_len, half), f32)
    cos = jnp.concatenate([c, c, jnp.ones(rest, f32)], 1)
    sa = jnp.concatenate([-s, zero_half, jnp.zeros(rest, f32)], 1)
    sb = jnp.concatenate([zero_half, s, jnp.zeros(rest, f32)], 1)
    return tuple(jnp.tile(t, (1, LANES // HEAD_DIM)) for t in (cos, sa, sb))


def attn_kernel(
    q_ref, k_ref, v_ref, qb_ref, kb_ref, vb_ref, cos_ref, sa_ref, sb_ref, segr_ref, segc_ref, out_ref, keep_ref, log_ref
):
    full_len = q_ref.shape[0]
    size = min(256, full_len)
    half = ROT // 2
    heads = LANES // HEAD_DIM
    cos, sa, sb = cos_ref[...], sa_ref[...], sb_ref[...]

    def rope(x):
        return x * cos + pltpu.roll(x, LANES - half, 1) * sa + pltpu.roll(x, half, 1) * sb

    lane = lax.broadcasted_iota(jnp.int32, (1, LANES), 1)
    q = (rope(q_ref[...] + qb_ref[...]) * (HEAD_DIM**-0.5)).astype(bf16)
    k = rope(k_ref[...] + kb_ref[...]).astype(bf16)
    v = (v_ref[...] + vb_ref[...]).astype(bf16)
    keep_ref[0] = q
    keep_ref[1] = k
    keep_ref[2] = v
    v_t = v.astype(f32).T.astype(bf16)
    tri = lax.broadcasted_iota(jnp.int32, (size, size), 0) <= lax.broadcasted_iota(jnp.int32, (size, size), 1)
    zero = jnp.zeros((), bf16)
    for j in range(full_len // size):
        cols = slice(j * size, (j + 1) * size)
        seg_q = segr_ref[:, cols]
        out_rows = []
        for h in range(heads):
            mine = (lane >= h * HEAD_DIM) & (lane < (h + 1) * HEAD_DIM)
            span = slice(h * HEAD_DIM, (h + 1) * HEAD_DIM)
            qh = jnp.where(mine, q[cols], zero)
            tiles, top, total, out = [], None, None, None
            for i in range(j + 1):
                rows = slice(i * size, (i + 1) * size)
                ok = segc_ref[rows] == seg_q
                if i == j:
                    ok = ok & tri
                s = jnp.where(ok, mm(k[rows], qh, NT), masked_score)
                m = jnp.max(s, 0, keepdims=True)
                top = m if top is None else jnp.maximum(top, m)
                tiles.append(s)
            for i in range(j + 1):
                e = jnp.exp(tiles[i] - top)
                t = jnp.sum(e, 0, keepdims=True)
                total = t if total is None else total + t
                t = mm(v_t[span, i * size : (i + 1) * size], e.astype(bf16))
                out = t if out is None else out + t
            out_rows.append(out * (1.0 / total))
            log_ref[h : h + 1, cols] = top + jnp.log(total)
        out_ref[cols] = jnp.concatenate(out_rows, 0).T.astype(bf16)


def attention(proj, bias, tables, segment, deps=()):
    full_len, wide = proj.shape
    width = wide // 3
    pairs = width // LANES
    bias = bias.reshape(1, wide)

    def part(c):
        return pl.BlockSpec((full_len, LANES), lambda p: (0, c * pairs + p))

    def bias_part(c):
        return pl.BlockSpec((1, LANES), lambda p: (0, c * pairs + p))

    def whole(*shape):
        return pl.BlockSpec(shape, lambda p: (0, 0))

    table = whole(full_len, LANES)
    return call(
        attn_kernel,
        deps,
        (proj, proj, proj, bias, bias, bias, *tables, segment.reshape(1, -1), segment.reshape(-1, 1)),
        grid=(pairs,),
        in_specs=[part(0), part(1), part(2), bias_part(0), bias_part(1), bias_part(2), table, table, table,
                  whole(1, full_len), whole(full_len, 1)],
        out_specs=[
            pl.BlockSpec((full_len, LANES), lambda p: (0, p)),
            pl.BlockSpec((3, full_len, LANES), lambda p: (0, 0, p)),
            pl.BlockSpec((8, full_len), lambda p: (p, 0)),
        ],
        out_shape=[
            jax.ShapeDtypeStruct((full_len, width), bf16),
            jax.ShapeDtypeStruct((3, full_len, width), bf16),
            jax.ShapeDtypeStruct((8 * pairs, full_len), f32),
        ],
        name="attention",
    )


def attn_grad_kernel(
    keep_ref, log_ref, ao_ref, ga_ref, cos_ref, sa_ref, sb_ref, segr_ref, segc_ref, dp_ref, db_ref, dk_acc, dv_acc
):
    full_len = ao_ref.shape[0]
    size = min(256, full_len)
    half = ROT // 2
    heads = LANES // HEAD_DIM
    cos, sa, sb = cos_ref[...], sa_ref[...], sb_ref[...]

    def unrope(g):
        return g * cos + pltpu.roll(g * sa, half, 1) + pltpu.roll(g * sb, LANES - half, 1)

    lane = lax.broadcasted_iota(jnp.int32, (1, LANES), 1)
    q, k, v, do = keep_ref[0], keep_ref[1], keep_ref[2], ga_ref[...]
    k_t = k.astype(f32).T.astype(bf16)
    inner_t = (do.astype(f32) * ao_ref[...].astype(f32)).T
    tri = lax.broadcasted_iota(jnp.int32, (size, size), 0) <= lax.broadcasted_iota(jnp.int32, (size, size), 1)
    zero = jnp.zeros((), bf16)
    dq_blocks = []
    for j in range(full_len // size):
        cols = slice(j * size, (j + 1) * size)
        seg_q = segr_ref[:, cols]
        spans, masks, queries, grads, logs, inners = [], [], [], [], [], []
        for h in range(heads):
            mine = (lane >= h * HEAD_DIM) & (lane < (h + 1) * HEAD_DIM)
            spans.append(slice(h * HEAD_DIM, (h + 1) * HEAD_DIM))
            queries.append(jnp.where(mine, q[cols], zero))
            grads.append(jnp.where(mine, do[cols], zero))
            logs.append(log_ref[h : h + 1, cols])
            inners.append(jnp.sum(inner_t[spans[h], cols], 0, keepdims=True))
        dq = [None] * heads
        for i in range(j + 1):
            rows = slice(i * size, (i + 1) * size)
            ok = segc_ref[rows] == seg_q
            if i == j:
                ok = ok & tri
            dv = dk = None
            for h in range(heads):
                p = jnp.exp(jnp.where(ok, mm(k[rows], queries[h], NT) - logs[h], masked_score))
                g = (p * (mm(v[rows], grads[h], NT) - inners[h])).astype(bf16)
                t = mm(p.astype(bf16), grads[h])
                dv = t if dv is None else dv + t
                t = mm(g, queries[h])
                dk = t if dk is None else dk + t
                t = mm(k_t[spans[h], rows], g)
                dq[h] = t if dq[h] is None else dq[h] + t
            if i == j:
                dv_acc[rows] = dv
                dk_acc[rows] = dk
            else:
                dv_acc[rows] += dv
                dk_acc[rows] += dk
        dq_blocks.append((jnp.concatenate(dq, 0) * (HEAD_DIM**-0.5)).T)
    dq = unrope(jnp.concatenate(dq_blocks, 0)).astype(bf16)
    dk = unrope(dk_acc[...]).astype(bf16)
    dv = dv_acc[...].astype(bf16)
    for part, g in enumerate((dq, dk, dv)):
        dp_ref[part] = g
        db_ref[part : part + 1] = jnp.sum(g.astype(f32), 0, keepdims=True)


def attention_grad(keep, logs, attn, grad_attn, tables, segment, deps=()):
    _, full_len, width = keep.shape

    def whole(*shape):
        return pl.BlockSpec(shape, lambda p: (0, 0))

    table = whole(full_len, LANES)
    cols = pl.BlockSpec((full_len, LANES), lambda p: (0, p))
    three = pl.BlockSpec((3, full_len, LANES), lambda p: (0, 0, p))
    return call(
        attn_grad_kernel,
        deps,
        (keep, logs, attn, grad_attn, *tables, segment.reshape(1, -1), segment.reshape(-1, 1)),
        grid=(width // LANES,),
        in_specs=[three, pl.BlockSpec((8, full_len), lambda p: (p, 0)), cols, cols, table, table, table,
                  whole(1, full_len), whole(full_len, 1)],
        out_specs=[three, pl.BlockSpec((8, LANES), lambda p: (0, p))],
        out_shape=[jax.ShapeDtypeStruct((3, full_len, width), bf16), jax.ShapeDtypeStruct((8, width), f32)],
        scratch=[pltpu.VMEM((full_len, LANES), f32), pltpu.VMEM((full_len, LANES), f32)],
        name="attention_grad",
    )


def act_kernel(n_ref, up_ref, bias_ref, act_ref, slope_ref):
    rows = n_ref.shape[0]
    step = min(256, rows)
    k0 = 0.7978845608028654
    k1 = k0 * 0.044715
    for i in range(rows // step):
        at = slice(i * step, (i + 1) * step)
        v = mm(n_ref[at], up_ref[...]) + bias_ref[...]
        v2 = v * v
        t = jnp.tanh(v * (k0 + k1 * v2))
        h = 0.5 * t + 0.5
        act_ref[at] = (v * h).astype(bf16)
        slope_ref[at] = (h + v * (1.0 - t * t) * (0.5 * k0 + 1.5 * k1 * v2)).astype(bf16)


def mlp_act(n, up, bias, deps=()):
    rows, depth = n.shape
    near, _, hidden = up.shape
    br, bh = min(1024, rows), min(512, hidden)
    per = hidden // bh
    out = pl.BlockSpec((br, bh), lambda j, i: (i, j))
    shape = jax.ShapeDtypeStruct((rows, near * hidden), bf16)
    return call(
        act_kernel,
        deps,
        (n, up, bias.reshape(1, -1)),
        grid=(near * per, rows // br),
        in_specs=[pl.BlockSpec((br, depth), lambda j, i: (i, 0)),
                  pl.BlockSpec((None, depth, bh), lambda j, i: (j // per, 0, j % per)),
                  pl.BlockSpec((1, bh), lambda j, i: (0, j))],
        out_specs=[out, out],
        out_shape=[shape, shape],
        name="mlp_act",
    )


def pre_kernel(c_ref, down_ref, slope_ref, pre_ref, sum_ref):
    rows = c_ref.shape[0]
    step = min(256, rows)
    total = None
    for i in range(rows // step):
        at = slice(i * step, (i + 1) * step)
        p = (mm(c_ref[at], down_ref[...]) * slope_ref[at].astype(f32)).astype(bf16)
        pre_ref[at] = p
        s = jnp.sum(p.astype(f32), 0, keepdims=True)
        total = s if total is None else total + s
    sum_ref[...] = jnp.broadcast_to(total, sum_ref.shape)


def mlp_pre(c, down_t, slope, deps=()):
    rows, depth = c.shape
    near, _, hidden = down_t.shape
    br, bh = min(1024, rows), min(512, hidden)
    per = hidden // bh
    out = pl.BlockSpec((br, bh), lambda j, i: (i, j))
    pre, sums = call(
        pre_kernel,
        deps,
        (c, down_t, slope),
        grid=(near * per, rows // br),
        in_specs=[pl.BlockSpec((br, depth), lambda j, i: (i, 0)),
                  pl.BlockSpec((None, depth, bh), lambda j, i: (j // per, 0, j % per)), out],
        out_specs=[out, pl.BlockSpec((8, bh), lambda j, i: (i, j))],
        out_shape=[
            jax.ShapeDtypeStruct((rows, near * hidden), bf16),
            jax.ShapeDtypeStruct((rows // br * 8, near * hidden), f32),
        ],
        name="mlp_pre",
    )
    return pre, jnp.sum(sums.reshape(-1, 8, near * hidden)[:, 0], 0)


def mixed_kernel(act_ref, attn_ref, down_ref, dense_ref, out_ref):
    rows = act_ref.shape[0]
    near, _, hidden = down_ref.shape
    step = min(512, rows)
    for i in range(rows // step):
        at = slice(i * step, (i + 1) * step)
        total = mm(attn_ref[at], dense_ref[...], NT)
        for r in range(near):
            total = total + mm(act_ref[at, r * hidden : (r + 1) * hidden], down_ref[r], NT)
        out_ref[at] = total.astype(bf16)


def mixed_part(act, attn, down_t, dense_t, deps=()):
    rows = act.shape[0]
    width = attn.shape[1]
    near, depth, hidden = down_t.shape
    br, bn = min(1024, rows), min(512, depth)
    return call(
        mixed_kernel,
        deps,
        (act, attn, down_t, dense_t),
        grid=(depth // bn, rows // br),
        in_specs=[pl.BlockSpec((br, near * hidden), lambda j, i: (i, 0)), pl.BlockSpec((br, width), lambda j, i: (i, 0)),
                  pl.BlockSpec((near, bn, hidden), lambda j, i: (0, j, 0)), pl.BlockSpec((bn, width), lambda j, i: (j, 0))],
        out_specs=pl.BlockSpec((br, bn), lambda j, i: (i, j)),
        out_shape=jax.ShapeDtypeStruct((rows, depth), bf16),
        name="mixed_part",
    )


def back_kernel(pre_ref, dp_ref, up_ref, qkv_ref, n_ref, out_ref, sum_ref):
    rows = pre_ref.shape[0]
    near, _, hidden = up_ref.shape
    parts, _, width = dp_ref.shape
    step = min(512, rows)
    plain = scaled = None
    for i in range(rows // step):
        at = slice(i * step, (i + 1) * step)
        total = None
        for r in range(near):
            t = mm(pre_ref[at, r * hidden : (r + 1) * hidden], up_ref[r], NT)
            total = t if total is None else total + t
        for c in range(parts):
            total = total + mm(dp_ref[c, at], qkv_ref[:, c * width : (c + 1) * width], NT)
        out_ref[at] = total.astype(bf16)
        a = jnp.sum(total, 0, keepdims=True)
        b = jnp.sum(total * n_ref[at].astype(f32), 0, keepdims=True)
        plain = a if plain is None else plain + a
        scaled = b if scaled is None else scaled + b
    sum_ref[0:1] = plain
    sum_ref[1:2] = scaled


def back_part(pre, dp, up, qkv, n, deps=()):
    rows = pre.shape[0]
    parts, _, width = dp.shape
    near, depth, hidden = up.shape
    br, bn = min(1024, rows), min(512, depth)
    out, sums = call(
        back_kernel,
        deps,
        (pre, dp, up, qkv, n),
        grid=(depth // bn, rows // br),
        in_specs=[pl.BlockSpec((br, near * hidden), lambda j, i: (i, 0)), pl.BlockSpec((parts, br, width), lambda j, i: (0, i, 0)),
                  pl.BlockSpec((near, bn, hidden), lambda j, i: (0, j, 0)), pl.BlockSpec((bn, parts * width), lambda j, i: (j, 0)),
                  pl.BlockSpec((br, bn), lambda j, i: (i, j))],
        out_specs=[pl.BlockSpec((br, bn), lambda j, i: (i, j)), pl.BlockSpec((8, bn), lambda j, i: (i, j))],
        out_shape=[jax.ShapeDtypeStruct((rows, depth), bf16), jax.ShapeDtypeStruct((rows // br * 8, depth), f32)],
        name="back_part",
    )
    return out, jnp.sum(sums.reshape(-1, 8, depth)[:, :2], 0)


def store_quarters(at_ref, total, held, keep_ref, send_ref):
    held[...] = total.astype(bf16)
    rows = held.shape[0] // 4
    y, core = at_ref[0], at_ref[1]
    for d in range(2):
        row = 2 * (1 - y if d else y)
        keep_ref[d] = held[pl.ds(pl.multiple_of((row + core) * rows, rows), rows)]
        send_ref[d] = held[pl.ds(pl.multiple_of((row + 1 - core) * rows, rows), rows)]


def weight_grad(at, xs, ys, deps=()):
    rows, m = xs[0].shape
    hidden = ys[0].shape[1] // 2
    tile = min(hidden, 512)
    per = hidden // tile
    count = len(xs)

    def kernel(at_ref, *refs):
        total = None
        for x, y in zip(refs[:count], refs[count : 2 * count], strict=True):
            t = mm(x[...], y[...], TN)
            total = t if total is None else total + t
        keep_ref, send_ref, held = refs[2 * count :]
        store_quarters(at_ref, total, held, keep_ref, send_ref)

    x_spec = pl.BlockSpec((rows, m), lambda j, at: (0, 0), pipeline_mode=pl.Buffered(1))
    y_spec = pl.BlockSpec((rows, tile), lambda j, at: (0, j))
    out = pl.BlockSpec((None, 2, m // 4, tile), lambda j, at: (j // per, 0, 0, j % per))
    shape = jax.ShapeDtypeStruct((2, 2, m // 4, hidden), bf16)
    return call(
        kernel,
        deps,
        (at, *xs, *ys),
        grid=(2 * per,),
        in_specs=[x_spec] * count + [y_spec] * count,
        out_specs=[out, out],
        out_shape=[shape, shape],
        scratch=[pltpu.VMEM((m, tile), bf16)],
        prefetch=1,
        name="weight_grad",
    )


def heads_grad(at, ns, dps, cs, attns, deps=()):
    parts, rows, wide = dps[0].shape
    m = ns[0].shape[1]
    width = wide // 2
    count = len(ns)
    out_cols = (parts + 1) * width
    if width % LANES:
        blocks = [sum(mm(n, dp[c], TN) for n, dp in zip(ns, dps, strict=True)) for c in range(parts)]
        blocks.append(sum(mm(c, a, TN) for c, a in zip(cs, attns, strict=True)))
        g = jnp.stack([jnp.concatenate([b[:, r * width : (r + 1) * width] for b in blocks], 1) for r in range(2)], 0)
        g = g.astype(bf16).reshape(2, 2, 2, m // 4, out_cols)
        g = jnp.where(at[0] == 0, g, g[:, ::-1])
        return jnp.where(at[1] == 0, g[:, :, 0], g[:, :, 1]), jnp.where(at[1] == 0, g[:, :, 1], g[:, :, 0])

    def kernel(at_ref, *refs):
        n_refs, dp_refs, c_refs, a_refs = (refs[i * count : (i + 1) * count] for i in range(4))
        keep_ref, send_ref, held = refs[4 * count :]
        part = pl.program_id(0)

        def store(total):
            for d in range(2):
                store_quarters(at_ref, total[:, d * width : (d + 1) * width], held, keep_ref.at[d], send_ref.at[d])

        @pl.when(part < parts)
        def _():
            store(sum(mm(n[...], d[...], TN) for n, d in zip(n_refs, dp_refs, strict=True)))

        @pl.when(part == parts)
        def _():
            store(sum(mm(c[...], a[...], TN) for c, a in zip(c_refs, a_refs, strict=True)))

    x_spec = pl.BlockSpec((rows, m), lambda p, at: (0, 0), pipeline_mode=pl.Buffered(1))
    dp_spec = pl.BlockSpec((None, rows, wide), lambda p, at: (jnp.minimum(p, parts - 1), 0, 0))
    a_spec = pl.BlockSpec((rows, wide), lambda p, at: (0, 0))
    out = pl.BlockSpec((2, 2, m // 4, width), lambda p, at: (0, 0, 0, p))
    shape = jax.ShapeDtypeStruct((2, 2, m // 4, out_cols), bf16)
    return call(
        kernel,
        deps,
        (at, *ns, *dps, *cs, *attns),
        grid=(parts + 1,),
        in_specs=[x_spec] * count + [dp_spec] * count + [x_spec] * count + [a_spec] * count,
        out_specs=[out, out],
        out_shape=[shape, shape],
        scratch=[pltpu.VMEM((m, width), bf16)],
        prefetch=1,
        name="heads_grad",
    )


SWAP = [(0, 1), (1, 0)]
FOLD = ("batch", "branch")


def flip(a, axis):
    return lax.ppermute(a, axis, SWAP)


def pick(a, index, axis=0):
    return lax.dynamic_index_in_dim(a, index, axis, keepdims=False)


def block_row(at_ref, k):
    y, core = at_ref[0], at_ref[1]
    chip, other = k // 2, k % 2
    return chip % 2, 2 * (1 - y if chip // 2 else y) + (1 - core if other else core)


def assemble(blocks, at, deps=()):
    rows, cols = blocks[0].shape
    tile = 256 if cols % 256 == 0 else cols

    def kernel(at_ref, *refs):
        for k in range(8):
            d, row = block_row(at_ref, k)
            refs[8][d, pl.ds(pl.multiple_of(row * rows, rows), rows)] = refs[k][...]

    return call(
        kernel,
        deps,
        (at, *blocks),
        grid=(cols // tile,),
        in_specs=[pl.BlockSpec((rows, tile), lambda j, at: (0, j))] * 8,
        out_specs=pl.BlockSpec((2, 4 * rows, tile), lambda j, at: (0, 0, j)),
        out_shape=jax.ShapeDtypeStruct((2, 4 * rows, cols), blocks[0].dtype),
        prefetch=1,
        name="assemble",
    )


def assemble_heads(blocks, at, parts, width, deps=()):
    rows, cols = blocks[0].shape
    hidden = cols - (parts + 1) * width
    if width % LANES:
        w = assemble(blocks, at)
        columns = [w[r, :, c * width : (c + 1) * width] for c in range(parts + 1) for r in range(2)]
        return jnp.concatenate(columns[: 2 * parts], 1), jnp.concatenate(columns[2 * parts :], 1), w[:, :, cols - hidden :]

    def kernel(at_ref, *refs):
        qkv_ref, dense_ref, up_ref = refs[8:]
        j = pl.program_id(0)
        for k in range(8):
            d, row = block_row(at_ref, k)
            at = pl.ds(pl.multiple_of(row * rows, rows), rows)
            for d_k in range(2):
                if d_k != d:
                    continue

                @pl.when(j < parts)
                def _():
                    qkv_ref[at, d_k * width : (d_k + 1) * width] = refs[k][...]

                @pl.when(j == parts)
                def _():
                    dense_ref[at, d_k * width : (d_k + 1) * width] = refs[k][...]

                @pl.when(j > parts)
                def _():
                    up_ref[d_k, at] = refs[k][...]

    depth = 4 * rows
    return call(
        kernel,
        deps,
        (at, *blocks),
        grid=(cols // width,),
        in_specs=[pl.BlockSpec((rows, width), lambda j, at: (0, j))] * 8,
        out_specs=[
            pl.BlockSpec((depth, 2 * width), lambda j, at: (0, jnp.minimum(j, parts - 1))),
            pl.BlockSpec((depth, 2 * width), lambda j, at: (0, 0)),
            pl.BlockSpec((2, depth, width), lambda j, at: (0, 0, jnp.maximum(j - parts - 1, 0))),
        ],
        out_shape=[
            jax.ShapeDtypeStruct((depth, 2 * parts * width), bf16),
            jax.ShapeDtypeStruct((depth, 2 * width), bf16),
            jax.ShapeDtypeStruct((2, depth, hidden), bf16),
        ],
        prefetch=1,
        name="assemble_heads",
    )


class Gather:
    def __init__(self, w):
        self.w = w
        self.half = w.shape[0] // 2
        self.blocks = [w, flip(w, "branch")]

    def first(self, *deps):
        w = tie(self.w, *deps) if deps else self.w
        self.x, self.y = flip(w, "near"), flip(w, "batch")

    def second(self, *deps):
        if deps:
            self.x, self.y = (tie(a, *deps) for a in (self.x, self.y))
        self.halves = self.y[: self.half], self.x[self.half :]
        self.corner = flip(self.halves[0], "near"), flip(self.halves[1], "batch")

    def third(self):
        for b in (self.x, self.y, jnp.concatenate(self.corner, 0)):
            self.blocks += [b, flip(b, "branch")]
        return self.blocks


class Scatter:
    def __init__(self, keep, send):
        self.keep, self.got = keep, flip(send, "branch")
        self.half = keep.shape[2] // 2

    def first(self, *deps):
        g = self.keep + (tie(self.got, *deps) if deps else self.got)
        corner = g[1, 1]
        self.own, self.to_y, self.to_x = g[0, 0], g[0, 1], g[1, 0]
        self.got = flip(corner[: self.half], "near"), flip(corner[self.half :], "batch")
        return (self.own,)

    def second(self, *deps):
        h = self.half
        got = tuple(tie(a, *deps) for a in self.got) if deps else self.got
        to_y = jnp.concatenate([self.to_y[:h] + got[0], self.to_y[h:]], 0)
        to_x = jnp.concatenate([self.to_x[:h], self.to_x[h:] + got[1]], 0)
        self.got = flip(to_x, "near"), flip(to_y, "batch")
        return to_x, to_y

    def result(self, *deps):
        got = tuple(tie(a, *deps) for a in self.got) if deps else self.got
        return self.own.astype(f32) + got[0].astype(f32) + got[1].astype(f32)


def body(
    line_size,
    tokens,
    cotangent,
    segments,
    positions,
    ln_gain,
    ln_bias,
    qkv_weight,
    qkv_bias,
    dense_weight,
    dense_bias,
    up_weight,
    up_bias,
    down_weight,
    down_bias,
):
    micros, seqs, shard, depth = tokens.shape
    full_len = segments.shape[2]
    quarter, parts, width = qkv_weight.shape
    hidden = up_weight.shape[1]
    x, y, core, z = (lax.axis_index(a) for a in ("near", "batch", "branch", "line"))
    first = x == 0

    def to_group(a, start=(), end=()):
        send = jnp.where(first, a[1], a[0])
        got = flip(tie(send, *start) if start else send, "near")
        kept = jnp.where(first, a[0], a[1])
        got = tie(got, *end) if end else got
        return jnp.concatenate([jnp.where(first, kept, got), jnp.where(first, got, kept)], 0)

    def from_group(a):
        lo, hi = a[:shard], a[shard:]
        send = jnp.where(first, hi, lo)
        got = flip(send, "near")

        def finish(*deps):
            other = tie(got, *deps) if deps else got
            kept = jnp.where(first, lo, hi)
            return jnp.where(first, kept, other), jnp.where(first, other, kept)

        return send, finish

    at = jnp.stack([y, core]).astype(jnp.int32)

    units, scales, groups_n, groups_c = [], [], [], []
    for s in range(seqs):
        r = tokens[:, s].astype(f32)
        centered = r - jnp.mean(r, -1, keepdims=True)
        scales.append(lax.rsqrt(jnp.mean(centered * centered, -1, keepdims=True) + eps_norm))
        units.append(centered * scales[s])

    def normed(s):
        return (units[s] * ln_gain + ln_bias).astype(bf16)

    def gather_rows(group):
        return lax.all_gather(group, "line", axis=0, tiled=True)

    segment = jnp.where(first, segments[0], segments[1])
    place = jnp.where(first, positions[0], positions[1])
    tables = [rope_tables(place[s]) for s in range(seqs)]
    n_0 = to_group(normed(0))
    c_0 = to_group(cotangent[:, 0], (n_0,))
    rows_n, rows_c = [gather_rows(n_0)], [gather_rows(c_0)]
    early = Gather(jnp.concatenate([qkv_weight.reshape(quarter, parts * width), dense_weight.T, up_weight], 1))
    late = Gather(down_weight.T)
    early.first(c_0)
    early.second(*tables[0], *tables[1])
    late.first(*early.corner)
    qkv, dense_t, up = assemble_heads(early.third(), at, parts, width)
    bias_qkv = jnp.concatenate([qkv_bias, flip(qkv_bias, "near")], 1)
    bias_up = jnp.concatenate([up_bias, flip(up_bias, "near")], 0)

    def scatter_rows(part):
        return lax.psum_scatter(part, "line", scatter_dimension=0, tiled=True)

    proj = project(rows_n[0], qkv, f32)
    n_1 = to_group(normed(1), early.corner, (dense_t,))
    late.second(proj)
    attn_0, keep, log = attention(proj, bias_qkv, tables[0], segment[0], (n_1, *late.halves))
    rows_n.append(gather_rows(n_1))
    act_0, slope = mlp_act(rows_n[0], up, bias_up, (attn_0, *late.corner))
    down_t = assemble(late.third(), at, (act_0,))
    part = mixed_part(act_0, attn_0, down_t, dense_t)
    mixed_0 = scatter_rows(part)
    c_1 = to_group(cotangent[:, 1], (act_0,), (part,))
    rows_c.append(gather_rows(c_1))
    grad_attn = project(rows_c[0], dense_t, bf16, (part, c_1))
    dp_0, db_0 = attention_grad(keep, log, attn_0, grad_attn, tables[0], segment[0])
    pre_0, up_0 = mlp_pre(rows_c[0], down_t, slope, (dp_0,))
    part, back_0 = back_part(pre_0, dp_0, up, qkv, rows_n[0])
    back_sum_0 = scatter_rows(part)
    proj = project(rows_n[1], qkv, f32, (part,))
    attn_1, keep, log = attention(proj, bias_qkv, tables[1], segment[1])
    act_1, slope = mlp_act(rows_n[1], up, bias_up, (attn_1,))
    pre_1, up_1 = mlp_pre(rows_c[1], down_t, slope)
    grad_up = Scatter(*weight_grad(at, rows_n, (pre_0, pre_1)))
    grad_down = Scatter(*weight_grad(at, rows_c, (act_0, act_1), (grad_up.keep,)))
    sends = grad_up.first(grad_down.keep)
    part = mixed_part(act_1, attn_1, down_t, dense_t, sends)
    mixed_1 = scatter_rows(part)
    send, finish = from_group(tie(mixed_0, part))
    grad_attn = project(rows_c[1], dense_t, bf16, (part, send))
    dp_1, db_1 = attention_grad(keep, log, attn_1, grad_attn, tables[1], segment[1])
    mixed_0 = finish(dp_1)
    sends = (*grad_up.second(dp_1), *grad_down.first(dp_1))
    part, back_1 = back_part(pre_1, dp_1, up, qkv, rows_n[1], (*sends, *mixed_0))
    back_sum_1 = scatter_rows(part)
    sends = grad_down.second(part)
    grad_up = grad_up.result()
    grad_heads = Scatter(*heads_grad(at, rows_n, (dp_0, dp_1), rows_c, (attn_0, attn_1), (*sends, grad_up)))
    grad_down = grad_down.result(grad_heads.keep)
    own_heads = grad_heads.first(tie(grad_down[:8, :LANES], units=200))
    _, finish = from_group(tie(back_sum_0, *own_heads))
    sends = grad_heads.second()
    back_sum_0 = finish(*sends)
    mixed_1 = from_group(tie(mixed_1, *back_sum_0))[1]()
    grad_down = grad_down.T
    grad_heads = grad_heads.result()
    grad_qkv = grad_heads[:, : parts * width].reshape(quarter, parts, width)
    grad_dense = grad_heads[:, parts * width :].T
    sum_qkv = (db_0 + db_1)[:parts].reshape(parts, 2, width)
    sum_up = (up_0 + up_1).reshape(2, hidden)
    out_bias = jnp.sum(cotangent, (0, 1, 2), dtype=f32)
    own, other = (jnp.concatenate([sum_qkv[:, d].reshape(-1), sum_up[d]]) for d in range(2))
    rest = jnp.concatenate([(back_0 + back_1).reshape(-1), out_bias])
    size = own.shape[0]
    sums = tie(jnp.concatenate([other, rest]), grad_heads, *mixed_1)
    sums = jnp.concatenate([own, rest]) + flip(sums, "near")
    for axis in FOLD:
        sums = sums + flip(sums, axis)
    bias_sums, rest = sums[:size], sums[size:]
    reach = 1
    while reach < line_size:
        rest = rest + lax.ppermute(rest, "line", [(i, i ^ reach) for i in range(line_size)])
        reach *= 2
    rest = rest.reshape(3, depth)
    shift_grad = rest[0]
    gain_grad = (rest[1] - ln_bias * shift_grad) / ln_gain

    mixed, tokens_grad = [], []
    back_sum_1 = from_group(tie(back_sum_1, *mixed_1, rest))[1]()
    for s, (m, g) in enumerate(((mixed_0, back_sum_0), (mixed_1, back_sum_1))):
        mixed.append((tokens[:, s].astype(f32) + jnp.stack(m, 0).astype(f32) + dense_bias + down_bias).astype(bf16))
        w = jnp.stack(g, 0).astype(f32) * ln_gain
        u = units[s]
        tokens_grad.append(
            cotangent[:, s].astype(f32)
            + scales[s] * (w - jnp.mean(w, -1, keepdims=True) - u * jnp.mean(w * u, -1, keepdims=True))
        )

    return (
        jnp.stack(mixed, 1),
        jnp.stack(tokens_grad, 1),
        gain_grad,
        shift_grad,
        grad_qkv,
        bias_sums[: parts * width].reshape(parts, width),
        grad_dense,
        rest[2],
        grad_up,
        bias_sums[parts * width :],
        grad_down,
        rest[2],
    )


def solution(mesh):
    batch, branch, tensor = (mesh.shape[a] for a in ("batch", "branch", "tensor"))
    inner = Mesh(mesh.devices.reshape(batch, branch, tensor // 2, 2), ("batch", "branch", "line", "near"))
    tensor = ("line", "near")
    rows = P(None, FOLD, tensor, None)
    first = P(FOLD, None, tensor)
    weights = (first, P(None, tensor), P(tensor, FOLD), P(), P(FOLD, tensor), P(tensor), P(tensor, FOLD), P())
    return jax.shard_map(
        partial(body, inner.shape["line"]),
        mesh=inner,
        in_specs=(rows, rows, P(None, FOLD, None), P(None, FOLD, None), P(), P(), *weights),
        out_specs=(rows, rows, P(), P(), *weights),
        check_vma=False,
    )
```

```python
from functools import partial

import jax
import jax.numpy as jnp
from jax import lax
from jax.experimental import pallas as pl
from jax.experimental.pallas import tpu as pltpu
from jax.sharding import Mesh
from jax.sharding import PartitionSpec as P

HEAD_DIM = 64
ROT = 32
LANES = 128
VMEM = 60 * 2**20
COST = {"attention": 100, "attention_grad": 100, "mlp_act": 100, "mlp_pre": 60, "mixed_part": 60, "back_part": 100,
        "weight_grad": 100, "heads_grad": 100, "project": 50, "assemble": 8, "assemble_heads": 14}


def cost(units):
    return pl.CostEstimate(flops=units * 250000000 + 1, bytes_accessed=units * 250000 + 1, transcendentals=0)


eps_norm = 1e-05
rope_base = 10000.0
masked_score = -1e30
f32 = jnp.float32
bf16 = jnp.bfloat16

NN = (((1,), (0,)), ((), ()))
NT = (((1,), (1,)), ((), ()))
TN = (((0,), (0,)), ((), ()))


def mm(a, b, dims=NN):
    return lax.dot_general(a, b, dims, preferred_element_type=f32)


def call(kernel, deps, args, *, grid, in_specs, out_specs, out_shape, name, scratch=(), prefetch=0):
    deps = list(deps)
    inputs = prefetch + len(in_specs)

    def run(*refs):
        kernel(*refs[:inputs], *refs[inputs + len(deps) :])

    spec = pltpu.PrefetchScalarGridSpec(
        num_scalar_prefetch=prefetch,
        grid=grid,
        in_specs=list(in_specs) + [pl.BlockSpec(memory_space=pl.ANY)] * len(deps),
        out_specs=out_specs,
        scratch_shapes=list(scratch),
    )
    return pl.pallas_call(
        run,
        grid_spec=spec,
        out_shape=out_shape,
        compiler_params=pltpu.CompilerParams(vmem_limit_bytes=VMEM),
        cost_estimate=cost(COST[name]),
        name=name,
    )(*args, *deps)


def tie(a, *deps, units=0):
    return pl.pallas_call(
        lambda *refs: None,
        in_specs=[pl.BlockSpec(memory_space=pl.ANY)] * (1 + len(deps)),
        out_specs=pl.BlockSpec(memory_space=pl.ANY),
        out_shape=jax.ShapeDtypeStruct(a.shape, a.dtype),
        input_output_aliases={0: 0},
        cost_estimate=cost(units),
        name="tie",
    )(a, *deps)


def project_kernel(a_ref, w_ref, out_ref):
    rows = a_ref.shape[0]
    step = min(512, rows)
    for i in range(rows // step):
        at = slice(i * step, (i + 1) * step)
        out_ref[at] = mm(a_ref[at], w_ref[...]).astype(out_ref.dtype)


def project(a, w, dtype, deps=()):
    rows, depth = a.shape
    cols = w.shape[1]
    bn = 256 if cols % 256 == 0 else 128
    return call(
        project_kernel,
        deps,
        (a, w),
        grid=(cols // bn,),
        in_specs=[pl.BlockSpec((rows, depth), lambda j: (0, 0)), pl.BlockSpec((depth, bn), lambda j: (0, j))],
        out_specs=pl.BlockSpec((rows, bn), lambda j: (0, j)),
        out_shape=jax.ShapeDtypeStruct((rows, cols), dtype),
        name="project",
    )


def rope_tables(token_place):
    full_len = token_place.shape[0]
    half = ROT // 2
    inverse = rope_base ** (-(jnp.arange(half, dtype=f32) * (2.0 / ROT)))
    angles = token_place.astype(f32)[:, None] * inverse
    c, s = jnp.cos(angles), jnp.sin(angles)
    rest = (full_len, HEAD_DIM - ROT)
    zero_half = jnp.zeros((full_len, half), f32)
    cos = jnp.concatenate([c, c, jnp.ones(rest, f32)], 1)
    sa = jnp.concatenate([-s, zero_half, jnp.zeros(rest, f32)], 1)
    sb = jnp.concatenate([zero_half, s, jnp.zeros(rest, f32)], 1)
    return tuple(jnp.tile(t, (1, LANES // HEAD_DIM)) for t in (cos, sa, sb))


def attn_kernel(
    q_ref, k_ref, v_ref, qb_ref, kb_ref, vb_ref, cos_ref, sa_ref, sb_ref, segr_ref, segc_ref, out_ref, keep_ref, log_ref
):
    full_len = q_ref.shape[0]
    size = min(256, full_len)
    half = ROT // 2
    heads = LANES // HEAD_DIM
    cos, sa, sb = cos_ref[...], sa_ref[...], sb_ref[...]

    def rope(x):
        return x * cos + pltpu.roll(x, LANES - half, 1) * sa + pltpu.roll(x, half, 1) * sb

    lane = lax.broadcasted_iota(jnp.int32, (1, LANES), 1)
    q = (rope(q_ref[...] + qb_ref[...]) * (HEAD_DIM**-0.5)).astype(bf16)
    k = rope(k_ref[...] + kb_ref[...]).astype(bf16)
    v = (v_ref[...] + vb_ref[...]).astype(bf16)
    keep_ref[0] = q
    keep_ref[1] = k
    keep_ref[2] = v
    v_t = v.astype(f32).T.astype(bf16)
    tri = lax.broadcasted_iota(jnp.int32, (size, size), 0) <= lax.broadcasted_iota(jnp.int32, (size, size), 1)
    zero = jnp.zeros((), bf16)
    for j in range(full_len // size):
        cols = slice(j * size, (j + 1) * size)
        seg_q = segr_ref[:, cols]
        out_rows = []
        for h in range(heads):
            mine = (lane >= h * HEAD_DIM) & (lane < (h + 1) * HEAD_DIM)
            span = slice(h * HEAD_DIM, (h + 1) * HEAD_DIM)
            qh = jnp.where(mine, q[cols], zero)
            tiles, top, total, out = [], None, None, None
            for i in range(j + 1):
                rows = slice(i * size, (i + 1) * size)
                ok = segc_ref[rows] == seg_q
                if i == j:
                    ok = ok & tri
                s = jnp.where(ok, mm(k[rows], qh, NT), masked_score)
                m = jnp.max(s, 0, keepdims=True)
                top = m if top is None else jnp.maximum(top, m)
                tiles.append(s)
            for i in range(j + 1):
                e = jnp.exp(tiles[i] - top)
                t = jnp.sum(e, 0, keepdims=True)
                total = t if total is None else total + t
                t = mm(v_t[span, i * size : (i + 1) * size], e.astype(bf16))
                out = t if out is None else out + t
            out_rows.append(out * (1.0 / total))
            log_ref[h : h + 1, cols] = top + jnp.log(total)
        out_ref[cols] = jnp.concatenate(out_rows, 0).T.astype(bf16)


def attention(proj, bias, tables, segment, deps=()):
    full_len, wide = proj.shape
    width = wide // 3
    pairs = width // LANES
    bias = bias.reshape(1, wide)

    def part(c):
        return pl.BlockSpec((full_len, LANES), lambda p: (0, c * pairs + p))

    def bias_part(c):
        return pl.BlockSpec((1, LANES), lambda p: (0, c * pairs + p))

    def whole(*shape):
        return pl.BlockSpec(shape, lambda p: (0, 0))

    table = whole(full_len, LANES)
    return call(
        attn_kernel,
        deps,
        (proj, proj, proj, bias, bias, bias, *tables, segment.reshape(1, -1), segment.reshape(-1, 1)),
        grid=(pairs,),
        in_specs=[part(0), part(1), part(2), bias_part(0), bias_part(1), bias_part(2), table, table, table,
                  whole(1, full_len), whole(full_len, 1)],
        out_specs=[
            pl.BlockSpec((full_len, LANES), lambda p: (0, p)),
            pl.BlockSpec((3, full_len, LANES), lambda p: (0, 0, p)),
            pl.BlockSpec((8, full_len), lambda p: (p, 0)),
        ],
        out_shape=[
            jax.ShapeDtypeStruct((full_len, width), bf16),
            jax.ShapeDtypeStruct((3, full_len, width), bf16),
            jax.ShapeDtypeStruct((8 * pairs, full_len), f32),
        ],
        name="attention",
    )


def attn_grad_kernel(
    keep_ref, log_ref, ao_ref, ga_ref, cos_ref, sa_ref, sb_ref, segr_ref, segc_ref, dp_ref, db_ref, dk_acc, dv_acc
):
    full_len = ao_ref.shape[0]
    size = min(256, full_len)
    half = ROT // 2
    heads = LANES // HEAD_DIM
    cos, sa, sb = cos_ref[...], sa_ref[...], sb_ref[...]

    def unrope(g):
        return g * cos + pltpu.roll(g * sa, half, 1) + pltpu.roll(g * sb, LANES - half, 1)

    lane = lax.broadcasted_iota(jnp.int32, (1, LANES), 1)
    q, k, v, do = keep_ref[0], keep_ref[1], keep_ref[2], ga_ref[...]
    k_t = k.astype(f32).T.astype(bf16)
    inner_t = (do.astype(f32) * ao_ref[...].astype(f32)).T
    tri = lax.broadcasted_iota(jnp.int32, (size, size), 0) <= lax.broadcasted_iota(jnp.int32, (size, size), 1)
    zero = jnp.zeros((), bf16)
    dq_blocks = []
    for j in range(full_len // size):
        cols = slice(j * size, (j + 1) * size)
        seg_q = segr_ref[:, cols]
        spans, masks, queries, grads, logs, inners = [], [], [], [], [], []
        for h in range(heads):
            mine = (lane >= h * HEAD_DIM) & (lane < (h + 1) * HEAD_DIM)
            spans.append(slice(h * HEAD_DIM, (h + 1) * HEAD_DIM))
            queries.append(jnp.where(mine, q[cols], zero))
            grads.append(jnp.where(mine, do[cols], zero))
            logs.append(log_ref[h : h + 1, cols])
            inners.append(jnp.sum(inner_t[spans[h], cols], 0, keepdims=True))
        dq = [None] * heads
        for i in range(j + 1):
            rows = slice(i * size, (i + 1) * size)
            ok = segc_ref[rows] == seg_q
            if i == j:
                ok = ok & tri
            dv = dk = None
            for h in range(heads):
                p = jnp.exp(jnp.where(ok, mm(k[rows], queries[h], NT) - logs[h], masked_score))
                g = (p * (mm(v[rows], grads[h], NT) - inners[h])).astype(bf16)
                t = mm(p.astype(bf16), grads[h])
                dv = t if dv is None else dv + t
                t = mm(g, queries[h])
                dk = t if dk is None else dk + t
                t = mm(k_t[spans[h], rows], g)
                dq[h] = t if dq[h] is None else dq[h] + t
            if i == j:
                dv_acc[rows] = dv
                dk_acc[rows] = dk
            else:
                dv_acc[rows] += dv
                dk_acc[rows] += dk
        dq_blocks.append((jnp.concatenate(dq, 0) * (HEAD_DIM**-0.5)).T)
    dq = unrope(jnp.concatenate(dq_blocks, 0)).astype(bf16)
    dk = unrope(dk_acc[...]).astype(bf16)
    dv = dv_acc[...].astype(bf16)
    for part, g in enumerate((dq, dk, dv)):
        dp_ref[part] = g
        db_ref[part : part + 1] = jnp.sum(g.astype(f32), 0, keepdims=True)


def attention_grad(keep, logs, attn, grad_attn, tables, segment, deps=()):
    _, full_len, width = keep.shape

    def whole(*shape):
        return pl.BlockSpec(shape, lambda p: (0, 0))

    table = whole(full_len, LANES)
    cols = pl.BlockSpec((full_len, LANES), lambda p: (0, p))
    three = pl.BlockSpec((3, full_len, LANES), lambda p: (0, 0, p))
    return call(
        attn_grad_kernel,
        deps,
        (keep, logs, attn, grad_attn, *tables, segment.reshape(1, -1), segment.reshape(-1, 1)),
        grid=(width // LANES,),
        in_specs=[three, pl.BlockSpec((8, full_len), lambda p: (p, 0)), cols, cols, table, table, table,
                  whole(1, full_len), whole(full_len, 1)],
        out_specs=[three, pl.BlockSpec((8, LANES), lambda p: (0, p))],
        out_shape=[jax.ShapeDtypeStruct((3, full_len, width), bf16), jax.ShapeDtypeStruct((8, width), f32)],
        scratch=[pltpu.VMEM((full_len, LANES), f32), pltpu.VMEM((full_len, LANES), f32)],
        name="attention_grad",
    )


def act_kernel(n_ref, up_ref, bias_ref, act_ref, slope_ref):
    rows = n_ref.shape[0]
    step = min(256, rows)
    k0 = 0.7978845608028654
    k1 = k0 * 0.044715
    for i in range(rows // step):
        at = slice(i * step, (i + 1) * step)
        v = mm(n_ref[at], up_ref[...]) + bias_ref[...]
        v2 = v * v
        t = jnp.tanh(v * (k0 + k1 * v2))
        h = 0.5 * t + 0.5
        act_ref[at] = (v * h).astype(bf16)
        slope_ref[at] = (h + v * (1.0 - t * t) * (0.5 * k0 + 1.5 * k1 * v2)).astype(bf16)


def mlp_act(n, up, bias, deps=()):
    rows, depth = n.shape
    near, _, hidden = up.shape
    br, bh = min(1024, rows), min(512, hidden)
    per = hidden // bh
    out = pl.BlockSpec((br, bh), lambda j, i: (i, j))
    shape = jax.ShapeDtypeStruct((rows, near * hidden), bf16)
    return call(
        act_kernel,
        deps,
        (n, up, bias.reshape(1, -1)),
        grid=(near * per, rows // br),
        in_specs=[pl.BlockSpec((br, depth), lambda j, i: (i, 0)),
                  pl.BlockSpec((None, depth, bh), lambda j, i: (j // per, 0, j % per)),
                  pl.BlockSpec((1, bh), lambda j, i: (0, j))],
        out_specs=[out, out],
        out_shape=[shape, shape],
        name="mlp_act",
    )


def pre_kernel(c_ref, down_ref, slope_ref, pre_ref, sum_ref):
    rows = c_ref.shape[0]
    step = min(256, rows)
    total = None
    for i in range(rows // step):
        at = slice(i * step, (i + 1) * step)
        p = (mm(c_ref[at], down_ref[...]) * slope_ref[at].astype(f32)).astype(bf16)
        pre_ref[at] = p
        s = jnp.sum(p.astype(f32), 0, keepdims=True)
        total = s if total is None else total + s
    sum_ref[...] = jnp.broadcast_to(total, sum_ref.shape)


def mlp_pre(c, down_t, slope, deps=()):
    rows, depth = c.shape
    near, _, hidden = down_t.shape
    br, bh = min(1024, rows), min(512, hidden)
    per = hidden // bh
    out = pl.BlockSpec((br, bh), lambda j, i: (i, j))
    pre, sums = call(
        pre_kernel,
        deps,
        (c, down_t, slope),
        grid=(near * per, rows // br),
        in_specs=[pl.BlockSpec((br, depth), lambda j, i: (i, 0)),
                  pl.BlockSpec((None, depth, bh), lambda j, i: (j // per, 0, j % per)), out],
        out_specs=[out, pl.BlockSpec((8, bh), lambda j, i: (i, j))],
        out_shape=[
            jax.ShapeDtypeStruct((rows, near * hidden), bf16),
            jax.ShapeDtypeStruct((rows // br * 8, near * hidden), f32),
        ],
        name="mlp_pre",
    )
    return pre, jnp.sum(sums.reshape(-1, 8, near * hidden)[:, 0], 0)


def mixed_kernel(act_ref, attn_ref, down_ref, dense_ref, out_ref):
    rows = act_ref.shape[0]
    near, _, hidden = down_ref.shape
    step = min(512, rows)
    for i in range(rows // step):
        at = slice(i * step, (i + 1) * step)
        total = mm(attn_ref[at], dense_ref[...], NT)
        for r in range(near):
            total = total + mm(act_ref[at, r * hidden : (r + 1) * hidden], down_ref[r], NT)
        out_ref[at] = total.astype(bf16)


def mixed_part(act, attn, down_t, dense_t, deps=()):
    rows = act.shape[0]
    width = attn.shape[1]
    near, depth, hidden = down_t.shape
    br, bn = min(1024, rows), min(512, depth)
    return call(
        mixed_kernel,
        deps,
        (act, attn, down_t, dense_t),
        grid=(depth // bn, rows // br),
        in_specs=[pl.BlockSpec((br, near * hidden), lambda j, i: (i, 0)), pl.BlockSpec((br, width), lambda j, i: (i, 0)),
                  pl.BlockSpec((near, bn, hidden), lambda j, i: (0, j, 0)), pl.BlockSpec((bn, width), lambda j, i: (j, 0))],
        out_specs=pl.BlockSpec((br, bn), lambda j, i: (i, j)),
        out_shape=jax.ShapeDtypeStruct((rows, depth), bf16),
        name="mixed_part",
    )


def back_kernel(pre_ref, dp_ref, up_ref, qkv_ref, n_ref, out_ref, sum_ref):
    rows = pre_ref.shape[0]
    near, _, hidden = up_ref.shape
    parts, _, width = dp_ref.shape
    step = min(512, rows)
    plain = scaled = None
    for i in range(rows // step):
        at = slice(i * step, (i + 1) * step)
        total = None
        for r in range(near):
            t = mm(pre_ref[at, r * hidden : (r + 1) * hidden], up_ref[r], NT)
            total = t if total is None else total + t
        for c in range(parts):
            total = total + mm(dp_ref[c, at], qkv_ref[:, c * width : (c + 1) * width], NT)
        out_ref[at] = total.astype(bf16)
        a = jnp.sum(total, 0, keepdims=True)
        b = jnp.sum(total * n_ref[at].astype(f32), 0, keepdims=True)
        plain = a if plain is None else plain + a
        scaled = b if scaled is None else scaled + b
    sum_ref[0:1] = plain
    sum_ref[1:2] = scaled


def back_part(pre, dp, up, qkv, n, deps=()):
    rows = pre.shape[0]
    parts, _, width = dp.shape
    near, depth, hidden = up.shape
    br, bn = min(1024, rows), min(512, depth)
    out, sums = call(
        back_kernel,
        deps,
        (pre, dp, up, qkv, n),
        grid=(depth // bn, rows // br),
        in_specs=[pl.BlockSpec((br, near * hidden), lambda j, i: (i, 0)), pl.BlockSpec((parts, br, width), lambda j, i: (0, i, 0)),
                  pl.BlockSpec((near, bn, hidden), lambda j, i: (0, j, 0)), pl.BlockSpec((bn, parts * width), lambda j, i: (j, 0)),
                  pl.BlockSpec((br, bn), lambda j, i: (i, j))],
        out_specs=[pl.BlockSpec((br, bn), lambda j, i: (i, j)), pl.BlockSpec((8, bn), lambda j, i: (i, j))],
        out_shape=[jax.ShapeDtypeStruct((rows, depth), bf16), jax.ShapeDtypeStruct((rows // br * 8, depth), f32)],
        name="back_part",
    )
    return out, jnp.sum(sums.reshape(-1, 8, depth)[:, :2], 0)


def store_quarters(at_ref, total, held, keep_ref, send_ref):
    held[...] = total.astype(bf16)
    rows = held.shape[0] // 4
    y, core = at_ref[0], at_ref[1]
    for d in range(2):
        row = 2 * (1 - y if d else y)
        keep_ref[d] = held[pl.ds(pl.multiple_of((row + core) * rows, rows), rows)]
        send_ref[d] = held[pl.ds(pl.multiple_of((row + 1 - core) * rows, rows), rows)]


def weight_grad(at, xs, ys, deps=()):
    rows, m = xs[0].shape
    hidden = ys[0].shape[1] // 2
    tile = min(hidden, 512)
    per = hidden // tile
    count = len(xs)

    def kernel(at_ref, *refs):
        total = None
        for x, y in zip(refs[:count], refs[count : 2 * count], strict=True):
            t = mm(x[...], y[...], TN)
            total = t if total is None else total + t
        keep_ref, send_ref, held = refs[2 * count :]
        store_quarters(at_ref, total, held, keep_ref, send_ref)

    x_spec = pl.BlockSpec((rows, m), lambda j, at: (0, 0), pipeline_mode=pl.Buffered(1))
    y_spec = pl.BlockSpec((rows, tile), lambda j, at: (0, j))
    out = pl.BlockSpec((None, 2, m // 4, tile), lambda j, at: (j // per, 0, 0, j % per))
    shape = jax.ShapeDtypeStruct((2, 2, m // 4, hidden), bf16)
    return call(
        kernel,
        deps,
        (at, *xs, *ys),
        grid=(2 * per,),
        in_specs=[x_spec] * count + [y_spec] * count,
        out_specs=[out, out],
        out_shape=[shape, shape],
        scratch=[pltpu.VMEM((m, tile), bf16)],
        prefetch=1,
        name="weight_grad",
    )


def heads_grad(at, ns, dps, cs, attns, deps=()):
    parts, rows, wide = dps[0].shape
    m = ns[0].shape[1]
    width = wide // 2
    count = len(ns)
    out_cols = (parts + 1) * width
    if width % LANES:
        blocks = [sum(mm(n, dp[c], TN) for n, dp in zip(ns, dps, strict=True)) for c in range(parts)]
        blocks.append(sum(mm(c, a, TN) for c, a in zip(cs, attns, strict=True)))
        g = jnp.stack([jnp.concatenate([b[:, r * width : (r + 1) * width] for b in blocks], 1) for r in range(2)], 0)
        g = g.astype(bf16).reshape(2, 2, 2, m // 4, out_cols)
        g = jnp.where(at[0] == 0, g, g[:, ::-1])
        return jnp.where(at[1] == 0, g[:, :, 0], g[:, :, 1]), jnp.where(at[1] == 0, g[:, :, 1], g[:, :, 0])

    def kernel(at_ref, *refs):
        n_refs, dp_refs, c_refs, a_refs = (refs[i * count : (i + 1) * count] for i in range(4))
        keep_ref, send_ref, held = refs[4 * count :]
        part = pl.program_id(0)

        def store(total):
            for d in range(2):
                store_quarters(at_ref, total[:, d * width : (d + 1) * width], held, keep_ref.at[d], send_ref.at[d])

        @pl.when(part < parts)
        def _():
            store(sum(mm(n[...], d[...], TN) for n, d in zip(n_refs, dp_refs, strict=True)))

        @pl.when(part == parts)
        def _():
            store(sum(mm(c[...], a[...], TN) for c, a in zip(c_refs, a_refs, strict=True)))

    x_spec = pl.BlockSpec((rows, m), lambda p, at: (0, 0), pipeline_mode=pl.Buffered(1))
    dp_spec = pl.BlockSpec((None, rows, wide), lambda p, at: (jnp.minimum(p, parts - 1), 0, 0))
    a_spec = pl.BlockSpec((rows, wide), lambda p, at: (0, 0))
    out = pl.BlockSpec((2, 2, m // 4, width), lambda p, at: (0, 0, 0, p))
    shape = jax.ShapeDtypeStruct((2, 2, m // 4, out_cols), bf16)
    return call(
        kernel,
        deps,
        (at, *ns, *dps, *cs, *attns),
        grid=(parts + 1,),
        in_specs=[x_spec] * count + [dp_spec] * count + [x_spec] * count + [a_spec] * count,
        out_specs=[out, out],
        out_shape=[shape, shape],
        scratch=[pltpu.VMEM((m, width), bf16)],
        prefetch=1,
        name="heads_grad",
    )


SWAP = [(0, 1), (1, 0)]
FOLD = ("batch", "branch")


def flip(a, axis):
    return lax.ppermute(a, axis, SWAP)


def pick(a, index, axis=0):
    return lax.dynamic_index_in_dim(a, index, axis, keepdims=False)


def block_row(at_ref, k):
    y, core = at_ref[0], at_ref[1]
    chip, other = k // 2, k % 2
    return chip % 2, 2 * (1 - y if chip // 2 else y) + (1 - core if other else core)


def assemble(blocks, at, deps=()):
    rows, cols = blocks[0].shape
    tile = 256 if cols % 256 == 0 else cols

    def kernel(at_ref, *refs):
        for k in range(8):
            d, row = block_row(at_ref, k)
            refs[8][d, pl.ds(pl.multiple_of(row * rows, rows), rows)] = refs[k][...]

    return call(
        kernel,
        deps,
        (at, *blocks),
        grid=(cols // tile,),
        in_specs=[pl.BlockSpec((rows, tile), lambda j, at: (0, j))] * 8,
        out_specs=pl.BlockSpec((2, 4 * rows, tile), lambda j, at: (0, 0, j)),
        out_shape=jax.ShapeDtypeStruct((2, 4 * rows, cols), blocks[0].dtype),
        prefetch=1,
        name="assemble",
    )


def assemble_heads(blocks, at, parts, width, deps=()):
    rows, cols = blocks[0].shape
    hidden = cols - (parts + 1) * width
    if width % LANES:
        w = assemble(blocks, at)
        columns = [w[r, :, c * width : (c + 1) * width] for c in range(parts + 1) for r in range(2)]
        return jnp.concatenate(columns[: 2 * parts], 1), jnp.concatenate(columns[2 * parts :], 1), w[:, :, cols - hidden :]

    def kernel(at_ref, *refs):
        qkv_ref, dense_ref, up_ref = refs[8:]
        j = pl.program_id(0)
        for k in range(8):
            d, row = block_row(at_ref, k)
            at = pl.ds(pl.multiple_of(row * rows, rows), rows)
            for d_k in range(2):
                if d_k != d:
                    continue

                @pl.when(j < parts)
                def _():
                    qkv_ref[at, d_k * width : (d_k + 1) * width] = refs[k][...]

                @pl.when(j == parts)
                def _():
                    dense_ref[at, d_k * width : (d_k + 1) * width] = refs[k][...]

                @pl.when(j > parts)
                def _():
                    up_ref[d_k, at] = refs[k][...]

    depth = 4 * rows
    return call(
        kernel,
        deps,
        (at, *blocks),
        grid=(cols // width,),
        in_specs=[pl.BlockSpec((rows, width), lambda j, at: (0, j))] * 8,
        out_specs=[
            pl.BlockSpec((depth, 2 * width), lambda j, at: (0, jnp.minimum(j, parts - 1))),
            pl.BlockSpec((depth, 2 * width), lambda j, at: (0, 0)),
            pl.BlockSpec((2, depth, width), lambda j, at: (0, 0, jnp.maximum(j - parts - 1, 0))),
        ],
        out_shape=[
            jax.ShapeDtypeStruct((depth, 2 * parts * width), bf16),
            jax.ShapeDtypeStruct((depth, 2 * width), bf16),
            jax.ShapeDtypeStruct((2, depth, hidden), bf16),
        ],
        prefetch=1,
        name="assemble_heads",
    )


class Gather:
    def __init__(self, w):
        self.w = w
        self.half = w.shape[0] // 2
        self.blocks = [w, flip(w, "branch")]

    def first(self, *deps):
        w = tie(self.w, *deps) if deps else self.w
        self.x, self.y = flip(w, "near"), flip(w, "batch")

    def second(self, *deps):
        if deps:
            self.x, self.y = (tie(a, *deps) for a in (self.x, self.y))
        self.halves = self.y[: self.half], self.x[self.half :]
        self.corner = flip(self.halves[0], "near"), flip(self.halves[1], "batch")

    def third(self):
        for b in (self.x, self.y, jnp.concatenate(self.corner, 0)):
            self.blocks += [b, flip(b, "branch")]
        return self.blocks


class Scatter:
    def __init__(self, keep, send):
        self.keep, self.got = keep, flip(send, "branch")
        self.half = keep.shape[2] // 2

    def first(self, *deps):
        g = self.keep + (tie(self.got, *deps) if deps else self.got)
        corner = g[1, 1]
        self.own, self.to_y, self.to_x = g[0, 0], g[0, 1], g[1, 0]
        self.got = flip(corner[: self.half], "near"), flip(corner[self.half :], "batch")
        return (self.own,)

    def second(self, *deps):
        h = self.half
        got = tuple(tie(a, *deps) for a in self.got) if deps else self.got
        to_y = jnp.concatenate([self.to_y[:h] + got[0], self.to_y[h:]], 0)
        to_x = jnp.concatenate([self.to_x[:h], self.to_x[h:] + got[1]], 0)
        self.got = flip(to_x, "near"), flip(to_y, "batch")
        return to_x, to_y

    def result(self, *deps):
        got = tuple(tie(a, *deps) for a in self.got) if deps else self.got
        return self.own.astype(f32) + got[0].astype(f32) + got[1].astype(f32)


def body(
    line_size,
    tokens,
    cotangent,
    segments,
    positions,
    ln_gain,
    ln_bias,
    qkv_weight,
    qkv_bias,
    dense_weight,
    dense_bias,
    up_weight,
    up_bias,
    down_weight,
    down_bias,
):
    micros, seqs, shard, depth = tokens.shape
    full_len = segments.shape[2]
    quarter, parts, width = qkv_weight.shape
    hidden = up_weight.shape[1]
    x, y, core, z = (lax.axis_index(a) for a in ("near", "batch", "branch", "line"))
    first = x == 0

    def to_group(a, start=(), end=()):
        send = jnp.where(first, a[1], a[0])
        got = flip(tie(send, *start) if start else send, "near")
        kept = jnp.where(first, a[0], a[1])
        got = tie(got, *end) if end else got
        return jnp.concatenate([jnp.where(first, kept, got), jnp.where(first, got, kept)], 0)

    def from_group(a):
        lo, hi = a[:shard], a[shard:]
        send = jnp.where(first, hi, lo)
        got = flip(send, "near")

        def finish(*deps):
            other = tie(got, *deps) if deps else got
            kept = jnp.where(first, lo, hi)
            return jnp.where(first, kept, other), jnp.where(first, other, kept)

        return send, finish

    at = jnp.stack([y, core]).astype(jnp.int32)

    units, scales, groups_n, groups_c = [], [], [], []
    for s in range(seqs):
        r = tokens[:, s].astype(f32)
        centered = r - jnp.mean(r, -1, keepdims=True)
        scales.append(lax.rsqrt(jnp.mean(centered * centered, -1, keepdims=True) + eps_norm))
        units.append(centered * scales[s])

    def normed(s):
        return (units[s] * ln_gain + ln_bias).astype(bf16)

    def gather_rows(group):
        return lax.all_gather(group, "line", axis=0, tiled=True)

    segment = jnp.where(first, segments[0], segments[1])
    place = jnp.where(first, positions[0], positions[1])
    tables = [rope_tables(place[s]) for s in range(seqs)]
    n_0 = to_group(normed(0))
    c_0 = to_group(cotangent[:, 0], (n_0,))
    rows_n, rows_c = [gather_rows(n_0)], [gather_rows(c_0)]
    early = Gather(jnp.concatenate([qkv_weight.reshape(quarter, parts * width), dense_weight.T, up_weight], 1))
    late = Gather(down_weight.T)
    early.first(c_0)
    early.second(*tables[0], *tables[1])
    late.first(*early.corner)
    qkv, dense_t, up = assemble_heads(early.third(), at, parts, width)
    bias_qkv = jnp.concatenate([qkv_bias, flip(qkv_bias, "near")], 1)
    bias_up = jnp.concatenate([up_bias, flip(up_bias, "near")], 0)

    def scatter_rows(part):
        return lax.psum_scatter(part, "line", scatter_dimension=0, tiled=True)

    proj = project(rows_n[0], qkv, f32)
    n_1 = to_group(normed(1), early.corner, (dense_t,))
    late.second(proj)
    attn_0, keep, log = attention(proj, bias_qkv, tables[0], segment[0], (n_1, *late.halves))
    rows_n.append(gather_rows(n_1))
    act_0, slope = mlp_act(rows_n[0], up, bias_up, (attn_0, *late.corner))
    down_t = assemble(late.third(), at, (act_0,))
    part = mixed_part(act_0, attn_0, down_t, dense_t)
    mixed_0 = scatter_rows(part)
    c_1 = to_group(cotangent[:, 1], (act_0,), (part,))
    rows_c.append(gather_rows(c_1))
    grad_attn = project(rows_c[0], dense_t, bf16, (part, c_1))
    dp_0, db_0 = attention_grad(keep, log, attn_0, grad_attn, tables[0], segment[0])
    pre_0, up_0 = mlp_pre(rows_c[0], down_t, slope, (dp_0,))
    part, back_0 = back_part(pre_0, dp_0, up, qkv, rows_n[0])
    back_sum_0 = scatter_rows(part)
    proj = project(rows_n[1], qkv, f32, (part,))
    attn_1, keep, log = attention(proj, bias_qkv, tables[1], segment[1])
    act_1, slope = mlp_act(rows_n[1], up, bias_up, (attn_1,))
    pre_1, up_1 = mlp_pre(rows_c[1], down_t, slope)
    grad_up = Scatter(*weight_grad(at, rows_n, (pre_0, pre_1)))
    grad_down = Scatter(*weight_grad(at, rows_c, (act_0, act_1), (grad_up.keep,)))
    sends = grad_up.first(grad_down.keep)
    part = mixed_part(act_1, attn_1, down_t, dense_t, sends)
    mixed_1 = scatter_rows(part)
    send, finish = from_group(tie(mixed_0, part))
    grad_attn = project(rows_c[1], dense_t, bf16, (part, send))
    dp_1, db_1 = attention_grad(keep, log, attn_1, grad_attn, tables[1], segment[1])
    mixed_0 = finish(dp_1)
    sends = (*grad_up.second(dp_1), *grad_down.first(dp_1))
    part, back_1 = back_part(pre_1, dp_1, up, qkv, rows_n[1], (*sends, *mixed_0))
    back_sum_1 = scatter_rows(part)
    sends = grad_down.second(part)
    grad_up = grad_up.result()
    grad_heads = Scatter(*heads_grad(at, rows_n, (dp_0, dp_1), rows_c, (attn_0, attn_1), (*sends, grad_up)))
    grad_down = grad_down.result(grad_heads.keep)
    sum_qkv = (db_0 + db_1)[:parts].reshape(parts, 2, width)
    sum_up = (up_0 + up_1).reshape(2, hidden)
    out_bias = jnp.sum(cotangent, (0, 1, 2), dtype=f32)
    own, other = (jnp.concatenate([sum_qkv[:, d].reshape(-1), sum_up[d]]) for d in range(2))
    rest = jnp.concatenate([(back_0 + back_1).reshape(-1), out_bias])
    size = own.shape[0]
    sums = jnp.concatenate([own, rest]) + tie(flip(jnp.concatenate([other, rest]), "near"), grad_heads.keep)
    got = flip(sums, "batch")
    own_heads = grad_heads.first(tie(grad_down[:8, :LANES], sums, units=200))
    sums = sums + tie(got, *own_heads)
    _, finish = from_group(tie(back_sum_0, *own_heads))
    sums = sums + flip(sums, "branch")
    sends = grad_heads.second(sums)
    back_sum_0 = finish(*sends)
    mixed_1 = from_group(tie(mixed_1, *back_sum_0))[1]()
    bias_sums, rest = sums[:size], tie(sums[size:], *sends)
    reach = 1
    while reach < line_size:
        rest = rest + lax.ppermute(rest, "line", [(i, i ^ reach) for i in range(line_size)])
        reach *= 2
    grad_down = grad_down.T
    grad_heads = grad_heads.result()
    grad_qkv = grad_heads[:, : parts * width].reshape(quarter, parts, width)
    grad_dense = grad_heads[:, parts * width :].T
    rest = rest.reshape(3, depth)
    shift_grad = rest[0]
    gain_grad = (rest[1] - ln_bias * shift_grad) / ln_gain

    mixed, tokens_grad = [], []
    back_sum_1 = from_group(tie(back_sum_1, *mixed_1, rest))[1]()
    for s, (m, g) in enumerate(((mixed_0, back_sum_0), (mixed_1, back_sum_1))):
        mixed.append((tokens[:, s].astype(f32) + jnp.stack(m, 0).astype(f32) + dense_bias + down_bias).astype(bf16))
        w = jnp.stack(g, 0).astype(f32) * ln_gain
        u = units[s]
        tokens_grad.append(
            cotangent[:, s].astype(f32)
            + scales[s] * (w - jnp.mean(w, -1, keepdims=True) - u * jnp.mean(w * u, -1, keepdims=True))
        )

    return (
        jnp.stack(mixed, 1),
        jnp.stack(tokens_grad, 1),
        gain_grad,
        shift_grad,
        grad_qkv,
        bias_sums[: parts * width].reshape(parts, width),
        grad_dense,
        rest[2],
        grad_up,
        bias_sums[parts * width :],
        grad_down,
        rest[2],
    )


def solution(mesh):
    batch, branch, tensor = (mesh.shape[a] for a in ("batch", "branch", "tensor"))
    inner = Mesh(mesh.devices.reshape(batch, branch, tensor // 2, 2), ("batch", "branch", "line", "near"))
    tensor = ("line", "near")
    rows = P(None, FOLD, tensor, None)
    first = P(FOLD, None, tensor)
    weights = (first, P(None, tensor), P(tensor, FOLD), P(), P(FOLD, tensor), P(tensor), P(tensor, FOLD), P())
    return jax.shard_map(
        partial(body, inner.shape["line"]),
        mesh=inner,
        in_specs=(rows, rows, P(None, FOLD, None), P(None, FOLD, None), P(), P(), *weights),
        out_specs=(rows, rows, P(), P(), *weights),
        check_vma=False,
    )
```

```python
from functools import partial

import jax
import jax.numpy as jnp
from jax import lax
from jax.experimental import pallas as pl
from jax.experimental.pallas import tpu as pltpu
from jax.sharding import Mesh
from jax.sharding import PartitionSpec as P

HEAD_DIM = 64
ROT = 32
LANES = 128
VMEM = 60 * 2**20
COST = {"attention": 100, "attention_grad": 100, "mlp_act": 100, "mlp_pre": 60, "mixed_part": 60, "back_part": 100,
        "weight_grad": 100, "heads_grad": 100, "project": 50, "assemble": 8, "assemble_heads": 14}


def cost(units):
    return pl.CostEstimate(flops=units * 250000000 + 1, bytes_accessed=units * 250000 + 1, transcendentals=0)


eps_norm = 1e-05
rope_base = 10000.0
masked_score = -1e30
f32 = jnp.float32
bf16 = jnp.bfloat16

NN = (((1,), (0,)), ((), ()))
NT = (((1,), (1,)), ((), ()))
TN = (((0,), (0,)), ((), ()))


def mm(a, b, dims=NN):
    return lax.dot_general(a, b, dims, preferred_element_type=f32)


def call(kernel, deps, args, *, grid, in_specs, out_specs, out_shape, name, scratch=(), prefetch=0):
    deps = list(deps)
    inputs = prefetch + len(in_specs)

    def run(*refs):
        kernel(*refs[:inputs], *refs[inputs + len(deps) :])

    spec = pltpu.PrefetchScalarGridSpec(
        num_scalar_prefetch=prefetch,
        grid=grid,
        in_specs=list(in_specs) + [pl.BlockSpec(memory_space=pl.ANY)] * len(deps),
        out_specs=out_specs,
        scratch_shapes=list(scratch),
    )
    return pl.pallas_call(
        run,
        grid_spec=spec,
        out_shape=out_shape,
        compiler_params=pltpu.CompilerParams(vmem_limit_bytes=VMEM),
        cost_estimate=cost(COST[name]),
        name=name,
    )(*args, *deps)


def tie(a, *deps, units=0):
    return pl.pallas_call(
        lambda *refs: None,
        in_specs=[pl.BlockSpec(memory_space=pl.ANY)] * (1 + len(deps)),
        out_specs=pl.BlockSpec(memory_space=pl.ANY),
        out_shape=jax.ShapeDtypeStruct(a.shape, a.dtype),
        input_output_aliases={0: 0},
        cost_estimate=cost(units),
        name="tie",
    )(a, *deps)


def project_kernel(a_ref, w_ref, out_ref):
    rows = a_ref.shape[0]
    step = min(512, rows)
    for i in range(rows // step):
        at = slice(i * step, (i + 1) * step)
        out_ref[at] = mm(a_ref[at], w_ref[...]).astype(out_ref.dtype)


def project(a, w, dtype, deps=()):
    rows, depth = a.shape
    cols = w.shape[1]
    bn = 256 if cols % 256 == 0 else 128
    return call(
        project_kernel,
        deps,
        (a, w),
        grid=(cols // bn,),
        in_specs=[pl.BlockSpec((rows, depth), lambda j: (0, 0)), pl.BlockSpec((depth, bn), lambda j: (0, j))],
        out_specs=pl.BlockSpec((rows, bn), lambda j: (0, j)),
        out_shape=jax.ShapeDtypeStruct((rows, cols), dtype),
        name="project",
    )


def rope_tables(token_place):
    full_len = token_place.shape[0]
    half = ROT // 2
    inverse = rope_base ** (-(jnp.arange(half, dtype=f32) * (2.0 / ROT)))
    angles = token_place.astype(f32)[:, None] * inverse
    c, s = jnp.cos(angles), jnp.sin(angles)
    rest = (full_len, HEAD_DIM - ROT)
    zero_half = jnp.zeros((full_len, half), f32)
    cos = jnp.concatenate([c, c, jnp.ones(rest, f32)], 1)
    sa = jnp.concatenate([-s, zero_half, jnp.zeros(rest, f32)], 1)
    sb = jnp.concatenate([zero_half, s, jnp.zeros(rest, f32)], 1)
    return tuple(jnp.tile(t, (1, LANES // HEAD_DIM)) for t in (cos, sa, sb))


def attn_kernel(
    q_ref, k_ref, v_ref, qb_ref, kb_ref, vb_ref, cos_ref, sa_ref, sb_ref, segr_ref, segc_ref, out_ref, keep_ref, log_ref
):
    full_len = q_ref.shape[0]
    size = min(256, full_len)
    half = ROT // 2
    heads = LANES // HEAD_DIM
    cos, sa, sb = cos_ref[...], sa_ref[...], sb_ref[...]

    def rope(x):
        return x * cos + pltpu.roll(x, LANES - half, 1) * sa + pltpu.roll(x, half, 1) * sb

    lane = lax.broadcasted_iota(jnp.int32, (1, LANES), 1)
    q = (rope(q_ref[...] + qb_ref[...]) * (HEAD_DIM**-0.5)).astype(bf16)
    k = rope(k_ref[...] + kb_ref[...]).astype(bf16)
    v = (v_ref[...] + vb_ref[...]).astype(bf16)
    keep_ref[0] = q
    keep_ref[1] = k
    keep_ref[2] = v
    v_t = v.astype(f32).T.astype(bf16)
    tri = lax.broadcasted_iota(jnp.int32, (size, size), 0) <= lax.broadcasted_iota(jnp.int32, (size, size), 1)
    zero = jnp.zeros((), bf16)
    for j in range(full_len // size):
        cols = slice(j * size, (j + 1) * size)
        seg_q = segr_ref[:, cols]
        out_rows = []
        for h in range(heads):
            mine = (lane >= h * HEAD_DIM) & (lane < (h + 1) * HEAD_DIM)
            span = slice(h * HEAD_DIM, (h + 1) * HEAD_DIM)
            qh = jnp.where(mine, q[cols], zero)
            tiles, top, total, out = [], None, None, None
            for i in range(j + 1):
                rows = slice(i * size, (i + 1) * size)
                ok = segc_ref[rows] == seg_q
                if i == j:
                    ok = ok & tri
                s = jnp.where(ok, mm(k[rows], qh, NT), masked_score)
                m = jnp.max(s, 0, keepdims=True)
                top = m if top is None else jnp.maximum(top, m)
                tiles.append(s)
            for i in range(j + 1):
                e = jnp.exp(tiles[i] - top)
                t = jnp.sum(e, 0, keepdims=True)
                total = t if total is None else total + t
                t = mm(v_t[span, i * size : (i + 1) * size], e.astype(bf16))
                out = t if out is None else out + t
            out_rows.append(out * (1.0 / total))
            log_ref[h : h + 1, cols] = top + jnp.log(total)
        out_ref[cols] = jnp.concatenate(out_rows, 0).T.astype(bf16)


def attention(proj, bias, tables, segment, deps=()):
    full_len, wide = proj.shape
    width = wide // 3
    pairs = width // LANES
    bias = bias.reshape(1, wide)

    def part(c):
        return pl.BlockSpec((full_len, LANES), lambda p: (0, c * pairs + p))

    def bias_part(c):
        return pl.BlockSpec((1, LANES), lambda p: (0, c * pairs + p))

    def whole(*shape):
        return pl.BlockSpec(shape, lambda p: (0, 0))

    table = whole(full_len, LANES)
    return call(
        attn_kernel,
        deps,
        (proj, proj, proj, bias, bias, bias, *tables, segment.reshape(1, -1), segment.reshape(-1, 1)),
        grid=(pairs,),
        in_specs=[part(0), part(1), part(2), bias_part(0), bias_part(1), bias_part(2), table, table, table,
                  whole(1, full_len), whole(full_len, 1)],
        out_specs=[
            pl.BlockSpec((full_len, LANES), lambda p: (0, p)),
            pl.BlockSpec((3, full_len, LANES), lambda p: (0, 0, p)),
            pl.BlockSpec((8, full_len), lambda p: (p, 0)),
        ],
        out_shape=[
            jax.ShapeDtypeStruct((full_len, width), bf16),
            jax.ShapeDtypeStruct((3, full_len, width), bf16),
            jax.ShapeDtypeStruct((8 * pairs, full_len), f32),
        ],
        name="attention",
    )


def attn_grad_kernel(
    keep_ref, log_ref, ao_ref, ga_ref, cos_ref, sa_ref, sb_ref, segr_ref, segc_ref, dp_ref, db_ref, dk_acc, dv_acc
):
    full_len = ao_ref.shape[0]
    size = min(256, full_len)
    half = ROT // 2
    heads = LANES // HEAD_DIM
    cos, sa, sb = cos_ref[...], sa_ref[...], sb_ref[...]

    def unrope(g):
        return g * cos + pltpu.roll(g * sa, half, 1) + pltpu.roll(g * sb, LANES - half, 1)

    lane = lax.broadcasted_iota(jnp.int32, (1, LANES), 1)
    q, k, v, do = keep_ref[0], keep_ref[1], keep_ref[2], ga_ref[...]
    k_t = k.astype(f32).T.astype(bf16)
    inner_t = (do.astype(f32) * ao_ref[...].astype(f32)).T
    tri = lax.broadcasted_iota(jnp.int32, (size, size), 0) <= lax.broadcasted_iota(jnp.int32, (size, size), 1)
    zero = jnp.zeros((), bf16)
    dq_blocks = []
    for j in range(full_len // size):
        cols = slice(j * size, (j + 1) * size)
        seg_q = segr_ref[:, cols]
        spans, masks, queries, grads, logs, inners = [], [], [], [], [], []
        for h in range(heads):
            mine = (lane >= h * HEAD_DIM) & (lane < (h + 1) * HEAD_DIM)
            spans.append(slice(h * HEAD_DIM, (h + 1) * HEAD_DIM))
            queries.append(jnp.where(mine, q[cols], zero))
            grads.append(jnp.where(mine, do[cols], zero))
            logs.append(log_ref[h : h + 1, cols])
            inners.append(jnp.sum(inner_t[spans[h], cols], 0, keepdims=True))
        dq = [None] * heads
        for i in range(j + 1):
            rows = slice(i * size, (i + 1) * size)
            ok = segc_ref[rows] == seg_q
            if i == j:
                ok = ok & tri
            dv = dk = None
            for h in range(heads):
                p = jnp.exp(jnp.where(ok, mm(k[rows], queries[h], NT) - logs[h], masked_score))
                g = (p * (mm(v[rows], grads[h], NT) - inners[h])).astype(bf16)
                t = mm(p.astype(bf16), grads[h])
                dv = t if dv is None else dv + t
                t = mm(g, queries[h])
                dk = t if dk is None else dk + t
                t = mm(k_t[spans[h], rows], g)
                dq[h] = t if dq[h] is None else dq[h] + t
            if i == j:
                dv_acc[rows] = dv
                dk_acc[rows] = dk
            else:
                dv_acc[rows] += dv
                dk_acc[rows] += dk
        dq_blocks.append((jnp.concatenate(dq, 0) * (HEAD_DIM**-0.5)).T)
    dq = unrope(jnp.concatenate(dq_blocks, 0)).astype(bf16)
    dk = unrope(dk_acc[...]).astype(bf16)
    dv = dv_acc[...].astype(bf16)
    for part, g in enumerate((dq, dk, dv)):
        dp_ref[part] = g
        db_ref[part : part + 1] = jnp.sum(g.astype(f32), 0, keepdims=True)


def attention_grad(keep, logs, attn, grad_attn, tables, segment, deps=()):
    _, full_len, width = keep.shape

    def whole(*shape):
        return pl.BlockSpec(shape, lambda p: (0, 0))

    table = whole(full_len, LANES)
    cols = pl.BlockSpec((full_len, LANES), lambda p: (0, p))
    three = pl.BlockSpec((3, full_len, LANES), lambda p: (0, 0, p))
    return call(
        attn_grad_kernel,
        deps,
        (keep, logs, attn, grad_attn, *tables, segment.reshape(1, -1), segment.reshape(-1, 1)),
        grid=(width // LANES,),
        in_specs=[three, pl.BlockSpec((8, full_len), lambda p: (p, 0)), cols, cols, table, table, table,
                  whole(1, full_len), whole(full_len, 1)],
        out_specs=[three, pl.BlockSpec((8, LANES), lambda p: (0, p))],
        out_shape=[jax.ShapeDtypeStruct((3, full_len, width), bf16), jax.ShapeDtypeStruct((8, width), f32)],
        scratch=[pltpu.VMEM((full_len, LANES), f32), pltpu.VMEM((full_len, LANES), f32)],
        name="attention_grad",
    )


def act_kernel(n_ref, up_ref, bias_ref, act_ref, slope_ref):
    rows = n_ref.shape[0]
    step = min(256, rows)
    k0 = 0.7978845608028654
    k1 = k0 * 0.044715
    for i in range(rows // step):
        at = slice(i * step, (i + 1) * step)
        v = mm(n_ref[at], up_ref[...]) + bias_ref[...]
        v2 = v * v
        t = jnp.tanh(v * (k0 + k1 * v2))
        h = 0.5 * t + 0.5
        act_ref[at] = (v * h).astype(bf16)
        slope_ref[at] = (h + v * (1.0 - t * t) * (0.5 * k0 + 1.5 * k1 * v2)).astype(bf16)


def mlp_act(n, up, bias, deps=()):
    rows, depth = n.shape
    near, _, hidden = up.shape
    br, bh = min(1024, rows), min(512, hidden)
    per = hidden // bh
    out = pl.BlockSpec((br, bh), lambda j, i: (i, j))
    shape = jax.ShapeDtypeStruct((rows, near * hidden), bf16)
    return call(
        act_kernel,
        deps,
        (n, up, bias.reshape(1, -1)),
        grid=(near * per, rows // br),
        in_specs=[pl.BlockSpec((br, depth), lambda j, i: (i, 0)),
                  pl.BlockSpec((None, depth, bh), lambda j, i: (j // per, 0, j % per)),
                  pl.BlockSpec((1, bh), lambda j, i: (0, j))],
        out_specs=[out, out],
        out_shape=[shape, shape],
        name="mlp_act",
    )


def pre_kernel(c_ref, down_ref, slope_ref, pre_ref, sum_ref):
    rows = c_ref.shape[0]
    step = min(256, rows)
    total = None
    for i in range(rows // step):
        at = slice(i * step, (i + 1) * step)
        p = (mm(c_ref[at], down_ref[...]) * slope_ref[at].astype(f32)).astype(bf16)
        pre_ref[at] = p
        s = jnp.sum(p.astype(f32), 0, keepdims=True)
        total = s if total is None else total + s
    sum_ref[...] = jnp.broadcast_to(total, sum_ref.shape)


def mlp_pre(c, down_t, slope, deps=()):
    rows, depth = c.shape
    near, _, hidden = down_t.shape
    br, bh = min(1024, rows), min(512, hidden)
    per = hidden // bh
    out = pl.BlockSpec((br, bh), lambda j, i: (i, j))
    pre, sums = call(
        pre_kernel,
        deps,
        (c, down_t, slope),
        grid=(near * per, rows // br),
        in_specs=[pl.BlockSpec((br, depth), lambda j, i: (i, 0)),
                  pl.BlockSpec((None, depth, bh), lambda j, i: (j // per, 0, j % per)), out],
        out_specs=[out, pl.BlockSpec((8, bh), lambda j, i: (i, j))],
        out_shape=[
            jax.ShapeDtypeStruct((rows, near * hidden), bf16),
            jax.ShapeDtypeStruct((rows // br * 8, near * hidden), f32),
        ],
        name="mlp_pre",
    )
    return pre, jnp.sum(sums.reshape(-1, 8, near * hidden)[:, 0], 0)


def mixed_kernel(act_ref, attn_ref, down_ref, dense_ref, out_ref):
    rows = act_ref.shape[0]
    near, _, hidden = down_ref.shape
    step = min(512, rows)
    for i in range(rows // step):
        at = slice(i * step, (i + 1) * step)
        total = mm(attn_ref[at], dense_ref[...], NT)
        for r in range(near):
            total = total + mm(act_ref[at, r * hidden : (r + 1) * hidden], down_ref[r], NT)
        out_ref[at] = total.astype(bf16)


def mixed_part(act, attn, down_t, dense_t, deps=()):
    rows = act.shape[0]
    width = attn.shape[1]
    near, depth, hidden = down_t.shape
    br, bn = min(1024, rows), min(512, depth)
    return call(
        mixed_kernel,
        deps,
        (act, attn, down_t, dense_t),
        grid=(depth // bn, rows // br),
        in_specs=[pl.BlockSpec((br, near * hidden), lambda j, i: (i, 0)), pl.BlockSpec((br, width), lambda j, i: (i, 0)),
                  pl.BlockSpec((near, bn, hidden), lambda j, i: (0, j, 0)), pl.BlockSpec((bn, width), lambda j, i: (j, 0))],
        out_specs=pl.BlockSpec((br, bn), lambda j, i: (i, j)),
        out_shape=jax.ShapeDtypeStruct((rows, depth), bf16),
        name="mixed_part",
    )


def back_kernel(pre_ref, dp_ref, up_ref, qkv_ref, n_ref, out_ref, sum_ref):
    rows = pre_ref.shape[0]
    near, _, hidden = up_ref.shape
    parts, _, width = dp_ref.shape
    step = min(512, rows)
    plain = scaled = None
    for i in range(rows // step):
        at = slice(i * step, (i + 1) * step)
        total = None
        for r in range(near):
            t = mm(pre_ref[at, r * hidden : (r + 1) * hidden], up_ref[r], NT)
            total = t if total is None else total + t
        for c in range(parts):
            total = total + mm(dp_ref[c, at], qkv_ref[:, c * width : (c + 1) * width], NT)
        out_ref[at] = total.astype(bf16)
        a = jnp.sum(total, 0, keepdims=True)
        b = jnp.sum(total * n_ref[at].astype(f32), 0, keepdims=True)
        plain = a if plain is None else plain + a
        scaled = b if scaled is None else scaled + b
    sum_ref[0:1] = plain
    sum_ref[1:2] = scaled


def back_part(pre, dp, up, qkv, n, deps=()):
    rows = pre.shape[0]
    parts, _, width = dp.shape
    near, depth, hidden = up.shape
    br, bn = min(1024, rows), min(512, depth)
    out, sums = call(
        back_kernel,
        deps,
        (pre, dp, up, qkv, n),
        grid=(depth // bn, rows // br),
        in_specs=[pl.BlockSpec((br, near * hidden), lambda j, i: (i, 0)), pl.BlockSpec((parts, br, width), lambda j, i: (0, i, 0)),
                  pl.BlockSpec((near, bn, hidden), lambda j, i: (0, j, 0)), pl.BlockSpec((bn, parts * width), lambda j, i: (j, 0)),
                  pl.BlockSpec((br, bn), lambda j, i: (i, j))],
        out_specs=[pl.BlockSpec((br, bn), lambda j, i: (i, j)), pl.BlockSpec((8, bn), lambda j, i: (i, j))],
        out_shape=[jax.ShapeDtypeStruct((rows, depth), bf16), jax.ShapeDtypeStruct((rows // br * 8, depth), f32)],
        name="back_part",
    )
    return out, jnp.sum(sums.reshape(-1, 8, depth)[:, :2], 0)


def store_quarters(at_ref, total, held, keep_ref, send_ref):
    held[...] = total.astype(bf16)
    rows = held.shape[0] // 4
    y, core = at_ref[0], at_ref[1]
    for d in range(2):
        row = 2 * (1 - y if d else y)
        keep_ref[d] = held[pl.ds(pl.multiple_of((row + core) * rows, rows), rows)]
        send_ref[d] = held[pl.ds(pl.multiple_of((row + 1 - core) * rows, rows), rows)]


def weight_grad(at, xs, ys, deps=()):
    rows, m = xs[0].shape
    hidden = ys[0].shape[1] // 2
    tile = min(hidden, 512)
    per = hidden // tile
    count = len(xs)

    def kernel(at_ref, *refs):
        total = None
        for x, y in zip(refs[:count], refs[count : 2 * count], strict=True):
            t = mm(x[...], y[...], TN)
            total = t if total is None else total + t
        keep_ref, send_ref, held = refs[2 * count :]
        store_quarters(at_ref, total, held, keep_ref, send_ref)

    x_spec = pl.BlockSpec((rows, m), lambda j, at: (0, 0), pipeline_mode=pl.Buffered(1))
    y_spec = pl.BlockSpec((rows, tile), lambda j, at: (0, j))
    out = pl.BlockSpec((None, 2, m // 4, tile), lambda j, at: (j // per, 0, 0, j % per))
    shape = jax.ShapeDtypeStruct((2, 2, m // 4, hidden), bf16)
    return call(
        kernel,
        deps,
        (at, *xs, *ys),
        grid=(2 * per,),
        in_specs=[x_spec] * count + [y_spec] * count,
        out_specs=[out, out],
        out_shape=[shape, shape],
        scratch=[pltpu.VMEM((m, tile), bf16)],
        prefetch=1,
        name="weight_grad",
    )


def heads_grad(at, ns, dps, cs, attns, deps=()):
    parts, rows, wide = dps[0].shape
    m = ns[0].shape[1]
    width = wide // 2
    count = len(ns)
    out_cols = (parts + 1) * width
    if width % LANES:
        blocks = [sum(mm(n, dp[c], TN) for n, dp in zip(ns, dps, strict=True)) for c in range(parts)]
        blocks.append(sum(mm(c, a, TN) for c, a in zip(cs, attns, strict=True)))
        g = jnp.stack([jnp.concatenate([b[:, r * width : (r + 1) * width] for b in blocks], 1) for r in range(2)], 0)
        g = g.astype(bf16).reshape(2, 2, 2, m // 4, out_cols)
        g = jnp.where(at[0] == 0, g, g[:, ::-1])
        return jnp.where(at[1] == 0, g[:, :, 0], g[:, :, 1]), jnp.where(at[1] == 0, g[:, :, 1], g[:, :, 0])

    def kernel(at_ref, *refs):
        n_refs, dp_refs, c_refs, a_refs = (refs[i * count : (i + 1) * count] for i in range(4))
        keep_ref, send_ref, held = refs[4 * count :]
        part = pl.program_id(0)

        def store(total):
            for d in range(2):
                store_quarters(at_ref, total[:, d * width : (d + 1) * width], held, keep_ref.at[d], send_ref.at[d])

        @pl.when(part < parts)
        def _():
            store(sum(mm(n[...], d[...], TN) for n, d in zip(n_refs, dp_refs, strict=True)))

        @pl.when(part == parts)
        def _():
            store(sum(mm(c[...], a[...], TN) for c, a in zip(c_refs, a_refs, strict=True)))

    x_spec = pl.BlockSpec((rows, m), lambda p, at: (0, 0), pipeline_mode=pl.Buffered(1))
    dp_spec = pl.BlockSpec((None, rows, wide), lambda p, at: (jnp.minimum(p, parts - 1), 0, 0))
    a_spec = pl.BlockSpec((rows, wide), lambda p, at: (0, 0))
    out = pl.BlockSpec((2, 2, m // 4, width), lambda p, at: (0, 0, 0, p))
    shape = jax.ShapeDtypeStruct((2, 2, m // 4, out_cols), bf16)
    return call(
        kernel,
        deps,
        (at, *ns, *dps, *cs, *attns),
        grid=(parts + 1,),
        in_specs=[x_spec] * count + [dp_spec] * count + [x_spec] * count + [a_spec] * count,
        out_specs=[out, out],
        out_shape=[shape, shape],
        scratch=[pltpu.VMEM((m, width), bf16)],
        prefetch=1,
        name="heads_grad",
    )


SWAP = [(0, 1), (1, 0)]
FOLD = ("batch", "branch")


def flip(a, axis):
    return lax.ppermute(a, axis, SWAP)


def pick(a, index, axis=0):
    return lax.dynamic_index_in_dim(a, index, axis, keepdims=False)


def block_row(at_ref, k):
    y, core = at_ref[0], at_ref[1]
    chip, other = k // 2, k % 2
    return chip % 2, 2 * (1 - y if chip // 2 else y) + (1 - core if other else core)


def assemble(blocks, at, deps=()):
    rows, cols = blocks[0].shape
    tile = 256 if cols % 256 == 0 else cols

    def kernel(at_ref, *refs):
        for k in range(8):
            d, row = block_row(at_ref, k)
            refs[8][d, pl.ds(pl.multiple_of(row * rows, rows), rows)] = refs[k][...]

    return call(
        kernel,
        deps,
        (at, *blocks),
        grid=(cols // tile,),
        in_specs=[pl.BlockSpec((rows, tile), lambda j, at: (0, j))] * 8,
        out_specs=pl.BlockSpec((2, 4 * rows, tile), lambda j, at: (0, 0, j)),
        out_shape=jax.ShapeDtypeStruct((2, 4 * rows, cols), blocks[0].dtype),
        prefetch=1,
        name="assemble",
    )


def assemble_heads(blocks, at, parts, width, deps=()):
    rows, cols = blocks[0].shape
    hidden = cols - (parts + 1) * width
    if width % LANES:
        w = assemble(blocks, at)
        columns = [w[r, :, c * width : (c + 1) * width] for c in range(parts + 1) for r in range(2)]
        return jnp.concatenate(columns[: 2 * parts], 1), jnp.concatenate(columns[2 * parts :], 1), w[:, :, cols - hidden :]

    def kernel(at_ref, *refs):
        qkv_ref, dense_ref, up_ref = refs[8:]
        j = pl.program_id(0)
        for k in range(8):
            d, row = block_row(at_ref, k)
            at = pl.ds(pl.multiple_of(row * rows, rows), rows)
            for d_k in range(2):
                if d_k != d:
                    continue

                @pl.when(j < parts)
                def _():
                    qkv_ref[at, d_k * width : (d_k + 1) * width] = refs[k][...]

                @pl.when(j == parts)
                def _():
                    dense_ref[at, d_k * width : (d_k + 1) * width] = refs[k][...]

                @pl.when(j > parts)
                def _():
                    up_ref[d_k, at] = refs[k][...]

    depth = 4 * rows
    return call(
        kernel,
        deps,
        (at, *blocks),
        grid=(cols // width,),
        in_specs=[pl.BlockSpec((rows, width), lambda j, at: (0, j))] * 8,
        out_specs=[
            pl.BlockSpec((depth, 2 * width), lambda j, at: (0, jnp.minimum(j, parts - 1))),
            pl.BlockSpec((depth, 2 * width), lambda j, at: (0, 0)),
            pl.BlockSpec((2, depth, width), lambda j, at: (0, 0, jnp.maximum(j - parts - 1, 0))),
        ],
        out_shape=[
            jax.ShapeDtypeStruct((depth, 2 * parts * width), bf16),
            jax.ShapeDtypeStruct((depth, 2 * width), bf16),
            jax.ShapeDtypeStruct((2, depth, hidden), bf16),
        ],
        prefetch=1,
        name="assemble_heads",
    )


class Gather:
    def __init__(self, w):
        self.w = w
        self.half = w.shape[0] // 2
        self.blocks = [w, flip(w, "branch")]

    def first(self, *deps):
        w = tie(self.w, *deps) if deps else self.w
        self.x, self.y = flip(w, "near"), flip(w, "batch")

    def second(self, *deps):
        if deps:
            self.x, self.y = (tie(a, *deps) for a in (self.x, self.y))
        self.halves = self.y[: self.half], self.x[self.half :]
        self.corner = flip(self.halves[0], "near"), flip(self.halves[1], "batch")

    def third(self):
        for b in (self.x, self.y, jnp.concatenate(self.corner, 0)):
            self.blocks += [b, flip(b, "branch")]
        return self.blocks


class Scatter:
    def __init__(self, keep, send):
        self.keep, self.got = keep, flip(send, "branch")
        self.half = keep.shape[2] // 2

    def first(self, *deps):
        core = tie(self.got, *deps) if deps else self.got
        own, to_y, to_x, corner = ((self.keep[i, j], core[i, j]) for i, j in ((0, 0), (0, 1), (1, 0), (1, 1)))
        self.own, self.to_y, self.to_x = own, to_y, to_x
        corner = corner[0] + corner[1]
        self.got = flip(corner[: self.half], "near"), flip(corner[self.half :], "batch")
        return (corner,)

    def second(self, *deps):
        h = self.half
        got = tuple(tie(a, *deps) for a in self.got) if deps else self.got
        to_y, to_x = self.to_y[0] + self.to_y[1], self.to_x[0] + self.to_x[1]
        to_y = jnp.concatenate([to_y[:h] + got[0], to_y[h:]], 0)
        to_x = jnp.concatenate([to_x[:h], to_x[h:] + got[1]], 0)
        self.got = flip(to_x, "near"), flip(to_y, "batch")
        return to_x, to_y

    def result(self, *deps):
        got = tuple(tie(a, *deps) for a in self.got) if deps else self.got
        return sum(a.astype(f32) for a in (*self.own, *got))


def norm_grad(at, tokens, cotangent, kept, got, gain, s, into=None):
    micros, seqs, shard, depth = tokens.shape
    tile = min(64, shard)

    def kernel(at_ref, x_ref, c_ref, kept_ref, got_ref, gain_ref, *refs):
        x = x_ref[...].astype(f32)
        centered = x - jnp.mean(x, -1, keepdims=True)
        scale = lax.rsqrt(jnp.mean(centered * centered, -1, keepdims=True) + eps_norm)
        unit = centered * scale
        mine = pl.program_id(0) == at_ref[0]
        w = jnp.where(mine, kept_ref[...].astype(f32), got_ref[...].astype(f32)) * gain_ref[...]
        refs[-1][...] = c_ref[...].astype(f32) + scale * (
            w - jnp.mean(w, -1, keepdims=True) - unit * jnp.mean(w * unit, -1, keepdims=True)
        )

    block = pl.BlockSpec((None, None, tile, depth), lambda m, i, at: (m, s, i, 0))
    rows = pl.BlockSpec((tile, depth), lambda m, i, at: (i, 0))
    extra = [] if into is None else [into]
    return pl.pallas_call(
        kernel,
        grid_spec=pltpu.PrefetchScalarGridSpec(
            num_scalar_prefetch=1,
            grid=(micros, shard // tile),
            in_specs=[block, block, rows, rows, pl.BlockSpec((1, depth), lambda m, i, at: (0, 0))]
            + [pl.BlockSpec(memory_space=pl.ANY)] * len(extra),
            out_specs=block,
        ),
        out_shape=jax.ShapeDtypeStruct(tokens.shape, f32),
        input_output_aliases={6: 0} if extra else {},
        compiler_params=pltpu.CompilerParams(vmem_limit_bytes=VMEM),
        cost_estimate=cost(3),
        name="norm_grad",
    )(at, tokens, cotangent, kept, got, gain.reshape(1, -1), *extra)


def body(
    line_size,
    tokens,
    cotangent,
    segments,
    positions,
    ln_gain,
    ln_bias,
    qkv_weight,
    qkv_bias,
    dense_weight,
    dense_bias,
    up_weight,
    up_bias,
    down_weight,
    down_bias,
):
    micros, seqs, shard, depth = tokens.shape
    full_len = segments.shape[2]
    quarter, parts, width = qkv_weight.shape
    hidden = up_weight.shape[1]
    x, y, core, z = (lax.axis_index(a) for a in ("near", "batch", "branch", "line"))
    first = x == 0

    def to_group(a, start=(), end=()):
        send = jnp.where(first, a[1], a[0])
        got = flip(tie(send, *start) if start else send, "near")
        kept = jnp.where(first, a[0], a[1])
        got = tie(got, *end) if end else got
        return jnp.concatenate([jnp.where(first, kept, got), jnp.where(first, got, kept)], 0)

    def from_group(a):
        lo, hi = a[:shard], a[shard:]
        send = jnp.where(first, hi, lo)
        got = flip(send, "near")

        def finish(*deps, by_micro=True):
            other = tie(got, *deps) if deps else got
            kept = jnp.where(first, lo, hi)
            if not by_micro:
                return kept, other
            return jnp.where(first, kept, other), jnp.where(first, other, kept)

        return send, finish

    at = jnp.stack([y, core]).astype(jnp.int32)

    units, scales, groups_n, groups_c = [], [], [], []
    for s in range(seqs):
        r = tokens[:, s].astype(f32)
        centered = r - jnp.mean(r, -1, keepdims=True)
        scales.append(lax.rsqrt(jnp.mean(centered * centered, -1, keepdims=True) + eps_norm))
        units.append(centered * scales[s])

    def normed(s):
        return (units[s] * ln_gain + ln_bias).astype(bf16)

    def gather_rows(group):
        return lax.all_gather(group, "line", axis=0, tiled=True)

    segment = jnp.where(first, segments[0], segments[1])
    place = jnp.where(first, positions[0], positions[1])
    tables = [rope_tables(place[s]) for s in range(seqs)]
    n_0 = to_group(normed(0))
    c_0 = to_group(cotangent[:, 0], (n_0,))
    rows_n, rows_c = [gather_rows(n_0)], [gather_rows(c_0)]
    early = Gather(jnp.concatenate([qkv_weight.reshape(quarter, parts * width), dense_weight.T, up_weight], 1))
    late = Gather(down_weight.T)
    early.first(c_0)
    early.second(*tables[0], *tables[1])
    late.first(*early.corner)
    qkv, dense_t, up = assemble_heads(early.third(), at, parts, width)
    bias_qkv = jnp.concatenate([qkv_bias, flip(qkv_bias, "near")], 1)
    bias_up = jnp.concatenate([up_bias, flip(up_bias, "near")], 0)

    def scatter_rows(part):
        return lax.psum_scatter(part, "line", scatter_dimension=0, tiled=True)

    proj = project(rows_n[0], qkv, f32)
    n_1 = to_group(normed(1), early.corner, (dense_t,))
    late.second(proj)
    attn_0, keep, log = attention(proj, bias_qkv, tables[0], segment[0], (n_1, *late.halves))
    rows_n.append(gather_rows(n_1))
    act_0, slope = mlp_act(rows_n[0], up, bias_up, (attn_0, *late.corner))
    down_t = assemble(late.third(), at, (act_0,))
    part = mixed_part(act_0, attn_0, down_t, dense_t)
    both = [part]
    c_1 = to_group(cotangent[:, 1], (act_0,), (part,))
    rows_c.append(gather_rows(c_1))
    grad_attn = project(rows_c[0], dense_t, bf16, (part, c_1))
    dp_0, db_0 = attention_grad(keep, log, attn_0, grad_attn, tables[0], segment[0])
    pre_0, up_0 = mlp_pre(rows_c[0], down_t, slope, (dp_0,))
    part, back_0 = back_part(pre_0, dp_0, up, qkv, rows_n[0])
    both = jnp.stack([a.reshape(line_size, 2 * shard, depth) for a in (*both, part)], 1)
    mixed_0, back_sum_0 = lax.psum_scatter(both, "line", scatter_dimension=0, tiled=False)
    proj = project(rows_n[1], qkv, f32, (part,))
    attn_1, keep, log = attention(proj, bias_qkv, tables[1], segment[1])
    act_1, slope = mlp_act(rows_n[1], up, bias_up, (attn_1,))
    pre_1, up_1 = mlp_pre(rows_c[1], down_t, slope)
    grad_up = Scatter(*weight_grad(at, rows_n, (pre_0, pre_1)))
    grad_down = Scatter(*weight_grad(at, rows_c, (act_0, act_1), (grad_up.keep,)))
    sends = grad_up.first(grad_down.keep)
    part = mixed_part(act_1, attn_1, down_t, dense_t, sends)
    mixed_1 = scatter_rows(part)
    grad_attn = project(rows_c[1], dense_t, bf16, (part,))
    dp_1, db_1 = attention_grad(keep, log, attn_1, grad_attn, tables[1], segment[1])
    sends = (*grad_up.second(dp_1), *grad_down.first(dp_1))
    part, back_1 = back_part(pre_1, dp_1, up, qkv, rows_n[1], sends)
    back_sum_1 = scatter_rows(part)
    sends = grad_down.second(part)
    grad_up = grad_up.result()
    grad_heads = Scatter(*heads_grad(at, rows_n, (dp_0, dp_1), rows_c, (attn_0, attn_1), (*sends, grad_up)))
    grad_down = grad_down.result(grad_heads.keep)
    sum_qkv = (db_0 + db_1)[:parts].reshape(parts, 2, width)
    sum_up = (up_0 + up_1).reshape(2, hidden)
    out_bias = jnp.sum(cotangent, (0, 1, 2), dtype=f32)
    own, other = (jnp.concatenate([sum_qkv[:, d].reshape(-1), sum_up[d]]) for d in range(2))
    rest = jnp.concatenate([(back_0 + back_1).reshape(-1), out_bias])
    size = own.shape[0]
    sums = jnp.concatenate([own, rest]) + tie(flip(jnp.concatenate([other, rest]), "near"), grad_heads.keep)
    got = flip(sums, "batch")
    own_heads = grad_heads.first(tie(grad_down[:8, :LANES], sums, units=200))
    sums = sums + tie(got, *own_heads)
    _, finish_m = from_group(tie(mixed_0, *own_heads))
    _, finish = from_group(tie(back_sum_0, *own_heads))
    sums = sums + flip(sums, "branch")
    sends = grad_heads.second(sums)
    mixed_0 = finish_m(*sends)
    back_sum_0 = finish(*sends, by_micro=False)
    mixed_1 = from_group(tie(mixed_1, *back_sum_0))[1]()
    bias_sums, rest = sums[:size], tie(sums[size:], *sends)
    reach = 1
    while reach < line_size:
        rest = rest + lax.ppermute(rest, "line", [(i, i ^ reach) for i in range(line_size)])
        reach *= 2
    grad_down = grad_down.T
    grad_heads = grad_heads.result()
    grad_qkv = grad_heads[:, : parts * width].reshape(quarter, parts, width)
    grad_dense = grad_heads[:, parts * width :].T
    rest = rest.reshape(3, depth)
    shift_grad = rest[0]
    gain_grad = (rest[1] - ln_bias * shift_grad) / ln_gain

    near_at = x.astype(jnp.int32).reshape(1)
    tokens_grad = norm_grad(near_at, tokens, cotangent, *back_sum_0, ln_gain, 0)
    back_sum_1 = from_group(tie(back_sum_1, *mixed_1, rest))[1](by_micro=False)
    tokens_grad = norm_grad(near_at, tokens, cotangent, *back_sum_1, ln_gain, 1, tokens_grad)
    mixed = [
        (tokens[:, s].astype(f32) + jnp.stack(m, 0).astype(f32) + dense_bias + down_bias).astype(bf16)
        for s, m in enumerate((mixed_0, mixed_1))
    ]

    return (
        jnp.stack(mixed, 1),
        tokens_grad,
        gain_grad,
        shift_grad,
        grad_qkv,
        bias_sums[: parts * width].reshape(parts, width),
        grad_dense,
        rest[2],
        grad_up,
        bias_sums[parts * width :],
        grad_down,
        rest[2],
    )


def solution(mesh):
    batch, branch, tensor = (mesh.shape[a] for a in ("batch", "branch", "tensor"))
    inner = Mesh(mesh.devices.reshape(batch, branch, tensor // 2, 2), ("batch", "branch", "line", "near"))
    tensor = ("line", "near")
    rows = P(None, FOLD, tensor, None)
    first = P(FOLD, None, tensor)
    weights = (first, P(None, tensor), P(tensor, FOLD), P(), P(FOLD, tensor), P(tensor), P(tensor, FOLD), P())
    return jax.shard_map(
        partial(body, inner.shape["line"]),
        mesh=inner,
        in_specs=(rows, rows, P(None, FOLD, None), P(None, FOLD, None), P(), P(), *weights),
        out_specs=(rows, rows, P(), P(), *weights),
        check_vma=False,
    )
```

```python
from functools import partial

import jax
import jax.numpy as jnp
from jax import lax
from jax.experimental import pallas as pl
from jax.experimental.pallas import tpu as pltpu
from jax.sharding import Mesh
from jax.sharding import PartitionSpec as P

HEAD_DIM = 64
ROT = 32
LANES = 128
VMEM = 60 * 2**20
COST = {"attention": 100, "attention_grad": 100, "mlp_act": 100, "mlp_pre": 60, "mixed_part": 60, "back_part": 100,
        "weight_grad": 100, "heads_grad": 100, "project": 50, "assemble": 8, "assemble_heads": 14}


def cost(units):
    return pl.CostEstimate(flops=units * 250000000 + 1, bytes_accessed=units * 250000 + 1, transcendentals=0)


eps_norm = 1e-05
rope_base = 10000.0
masked_score = -1e30
f32 = jnp.float32
bf16 = jnp.bfloat16

NN = (((1,), (0,)), ((), ()))
NT = (((1,), (1,)), ((), ()))
TN = (((0,), (0,)), ((), ()))


def mm(a, b, dims=NN):
    return lax.dot_general(a, b, dims, preferred_element_type=f32)


def call(kernel, deps, args, *, grid, in_specs, out_specs, out_shape, name, scratch=(), prefetch=0):
    deps = list(deps)
    inputs = prefetch + len(in_specs)

    def run(*refs):
        kernel(*refs[:inputs], *refs[inputs + len(deps) :])

    spec = pltpu.PrefetchScalarGridSpec(
        num_scalar_prefetch=prefetch,
        grid=grid,
        in_specs=list(in_specs) + [pl.BlockSpec(memory_space=pl.ANY)] * len(deps),
        out_specs=out_specs,
        scratch_shapes=list(scratch),
    )
    return pl.pallas_call(
        run,
        grid_spec=spec,
        out_shape=out_shape,
        compiler_params=pltpu.CompilerParams(vmem_limit_bytes=VMEM),
        cost_estimate=cost(COST[name]),
        name=name,
    )(*args, *deps)


def tie(a, *deps, units=0):
    return pl.pallas_call(
        lambda *refs: None,
        in_specs=[pl.BlockSpec(memory_space=pl.ANY)] * (1 + len(deps)),
        out_specs=pl.BlockSpec(memory_space=pl.ANY),
        out_shape=jax.ShapeDtypeStruct(a.shape, a.dtype),
        input_output_aliases={0: 0},
        cost_estimate=cost(units),
        name="tie",
    )(a, *deps)


def project_kernel(a_ref, w_ref, out_ref):
    rows = a_ref.shape[0]
    step = min(512, rows)
    for i in range(rows // step):
        at = slice(i * step, (i + 1) * step)
        out_ref[at] = mm(a_ref[at], w_ref[...]).astype(out_ref.dtype)


def project(a, w, dtype, deps=()):
    rows, depth = a.shape
    cols = w.shape[1]
    bn = 256 if cols % 256 == 0 else 128
    return call(
        project_kernel,
        deps,
        (a, w),
        grid=(cols // bn,),
        in_specs=[pl.BlockSpec((rows, depth), lambda j: (0, 0)), pl.BlockSpec((depth, bn), lambda j: (0, j))],
        out_specs=pl.BlockSpec((rows, bn), lambda j: (0, j)),
        out_shape=jax.ShapeDtypeStruct((rows, cols), dtype),
        name="project",
    )


def rope_tables(token_place):
    full_len = token_place.shape[0]
    half = ROT // 2
    inverse = rope_base ** (-(jnp.arange(half, dtype=f32) * (2.0 / ROT)))
    angles = token_place.astype(f32)[:, None] * inverse
    c, s = jnp.cos(angles), jnp.sin(angles)
    rest = (full_len, HEAD_DIM - ROT)
    zero_half = jnp.zeros((full_len, half), f32)
    cos = jnp.concatenate([c, c, jnp.ones(rest, f32)], 1)
    sa = jnp.concatenate([-s, zero_half, jnp.zeros(rest, f32)], 1)
    sb = jnp.concatenate([zero_half, s, jnp.zeros(rest, f32)], 1)
    return tuple(jnp.tile(t, (1, LANES // HEAD_DIM)) for t in (cos, sa, sb))


def attn_kernel(
    q_ref, k_ref, v_ref, qb_ref, kb_ref, vb_ref, cos_ref, sa_ref, sb_ref, segr_ref, segc_ref, out_ref, keep_ref, log_ref
):
    full_len = q_ref.shape[0]
    size = min(256, full_len)
    half = ROT // 2
    heads = LANES // HEAD_DIM
    cos, sa, sb = cos_ref[...], sa_ref[...], sb_ref[...]

    def rope(x):
        return x * cos + pltpu.roll(x, LANES - half, 1) * sa + pltpu.roll(x, half, 1) * sb

    lane = lax.broadcasted_iota(jnp.int32, (1, LANES), 1)
    q = (rope(q_ref[...] + qb_ref[...]) * (HEAD_DIM**-0.5)).astype(bf16)
    k = rope(k_ref[...] + kb_ref[...]).astype(bf16)
    v = (v_ref[...] + vb_ref[...]).astype(bf16)
    keep_ref[0] = q
    keep_ref[1] = k
    keep_ref[2] = v
    v_t = v.astype(f32).T.astype(bf16)
    tri = lax.broadcasted_iota(jnp.int32, (size, size), 0) <= lax.broadcasted_iota(jnp.int32, (size, size), 1)
    zero = jnp.zeros((), bf16)
    for j in range(full_len // size):
        cols = slice(j * size, (j + 1) * size)
        seg_q = segr_ref[:, cols]
        out_rows = []
        for h in range(heads):
            mine = (lane >= h * HEAD_DIM) & (lane < (h + 1) * HEAD_DIM)
            span = slice(h * HEAD_DIM, (h + 1) * HEAD_DIM)
            qh = jnp.where(mine, q[cols], zero)
            tiles, top, total, out = [], None, None, None
            for i in range(j + 1):
                rows = slice(i * size, (i + 1) * size)
                ok = segc_ref[rows] == seg_q
                if i == j:
                    ok = ok & tri
                s = jnp.where(ok, mm(k[rows], qh, NT), masked_score)
                m = jnp.max(s, 0, keepdims=True)
                top = m if top is None else jnp.maximum(top, m)
                tiles.append(s)
            for i in range(j + 1):
                e = jnp.exp(tiles[i] - top)
                t = jnp.sum(e, 0, keepdims=True)
                total = t if total is None else total + t
                t = mm(v_t[span, i * size : (i + 1) * size], e.astype(bf16))
                out = t if out is None else out + t
            out_rows.append(out * (1.0 / total))
            log_ref[h : h + 1, cols] = top + jnp.log(total)
        out_ref[cols] = jnp.concatenate(out_rows, 0).T.astype(bf16)


def attention(proj, bias, tables, segment, deps=()):
    full_len, wide = proj.shape
    width = wide // 3
    pairs = width // LANES
    bias = bias.reshape(1, wide)

    def part(c):
        return pl.BlockSpec((full_len, LANES), lambda p: (0, c * pairs + p))

    def bias_part(c):
        return pl.BlockSpec((1, LANES), lambda p: (0, c * pairs + p))

    def whole(*shape):
        return pl.BlockSpec(shape, lambda p: (0, 0))

    table = whole(full_len, LANES)
    return call(
        attn_kernel,
        deps,
        (proj, proj, proj, bias, bias, bias, *tables, segment.reshape(1, -1), segment.reshape(-1, 1)),
        grid=(pairs,),
        in_specs=[part(0), part(1), part(2), bias_part(0), bias_part(1), bias_part(2), table, table, table,
                  whole(1, full_len), whole(full_len, 1)],
        out_specs=[
            pl.BlockSpec((full_len, LANES), lambda p: (0, p)),
            pl.BlockSpec((3, full_len, LANES), lambda p: (0, 0, p)),
            pl.BlockSpec((8, full_len), lambda p: (p, 0)),
        ],
        out_shape=[
            jax.ShapeDtypeStruct((full_len, width), bf16),
            jax.ShapeDtypeStruct((3, full_len, width), bf16),
            jax.ShapeDtypeStruct((8 * pairs, full_len), f32),
        ],
        name="attention",
    )


def attn_grad_kernel(
    keep_ref, log_ref, ao_ref, ga_ref, cos_ref, sa_ref, sb_ref, segr_ref, segc_ref, dp_ref, db_ref, dk_acc, dv_acc
):
    full_len = ao_ref.shape[0]
    size = min(256, full_len)
    half = ROT // 2
    heads = LANES // HEAD_DIM
    cos, sa, sb = cos_ref[...], sa_ref[...], sb_ref[...]

    def unrope(g):
        return g * cos + pltpu.roll(g * sa, half, 1) + pltpu.roll(g * sb, LANES - half, 1)

    lane = lax.broadcasted_iota(jnp.int32, (1, LANES), 1)
    q, k, v, do = keep_ref[0], keep_ref[1], keep_ref[2], ga_ref[...]
    k_t = k.astype(f32).T.astype(bf16)
    inner_t = (do.astype(f32) * ao_ref[...].astype(f32)).T
    tri = lax.broadcasted_iota(jnp.int32, (size, size), 0) <= lax.broadcasted_iota(jnp.int32, (size, size), 1)
    zero = jnp.zeros((), bf16)
    dq_blocks = []
    for j in range(full_len // size):
        cols = slice(j * size, (j + 1) * size)
        seg_q = segr_ref[:, cols]
        spans, masks, queries, grads, logs, inners = [], [], [], [], [], []
        for h in range(heads):
            mine = (lane >= h * HEAD_DIM) & (lane < (h + 1) * HEAD_DIM)
            spans.append(slice(h * HEAD_DIM, (h + 1) * HEAD_DIM))
            queries.append(jnp.where(mine, q[cols], zero))
            grads.append(jnp.where(mine, do[cols], zero))
            logs.append(log_ref[h : h + 1, cols])
            inners.append(jnp.sum(inner_t[spans[h], cols], 0, keepdims=True))
        dq = [None] * heads
        for i in range(j + 1):
            rows = slice(i * size, (i + 1) * size)
            ok = segc_ref[rows] == seg_q
            if i == j:
                ok = ok & tri
            dv = dk = None
            for h in range(heads):
                p = jnp.exp(jnp.where(ok, mm(k[rows], queries[h], NT) - logs[h], masked_score))
                g = (p * (mm(v[rows], grads[h], NT) - inners[h])).astype(bf16)
                t = mm(p.astype(bf16), grads[h])
                dv = t if dv is None else dv + t
                t = mm(g, queries[h])
                dk = t if dk is None else dk + t
                t = mm(k_t[spans[h], rows], g)
                dq[h] = t if dq[h] is None else dq[h] + t
            if i == j:
                dv_acc[rows] = dv
                dk_acc[rows] = dk
            else:
                dv_acc[rows] += dv
                dk_acc[rows] += dk
        dq_blocks.append((jnp.concatenate(dq, 0) * (HEAD_DIM**-0.5)).T)
    dq = unrope(jnp.concatenate(dq_blocks, 0)).astype(bf16)
    dk = unrope(dk_acc[...]).astype(bf16)
    dv = dv_acc[...].astype(bf16)
    for part, g in enumerate((dq, dk, dv)):
        dp_ref[part] = g
        db_ref[part : part + 1] = jnp.sum(g.astype(f32), 0, keepdims=True)


def attention_grad(keep, logs, attn, grad_attn, tables, segment, deps=()):
    _, full_len, width = keep.shape

    def whole(*shape):
        return pl.BlockSpec(shape, lambda p: (0, 0))

    table = whole(full_len, LANES)
    cols = pl.BlockSpec((full_len, LANES), lambda p: (0, p))
    three = pl.BlockSpec((3, full_len, LANES), lambda p: (0, 0, p))
    return call(
        attn_grad_kernel,
        deps,
        (keep, logs, attn, grad_attn, *tables, segment.reshape(1, -1), segment.reshape(-1, 1)),
        grid=(width // LANES,),
        in_specs=[three, pl.BlockSpec((8, full_len), lambda p: (p, 0)), cols, cols, table, table, table,
                  whole(1, full_len), whole(full_len, 1)],
        out_specs=[three, pl.BlockSpec((8, LANES), lambda p: (0, p))],
        out_shape=[jax.ShapeDtypeStruct((3, full_len, width), bf16), jax.ShapeDtypeStruct((8, width), f32)],
        scratch=[pltpu.VMEM((full_len, LANES), f32), pltpu.VMEM((full_len, LANES), f32)],
        name="attention_grad",
    )


def act_kernel(n_ref, up_ref, bias_ref, act_ref, slope_ref):
    rows = n_ref.shape[0]
    step = min(256, rows)
    k0 = 0.7978845608028654
    k1 = k0 * 0.044715
    for i in range(rows // step):
        at = slice(i * step, (i + 1) * step)
        v = mm(n_ref[at], up_ref[...]) + bias_ref[...]
        v2 = v * v
        t = jnp.tanh(v * (k0 + k1 * v2))
        h = 0.5 * t + 0.5
        act_ref[at] = (v * h).astype(bf16)
        slope_ref[at] = (h + v * (1.0 - t * t) * (0.5 * k0 + 1.5 * k1 * v2)).astype(bf16)


def mlp_act(n, up, bias, deps=()):
    rows, depth = n.shape
    near, _, hidden = up.shape
    br, bh = min(1024, rows), min(512, hidden)
    per = hidden // bh
    out = pl.BlockSpec((br, bh), lambda j, i: (i, j))
    shape = jax.ShapeDtypeStruct((rows, near * hidden), bf16)
    return call(
        act_kernel,
        deps,
        (n, up, bias.reshape(1, -1)),
        grid=(near * per, rows // br),
        in_specs=[pl.BlockSpec((br, depth), lambda j, i: (i, 0)),
                  pl.BlockSpec((None, depth, bh), lambda j, i: (j // per, 0, j % per)),
                  pl.BlockSpec((1, bh), lambda j, i: (0, j))],
        out_specs=[out, out],
        out_shape=[shape, shape],
        name="mlp_act",
    )


def pre_kernel(c_ref, down_ref, slope_ref, pre_ref, sum_ref):
    rows = c_ref.shape[0]
    step = min(256, rows)
    total = None
    for i in range(rows // step):
        at = slice(i * step, (i + 1) * step)
        p = (mm(c_ref[at], down_ref[...]) * slope_ref[at].astype(f32)).astype(bf16)
        pre_ref[at] = p
        s = jnp.sum(p.astype(f32), 0, keepdims=True)
        total = s if total is None else total + s
    sum_ref[...] = jnp.broadcast_to(total, sum_ref.shape)


def mlp_pre(c, down_t, slope, deps=()):
    rows, depth = c.shape
    near, _, hidden = down_t.shape
    br, bh = min(1024, rows), min(512, hidden)
    per = hidden // bh
    out = pl.BlockSpec((br, bh), lambda j, i: (i, j))
    pre, sums = call(
        pre_kernel,
        deps,
        (c, down_t, slope),
        grid=(near * per, rows // br),
        in_specs=[pl.BlockSpec((br, depth), lambda j, i: (i, 0)),
                  pl.BlockSpec((None, depth, bh), lambda j, i: (j // per, 0, j % per)), out],
        out_specs=[out, pl.BlockSpec((8, bh), lambda j, i: (i, j))],
        out_shape=[
            jax.ShapeDtypeStruct((rows, near * hidden), bf16),
            jax.ShapeDtypeStruct((rows // br * 8, near * hidden), f32),
        ],
        name="mlp_pre",
    )
    return pre, jnp.sum(sums.reshape(-1, 8, near * hidden)[:, 0], 0)


def mixed_kernel(act_ref, attn_ref, down_ref, dense_ref, out_ref):
    rows = act_ref.shape[0]
    near, _, hidden = down_ref.shape
    step = min(512, rows)
    for i in range(rows // step):
        at = slice(i * step, (i + 1) * step)
        total = mm(attn_ref[at], dense_ref[...], NT)
        for r in range(near):
            total = total + mm(act_ref[at, r * hidden : (r + 1) * hidden], down_ref[r], NT)
        out_ref[at] = total.astype(bf16)


def mixed_part(act, attn, down_t, dense_t, deps=()):
    rows = act.shape[0]
    width = attn.shape[1]
    near, depth, hidden = down_t.shape
    br, bn = min(1024, rows), min(512, depth)
    return call(
        mixed_kernel,
        deps,
        (act, attn, down_t, dense_t),
        grid=(depth // bn, rows // br),
        in_specs=[pl.BlockSpec((br, near * hidden), lambda j, i: (i, 0)), pl.BlockSpec((br, width), lambda j, i: (i, 0)),
                  pl.BlockSpec((near, bn, hidden), lambda j, i: (0, j, 0)), pl.BlockSpec((bn, width), lambda j, i: (j, 0))],
        out_specs=pl.BlockSpec((br, bn), lambda j, i: (i, j)),
        out_shape=jax.ShapeDtypeStruct((rows, depth), bf16),
        name="mixed_part",
    )


def back_kernel(pre_ref, dp_ref, up_ref, qkv_ref, n_ref, out_ref, sum_ref):
    rows = pre_ref.shape[0]
    near, _, hidden = up_ref.shape
    parts, _, width = dp_ref.shape
    step = min(512, rows)
    plain = scaled = None
    for i in range(rows // step):
        at = slice(i * step, (i + 1) * step)
        total = None
        for r in range(near):
            t = mm(pre_ref[at, r * hidden : (r + 1) * hidden], up_ref[r], NT)
            total = t if total is None else total + t
        for c in range(parts):
            total = total + mm(dp_ref[c, at], qkv_ref[:, c * width : (c + 1) * width], NT)
        out_ref[at] = total.astype(bf16)
        a = jnp.sum(total, 0, keepdims=True)
        b = jnp.sum(total * n_ref[at].astype(f32), 0, keepdims=True)
        plain = a if plain is None else plain + a
        scaled = b if scaled is None else scaled + b
    sum_ref[0:1] = plain
    sum_ref[1:2] = scaled


def back_part(pre, dp, up, qkv, n, deps=()):
    rows = pre.shape[0]
    parts, _, width = dp.shape
    near, depth, hidden = up.shape
    br, bn = min(1024, rows), min(512, depth)
    out, sums = call(
        back_kernel,
        deps,
        (pre, dp, up, qkv, n),
        grid=(depth // bn, rows // br),
        in_specs=[pl.BlockSpec((br, near * hidden), lambda j, i: (i, 0)), pl.BlockSpec((parts, br, width), lambda j, i: (0, i, 0)),
                  pl.BlockSpec((near, bn, hidden), lambda j, i: (0, j, 0)), pl.BlockSpec((bn, parts * width), lambda j, i: (j, 0)),
                  pl.BlockSpec((br, bn), lambda j, i: (i, j))],
        out_specs=[pl.BlockSpec((br, bn), lambda j, i: (i, j)), pl.BlockSpec((8, bn), lambda j, i: (i, j))],
        out_shape=[jax.ShapeDtypeStruct((rows, depth), bf16), jax.ShapeDtypeStruct((rows // br * 8, depth), f32)],
        name="back_part",
    )
    return out, jnp.sum(sums.reshape(-1, 8, depth)[:, :2], 0)


def store_quarters(at_ref, total, held, keep_ref, send_ref):
    held[...] = total.astype(bf16)
    rows = held.shape[0] // 4
    y, core = at_ref[0], at_ref[1]
    for d in range(2):
        row = 2 * (1 - y if d else y)
        keep_ref[d] = held[pl.ds(pl.multiple_of((row + core) * rows, rows), rows)]
        send_ref[d] = held[pl.ds(pl.multiple_of((row + 1 - core) * rows, rows), rows)]


def weight_grad(at, xs, ys, deps=()):
    rows, m = xs[0].shape
    hidden = ys[0].shape[1] // 2
    tile = min(hidden, 512)
    per = hidden // tile
    count = len(xs)

    def kernel(at_ref, *refs):
        total = None
        for x, y in zip(refs[:count], refs[count : 2 * count], strict=True):
            t = mm(x[...], y[...], TN)
            total = t if total is None else total + t
        keep_ref, send_ref, held = refs[2 * count :]
        store_quarters(at_ref, total, held, keep_ref, send_ref)

    x_spec = pl.BlockSpec((rows, m), lambda j, at: (0, 0), pipeline_mode=pl.Buffered(1))
    y_spec = pl.BlockSpec((rows, tile), lambda j, at: (0, j))
    out = pl.BlockSpec((None, 2, m // 4, tile), lambda j, at: (j // per, 0, 0, j % per))
    shape = jax.ShapeDtypeStruct((2, 2, m // 4, hidden), bf16)
    return call(
        kernel,
        deps,
        (at, *xs, *ys),
        grid=(2 * per,),
        in_specs=[x_spec] * count + [y_spec] * count,
        out_specs=[out, out],
        out_shape=[shape, shape],
        scratch=[pltpu.VMEM((m, tile), bf16)],
        prefetch=1,
        name="weight_grad",
    )


def heads_grad(at, ns, dps, cs, attns, deps=()):
    parts, rows, wide = dps[0].shape
    m = ns[0].shape[1]
    width = wide // 2
    count = len(ns)
    out_cols = (parts + 1) * width
    if width % LANES:
        blocks = [sum(mm(n, dp[c], TN) for n, dp in zip(ns, dps, strict=True)) for c in range(parts)]
        blocks.append(sum(mm(c, a, TN) for c, a in zip(cs, attns, strict=True)))
        g = jnp.stack([jnp.concatenate([b[:, r * width : (r + 1) * width] for b in blocks], 1) for r in range(2)], 0)
        g = g.astype(bf16).reshape(2, 2, 2, m // 4, out_cols)
        g = jnp.where(at[0] == 0, g, g[:, ::-1])
        return jnp.where(at[1] == 0, g[:, :, 0], g[:, :, 1]), jnp.where(at[1] == 0, g[:, :, 1], g[:, :, 0])

    def kernel(at_ref, *refs):
        n_refs, dp_refs, c_refs, a_refs = (refs[i * count : (i + 1) * count] for i in range(4))
        keep_ref, send_ref, held = refs[4 * count :]
        part = pl.program_id(0)

        def store(total):
            for d in range(2):
                store_quarters(at_ref, total[:, d * width : (d + 1) * width], held, keep_ref.at[d], send_ref.at[d])

        @pl.when(part < parts)
        def _():
            store(sum(mm(n[...], d[...], TN) for n, d in zip(n_refs, dp_refs, strict=True)))

        @pl.when(part == parts)
        def _():
            store(sum(mm(c[...], a[...], TN) for c, a in zip(c_refs, a_refs, strict=True)))

    x_spec = pl.BlockSpec((rows, m), lambda p, at: (0, 0), pipeline_mode=pl.Buffered(1))
    dp_spec = pl.BlockSpec((None, rows, wide), lambda p, at: (jnp.minimum(p, parts - 1), 0, 0))
    a_spec = pl.BlockSpec((rows, wide), lambda p, at: (0, 0))
    out = pl.BlockSpec((2, 2, m // 4, width), lambda p, at: (0, 0, 0, p))
    shape = jax.ShapeDtypeStruct((2, 2, m // 4, out_cols), bf16)
    return call(
        kernel,
        deps,
        (at, *ns, *dps, *cs, *attns),
        grid=(parts + 1,),
        in_specs=[x_spec] * count + [dp_spec] * count + [x_spec] * count + [a_spec] * count,
        out_specs=[out, out],
        out_shape=[shape, shape],
        scratch=[pltpu.VMEM((m, width), bf16)],
        prefetch=1,
        name="heads_grad",
    )


SWAP = [(0, 1), (1, 0)]
FOLD = ("batch", "branch")


def flip(a, axis):
    return lax.ppermute(a, axis, SWAP)


def pick(a, index, axis=0):
    return lax.dynamic_index_in_dim(a, index, axis, keepdims=False)


def block_row(at_ref, k):
    y, core = at_ref[0], at_ref[1]
    chip, other = k // 2, k % 2
    return chip % 2, 2 * (1 - y if chip // 2 else y) + (1 - core if other else core)


def assemble(blocks, at, deps=()):
    rows, cols = blocks[0].shape
    tile = 256 if cols % 256 == 0 else cols

    def kernel(at_ref, *refs):
        for k in range(8):
            d, row = block_row(at_ref, k)
            refs[8][d, pl.ds(pl.multiple_of(row * rows, rows), rows)] = refs[k][...]

    return call(
        kernel,
        deps,
        (at, *blocks),
        grid=(cols // tile,),
        in_specs=[pl.BlockSpec((rows, tile), lambda j, at: (0, j))] * 8,
        out_specs=pl.BlockSpec((2, 4 * rows, tile), lambda j, at: (0, 0, j)),
        out_shape=jax.ShapeDtypeStruct((2, 4 * rows, cols), blocks[0].dtype),
        prefetch=1,
        name="assemble",
    )


def assemble_heads(blocks, at, parts, width, deps=()):
    rows, cols = blocks[0].shape
    hidden = cols - (parts + 1) * width
    if width % LANES:
        w = assemble(blocks, at)
        columns = [w[r, :, c * width : (c + 1) * width] for c in range(parts + 1) for r in range(2)]
        return jnp.concatenate(columns[: 2 * parts], 1), jnp.concatenate(columns[2 * parts :], 1), w[:, :, cols - hidden :]

    def kernel(at_ref, *refs):
        qkv_ref, dense_ref, up_ref = refs[8:]
        j = pl.program_id(0)
        for k in range(8):
            d, row = block_row(at_ref, k)
            at = pl.ds(pl.multiple_of(row * rows, rows), rows)
            for d_k in range(2):
                if d_k != d:
                    continue

                @pl.when(j < parts)
                def _():
                    qkv_ref[at, d_k * width : (d_k + 1) * width] = refs[k][...]

                @pl.when(j == parts)
                def _():
                    dense_ref[at, d_k * width : (d_k + 1) * width] = refs[k][...]

                @pl.when(j > parts)
                def _():
                    up_ref[d_k, at] = refs[k][...]

    depth = 4 * rows
    return call(
        kernel,
        deps,
        (at, *blocks),
        grid=(cols // width,),
        in_specs=[pl.BlockSpec((rows, width), lambda j, at: (0, j))] * 8,
        out_specs=[
            pl.BlockSpec((depth, 2 * width), lambda j, at: (0, jnp.minimum(j, parts - 1))),
            pl.BlockSpec((depth, 2 * width), lambda j, at: (0, 0)),
            pl.BlockSpec((2, depth, width), lambda j, at: (0, 0, jnp.maximum(j - parts - 1, 0))),
        ],
        out_shape=[
            jax.ShapeDtypeStruct((depth, 2 * parts * width), bf16),
            jax.ShapeDtypeStruct((depth, 2 * width), bf16),
            jax.ShapeDtypeStruct((2, depth, hidden), bf16),
        ],
        prefetch=1,
        name="assemble_heads",
    )


class Gather:
    def __init__(self, w):
        self.w = w
        self.half = w.shape[0] // 2
        self.blocks = [w, flip(w, "branch")]

    def first(self, *deps):
        w = tie(self.w, *deps) if deps else self.w
        self.x, self.y = flip(w, "near"), flip(w, "batch")

    def second(self, *deps):
        if deps:
            self.x, self.y = (tie(a, *deps) for a in (self.x, self.y))
        self.halves = self.y[: self.half], self.x[self.half :]
        self.corner = flip(self.halves[0], "near"), flip(self.halves[1], "batch")

    def third(self):
        for b in (self.x, self.y, jnp.concatenate(self.corner, 0)):
            self.blocks += [b, flip(b, "branch")]
        return self.blocks


class Scatter:
    def __init__(self, keep, send):
        self.keep, self.got = keep, flip(send, "branch")
        self.half = keep.shape[2] // 2

    def first(self, *deps):
        core = tie(self.got, *deps) if deps else self.got
        own, to_y, to_x, corner = ((self.keep[i, j], core[i, j]) for i, j in ((0, 0), (0, 1), (1, 0), (1, 1)))
        self.own, self.to_y, self.to_x = own, to_y, to_x
        corner = corner[0] + corner[1]
        self.got = flip(corner[: self.half], "near"), flip(corner[self.half :], "batch")
        return (corner,)

    def second(self, *deps):
        h = self.half
        got = tuple(tie(a, *deps) for a in self.got) if deps else self.got
        to_y, to_x = self.to_y[0] + self.to_y[1], self.to_x[0] + self.to_x[1]
        to_y = jnp.concatenate([to_y[:h] + got[0], to_y[h:]], 0)
        to_x = jnp.concatenate([to_x[:h], to_x[h:] + got[1]], 0)
        self.got = flip(to_x, "near"), flip(to_y, "batch")
        return to_x, to_y

    def result(self, *deps):
        got = tuple(tie(a, *deps) for a in self.got) if deps else self.got
        return sum(a.astype(f32) for a in (*self.own, *got))


def norm_grad(at, tokens, cotangent, kept, got, gain, s, into=None):
    shard, depth = tokens.shape[2:]
    both = kept is not None and got is not None
    at = jnp.concatenate([at, at if got is None else 1 - at])
    kept, got = (got if kept is None else kept), (kept if got is None else got)
    tile = min(64, shard)

    def kernel(at_ref, x_ref, c_ref, kept_ref, got_ref, gain_ref, *refs):
        x = x_ref[...].astype(f32)
        centered = x - jnp.mean(x, -1, keepdims=True)
        scale = lax.rsqrt(jnp.mean(centered * centered, -1, keepdims=True) + eps_norm)
        unit = centered * scale
        grad = kept_ref[...].astype(f32)
        if both:
            grad = jnp.where(pl.program_id(0) == at_ref[0], grad, got_ref[...].astype(f32))
        w = grad * gain_ref[...]
        refs[-1][...] = c_ref[...].astype(f32) + scale * (
            w - jnp.mean(w, -1, keepdims=True) - unit * jnp.mean(w * unit, -1, keepdims=True)
        )

    block = pl.BlockSpec((None, None, tile, depth), lambda m, i, at: (m if both else at[1], s, i, 0))
    rows = pl.BlockSpec((tile, depth), lambda m, i, at: (i, 0))
    extra = [] if into is None else [into]
    return pl.pallas_call(
        kernel,
        grid_spec=pltpu.PrefetchScalarGridSpec(
            num_scalar_prefetch=1,
            grid=(2 if both else 1, shard // tile),
            in_specs=[block, block, rows, rows, pl.BlockSpec((1, depth), lambda m, i, at: (0, 0))]
            + [pl.BlockSpec(memory_space=pl.ANY)] * len(extra),
            out_specs=block,
        ),
        out_shape=jax.ShapeDtypeStruct(tokens.shape, f32),
        input_output_aliases={6: 0} if extra else {},
        compiler_params=pltpu.CompilerParams(vmem_limit_bytes=VMEM),
        cost_estimate=cost(3),
        name="norm_grad",
    )(at, tokens, cotangent, kept, got, gain.reshape(1, -1), *extra)


def body(
    line_size,
    tokens,
    cotangent,
    segments,
    positions,
    ln_gain,
    ln_bias,
    qkv_weight,
    qkv_bias,
    dense_weight,
    dense_bias,
    up_weight,
    up_bias,
    down_weight,
    down_bias,
):
    micros, seqs, shard, depth = tokens.shape
    full_len = segments.shape[2]
    quarter, parts, width = qkv_weight.shape
    hidden = up_weight.shape[1]
    x, y, core, z = (lax.axis_index(a) for a in ("near", "batch", "branch", "line"))
    first = x == 0

    def to_group(a, start=(), end=()):
        send = jnp.where(first, a[1], a[0])
        got = flip(tie(send, *start) if start else send, "near")
        kept = jnp.where(first, a[0], a[1])
        got = tie(got, *end) if end else got
        return jnp.concatenate([jnp.where(first, kept, got), jnp.where(first, got, kept)], 0)

    def from_group(a):
        lo, hi = a[:shard], a[shard:]
        send = jnp.where(first, hi, lo)
        got = flip(send, "near")

        def finish(*deps, by_micro=True):
            other = tie(got, *deps) if deps else got
            kept = jnp.where(first, lo, hi)
            if not by_micro:
                return kept, other
            return jnp.where(first, kept, other), jnp.where(first, other, kept)

        return send, finish

    at = jnp.stack([y, core]).astype(jnp.int32)

    units, scales, groups_n, groups_c = [], [], [], []
    for s in range(seqs):
        r = tokens[:, s].astype(f32)
        centered = r - jnp.mean(r, -1, keepdims=True)
        scales.append(lax.rsqrt(jnp.mean(centered * centered, -1, keepdims=True) + eps_norm))
        units.append(centered * scales[s])

    def normed(s):
        return (units[s] * ln_gain + ln_bias).astype(bf16)

    def gather_rows(group):
        return lax.all_gather(group, "line", axis=0, tiled=True)

    segment = jnp.where(first, segments[0], segments[1])
    place = jnp.where(first, positions[0], positions[1])
    tables = [rope_tables(place[s]) for s in range(seqs)]
    n_0 = to_group(normed(0))
    c_0 = to_group(cotangent[:, 0], (n_0,))
    rows_n, rows_c = [gather_rows(n_0)], [gather_rows(c_0)]
    early = Gather(jnp.concatenate([qkv_weight.reshape(quarter, parts * width), dense_weight.T, up_weight], 1))
    late = Gather(down_weight.T)
    early.first(c_0)
    early.second(*tables[0], *tables[1])
    late.first(*early.corner)
    qkv, dense_t, up = assemble_heads(early.third(), at, parts, width)
    bias_qkv = jnp.concatenate([qkv_bias, flip(qkv_bias, "near")], 1)
    bias_up = jnp.concatenate([up_bias, flip(up_bias, "near")], 0)

    def scatter_rows(part):
        return lax.psum_scatter(part, "line", scatter_dimension=0, tiled=True)

    proj = project(rows_n[0], qkv, f32)
    n_1 = to_group(normed(1), early.corner, (dense_t,))
    late.second(proj)
    attn_0, keep, log = attention(proj, bias_qkv, tables[0], segment[0], (n_1, *late.halves))
    rows_n.append(gather_rows(n_1))
    act_0, slope = mlp_act(rows_n[0], up, bias_up, (attn_0, *late.corner))
    down_t = assemble(late.third(), at, (act_0,))
    part = mixed_part(act_0, attn_0, down_t, dense_t)
    both = [part]
    c_1 = to_group(cotangent[:, 1], (act_0,), (part,))
    rows_c.append(gather_rows(c_1))
    grad_attn = project(rows_c[0], dense_t, bf16, (part, c_1))
    dp_0, db_0 = attention_grad(keep, log, attn_0, grad_attn, tables[0], segment[0])
    pre_0, up_0 = mlp_pre(rows_c[0], down_t, slope, (dp_0,))
    part, back_0 = back_part(pre_0, dp_0, up, qkv, rows_n[0])
    both = jnp.stack([a.reshape(line_size, 2 * shard, depth) for a in (*both, part)], 1)
    mixed_0, back_sum_0 = lax.psum_scatter(both, "line", scatter_dimension=0, tiled=False)
    proj = project(rows_n[1], qkv, f32, (part,))
    attn_1, keep, log = attention(proj, bias_qkv, tables[1], segment[1])
    act_1, slope = mlp_act(rows_n[1], up, bias_up, (attn_1,))
    pre_1, up_1 = mlp_pre(rows_c[1], down_t, slope)
    grad_up = Scatter(*weight_grad(at, rows_n, (pre_0, pre_1)))
    grad_down = Scatter(*weight_grad(at, rows_c, (act_0, act_1), (grad_up.keep,)))
    sends = grad_up.first(grad_down.keep)
    part = mixed_part(act_1, attn_1, down_t, dense_t, sends)
    mixed_1 = scatter_rows(part)
    grad_attn = project(rows_c[1], dense_t, bf16, (part,))
    dp_1, db_1 = attention_grad(keep, log, attn_1, grad_attn, tables[1], segment[1])
    sends = (*grad_up.second(dp_1), *grad_down.first(dp_1))
    part, back_1 = back_part(pre_1, dp_1, up, qkv, rows_n[1], sends)
    back_sum_1 = scatter_rows(part)
    sends = grad_down.second(part)
    grad_up = grad_up.result()
    grad_heads = Scatter(*heads_grad(at, rows_n, (dp_0, dp_1), rows_c, (attn_0, attn_1), (*sends, grad_up)))
    grad_down = grad_down.result(grad_heads.keep)
    sum_qkv = (db_0 + db_1)[:parts].reshape(parts, 2, width)
    sum_up = (up_0 + up_1).reshape(2, hidden)
    out_bias = jnp.sum(cotangent, (0, 1, 2), dtype=f32)
    own, other = (jnp.concatenate([sum_qkv[:, d].reshape(-1), sum_up[d]]) for d in range(2))
    rest = jnp.concatenate([(back_0 + back_1).reshape(-1), out_bias])
    size = own.shape[0]
    sums = jnp.concatenate([own, rest]) + tie(flip(jnp.concatenate([other, rest]), "near"), grad_heads.keep)
    got = flip(sums, "batch")
    own_heads = grad_heads.first(tie(grad_down[:8, :LANES], sums, units=200))
    sums = sums + tie(got, *own_heads)
    _, finish_m = from_group(tie(mixed_0, *own_heads))
    _, finish = from_group(tie(back_sum_0, *own_heads))
    sums = sums + flip(sums, "branch")
    sends = grad_heads.second(sums)
    mixed_0 = finish_m(*sends)
    back_sum_0 = finish(*sends, by_micro=False)
    mixed_1 = from_group(tie(mixed_1, *back_sum_0))[1]()
    bias_sums, rest = sums[:size], tie(sums[size:], *sends)
    reach = 1
    while reach < line_size:
        rest = rest + lax.ppermute(rest, "line", [(i, i ^ reach) for i in range(line_size)])
        reach *= 2
    grad_down = grad_down.T
    grad_heads = grad_heads.result()
    grad_qkv = grad_heads[:, : parts * width].reshape(quarter, parts, width)
    grad_dense = grad_heads[:, parts * width :].T
    rest = rest.reshape(3, depth)
    shift_grad = rest[0]
    gain_grad = (rest[1] - ln_bias * shift_grad) / ln_gain

    near_at = x.astype(jnp.int32).reshape(1)
    tokens_grad = norm_grad(near_at, tokens, cotangent, *back_sum_0, ln_gain, 0)
    back_sum_1 = from_group(tie(back_sum_1, *mixed_1, rest))[1](by_micro=False)
    tokens_grad = norm_grad(near_at, tokens, cotangent, back_sum_1[0], None, ln_gain, 1, tokens_grad)
    tokens_grad = norm_grad(near_at, tokens, cotangent, None, back_sum_1[1], ln_gain, 1, tokens_grad)
    mixed = [
        (tokens[:, s].astype(f32) + jnp.stack(m, 0).astype(f32) + dense_bias + down_bias).astype(bf16)
        for s, m in enumerate((mixed_0, mixed_1))
    ]

    return (
        jnp.stack(mixed, 1),
        tokens_grad,
        gain_grad,
        shift_grad,
        grad_qkv,
        bias_sums[: parts * width].reshape(parts, width),
        grad_dense,
        rest[2],
        grad_up,
        bias_sums[parts * width :],
        grad_down,
        rest[2],
    )


def solution(mesh):
    batch, branch, tensor = (mesh.shape[a] for a in ("batch", "branch", "tensor"))
    inner = Mesh(mesh.devices.reshape(batch, branch, tensor // 2, 2), ("batch", "branch", "line", "near"))
    tensor = ("line", "near")
    rows = P(None, FOLD, tensor, None)
    first = P(FOLD, None, tensor)
    weights = (first, P(None, tensor), P(tensor, FOLD), P(), P(FOLD, tensor), P(tensor), P(tensor, FOLD), P())
    return jax.shard_map(
        partial(body, inner.shape["line"]),
        mesh=inner,
        in_specs=(rows, rows, P(None, FOLD, None), P(None, FOLD, None), P(), P(), *weights),
        out_specs=(rows, rows, P(), P(), *weights),
        check_vma=False,
    )
```

```python
from functools import partial

import jax
import jax.numpy as jnp
from jax import lax
from jax.experimental import pallas as pl
from jax.experimental.pallas import tpu as pltpu
from jax.sharding import Mesh
from jax.sharding import PartitionSpec as P

HEAD_DIM = 64
ROT = 32
LANES = 128
VMEM = 60 * 2**20
COST = {"attention": 100, "attention_grad": 100, "mlp_act": 100, "mlp_pre": 60, "mixed_part": 60, "back_part": 100,
        "weight_grad": 100, "heads_grad": 100, "project": 50, "assemble": 8, "assemble_heads": 14}


def cost(units):
    return pl.CostEstimate(flops=units * 250000000 + 1, bytes_accessed=units * 250000 + 1, transcendentals=0)


eps_norm = 1e-05
rope_base = 10000.0
masked_score = -1e30
f32 = jnp.float32
bf16 = jnp.bfloat16

NN = (((1,), (0,)), ((), ()))
NT = (((1,), (1,)), ((), ()))
TN = (((0,), (0,)), ((), ()))


def mm(a, b, dims=NN):
    return lax.dot_general(a, b, dims, preferred_element_type=f32)


def call(kernel, deps, args, *, grid, in_specs, out_specs, out_shape, name, scratch=(), prefetch=0):
    deps = list(deps)
    inputs = prefetch + len(in_specs)

    def run(*refs):
        kernel(*refs[:inputs], *refs[inputs + len(deps) :])

    spec = pltpu.PrefetchScalarGridSpec(
        num_scalar_prefetch=prefetch,
        grid=grid,
        in_specs=list(in_specs) + [pl.BlockSpec(memory_space=pl.ANY)] * len(deps),
        out_specs=out_specs,
        scratch_shapes=list(scratch),
    )
    return pl.pallas_call(
        run,
        grid_spec=spec,
        out_shape=out_shape,
        compiler_params=pltpu.CompilerParams(vmem_limit_bytes=VMEM),
        cost_estimate=cost(COST[name]),
        name=name,
    )(*args, *deps)


def tie(a, *deps, units=0):
    return pl.pallas_call(
        lambda *refs: None,
        in_specs=[pl.BlockSpec(memory_space=pl.ANY)] * (1 + len(deps)),
        out_specs=pl.BlockSpec(memory_space=pl.ANY),
        out_shape=jax.ShapeDtypeStruct(a.shape, a.dtype),
        input_output_aliases={0: 0},
        cost_estimate=cost(units),
        name="tie",
    )(a, *deps)


def project_kernel(a_ref, w_ref, out_ref):
    rows = a_ref.shape[0]
    step = min(512, rows)
    for i in range(rows // step):
        at = slice(i * step, (i + 1) * step)
        out_ref[at] = mm(a_ref[at], w_ref[...]).astype(out_ref.dtype)


def project(a, w, dtype, deps=()):
    rows, depth = a.shape
    cols = w.shape[1]
    bn = 256 if cols % 256 == 0 else 128
    return call(
        project_kernel,
        deps,
        (a, w),
        grid=(cols // bn,),
        in_specs=[pl.BlockSpec((rows, depth), lambda j: (0, 0)), pl.BlockSpec((depth, bn), lambda j: (0, j))],
        out_specs=pl.BlockSpec((rows, bn), lambda j: (0, j)),
        out_shape=jax.ShapeDtypeStruct((rows, cols), dtype),
        name="project",
    )


def rope_tables(token_place):
    full_len = token_place.shape[0]
    half = ROT // 2
    inverse = rope_base ** (-(jnp.arange(half, dtype=f32) * (2.0 / ROT)))
    angles = token_place.astype(f32)[:, None] * inverse
    c, s = jnp.cos(angles), jnp.sin(angles)
    rest = (full_len, HEAD_DIM - ROT)
    zero_half = jnp.zeros((full_len, half), f32)
    cos = jnp.concatenate([c, c, jnp.ones(rest, f32)], 1)
    sa = jnp.concatenate([-s, zero_half, jnp.zeros(rest, f32)], 1)
    sb = jnp.concatenate([zero_half, s, jnp.zeros(rest, f32)], 1)
    return tuple(jnp.tile(t, (1, LANES // HEAD_DIM)) for t in (cos, sa, sb))


def attn_kernel(
    q_ref, k_ref, v_ref, qb_ref, kb_ref, vb_ref, cos_ref, sa_ref, sb_ref, segr_ref, segc_ref, out_ref, keep_ref, log_ref
):
    full_len = q_ref.shape[0]
    size = min(256, full_len)
    half = ROT // 2
    heads = LANES // HEAD_DIM
    cos, sa, sb = cos_ref[...], sa_ref[...], sb_ref[...]

    def rope(x):
        return x * cos + pltpu.roll(x, LANES - half, 1) * sa + pltpu.roll(x, half, 1) * sb

    lane = lax.broadcasted_iota(jnp.int32, (1, LANES), 1)
    q = (rope(q_ref[...] + qb_ref[...]) * (HEAD_DIM**-0.5)).astype(bf16)
    k = rope(k_ref[...] + kb_ref[...]).astype(bf16)
    v = (v_ref[...] + vb_ref[...]).astype(bf16)
    keep_ref[0] = q
    keep_ref[1] = k
    keep_ref[2] = v
    v_t = v.astype(f32).T.astype(bf16)
    tri = lax.broadcasted_iota(jnp.int32, (size, size), 0) <= lax.broadcasted_iota(jnp.int32, (size, size), 1)
    zero = jnp.zeros((), bf16)
    for j in range(full_len // size):
        cols = slice(j * size, (j + 1) * size)
        seg_q = segr_ref[:, cols]
        out_rows = []
        for h in range(heads):
            mine = (lane >= h * HEAD_DIM) & (lane < (h + 1) * HEAD_DIM)
            span = slice(h * HEAD_DIM, (h + 1) * HEAD_DIM)
            qh = jnp.where(mine, q[cols], zero)
            tiles, top, total, out = [], None, None, None
            for i in range(j + 1):
                rows = slice(i * size, (i + 1) * size)
                ok = segc_ref[rows] == seg_q
                if i == j:
                    ok = ok & tri
                s = jnp.where(ok, mm(k[rows], qh, NT), masked_score)
                m = jnp.max(s, 0, keepdims=True)
                top = m if top is None else jnp.maximum(top, m)
                tiles.append(s)
            for i in range(j + 1):
                e = jnp.exp(tiles[i] - top)
                t = jnp.sum(e, 0, keepdims=True)
                total = t if total is None else total + t
                t = mm(v_t[span, i * size : (i + 1) * size], e.astype(bf16))
                out = t if out is None else out + t
            out_rows.append(out * (1.0 / total))
            log_ref[h : h + 1, cols] = top + jnp.log(total)
        out_ref[cols] = jnp.concatenate(out_rows, 0).T.astype(bf16)


def attention(proj, bias, tables, segment, deps=()):
    full_len, wide = proj.shape
    width = wide // 3
    pairs = width // LANES
    bias = bias.reshape(1, wide)

    def part(c):
        return pl.BlockSpec((full_len, LANES), lambda p: (0, c * pairs + p))

    def bias_part(c):
        return pl.BlockSpec((1, LANES), lambda p: (0, c * pairs + p))

    def whole(*shape):
        return pl.BlockSpec(shape, lambda p: (0, 0))

    table = whole(full_len, LANES)
    return call(
        attn_kernel,
        deps,
        (proj, proj, proj, bias, bias, bias, *tables, segment.reshape(1, -1), segment.reshape(-1, 1)),
        grid=(pairs,),
        in_specs=[part(0), part(1), part(2), bias_part(0), bias_part(1), bias_part(2), table, table, table,
                  whole(1, full_len), whole(full_len, 1)],
        out_specs=[
            pl.BlockSpec((full_len, LANES), lambda p: (0, p)),
            pl.BlockSpec((3, full_len, LANES), lambda p: (0, 0, p)),
            pl.BlockSpec((8, full_len), lambda p: (p, 0)),
        ],
        out_shape=[
            jax.ShapeDtypeStruct((full_len, width), bf16),
            jax.ShapeDtypeStruct((3, full_len, width), bf16),
            jax.ShapeDtypeStruct((8 * pairs, full_len), f32),
        ],
        name="attention",
    )


def attn_grad_kernel(
    keep_ref, log_ref, ao_ref, ga_ref, cos_ref, sa_ref, sb_ref, segr_ref, segc_ref, dp_ref, db_ref, dk_acc, dv_acc
):
    full_len = ao_ref.shape[0]
    size = min(256, full_len)
    half = ROT // 2
    heads = LANES // HEAD_DIM
    cos, sa, sb = cos_ref[...], sa_ref[...], sb_ref[...]

    def unrope(g):
        return g * cos + pltpu.roll(g * sa, half, 1) + pltpu.roll(g * sb, LANES - half, 1)

    lane = lax.broadcasted_iota(jnp.int32, (1, LANES), 1)
    q, k, v, do = keep_ref[0], keep_ref[1], keep_ref[2], ga_ref[...]
    k_t = k.astype(f32).T.astype(bf16)
    inner_t = (do.astype(f32) * ao_ref[...].astype(f32)).T
    tri = lax.broadcasted_iota(jnp.int32, (size, size), 0) <= lax.broadcasted_iota(jnp.int32, (size, size), 1)
    zero = jnp.zeros((), bf16)
    dq_blocks = []
    for j in range(full_len // size):
        cols = slice(j * size, (j + 1) * size)
        seg_q = segr_ref[:, cols]
        spans, masks, queries, grads, logs, inners = [], [], [], [], [], []
        for h in range(heads):
            mine = (lane >= h * HEAD_DIM) & (lane < (h + 1) * HEAD_DIM)
            spans.append(slice(h * HEAD_DIM, (h + 1) * HEAD_DIM))
            queries.append(jnp.where(mine, q[cols], zero))
            grads.append(jnp.where(mine, do[cols], zero))
            logs.append(log_ref[h : h + 1, cols])
            inners.append(jnp.sum(inner_t[spans[h], cols], 0, keepdims=True))
        dq = [None] * heads
        for i in range(j + 1):
            rows = slice(i * size, (i + 1) * size)
            ok = segc_ref[rows] == seg_q
            if i == j:
                ok = ok & tri
            dv = dk = None
            for h in range(heads):
                p = jnp.exp(jnp.where(ok, mm(k[rows], queries[h], NT) - logs[h], masked_score))
                g = (p * (mm(v[rows], grads[h], NT) - inners[h])).astype(bf16)
                t = mm(p.astype(bf16), grads[h])
                dv = t if dv is None else dv + t
                t = mm(g, queries[h])
                dk = t if dk is None else dk + t
                t = mm(k_t[spans[h], rows], g)
                dq[h] = t if dq[h] is None else dq[h] + t
            if i == j:
                dv_acc[rows] = dv
                dk_acc[rows] = dk
            else:
                dv_acc[rows] += dv
                dk_acc[rows] += dk
        dq_blocks.append((jnp.concatenate(dq, 0) * (HEAD_DIM**-0.5)).T)
    dq = unrope(jnp.concatenate(dq_blocks, 0)).astype(bf16)
    dk = unrope(dk_acc[...]).astype(bf16)
    dv = dv_acc[...].astype(bf16)
    for part, g in enumerate((dq, dk, dv)):
        dp_ref[part] = g
        db_ref[part : part + 1] = jnp.sum(g.astype(f32), 0, keepdims=True)


def attention_grad(keep, logs, attn, grad_attn, tables, segment, deps=()):
    _, full_len, width = keep.shape

    def whole(*shape):
        return pl.BlockSpec(shape, lambda p: (0, 0))

    table = whole(full_len, LANES)
    cols = pl.BlockSpec((full_len, LANES), lambda p: (0, p))
    three = pl.BlockSpec((3, full_len, LANES), lambda p: (0, 0, p))
    return call(
        attn_grad_kernel,
        deps,
        (keep, logs, attn, grad_attn, *tables, segment.reshape(1, -1), segment.reshape(-1, 1)),
        grid=(width // LANES,),
        in_specs=[three, pl.BlockSpec((8, full_len), lambda p: (p, 0)), cols, cols, table, table, table,
                  whole(1, full_len), whole(full_len, 1)],
        out_specs=[three, pl.BlockSpec((8, LANES), lambda p: (0, p))],
        out_shape=[jax.ShapeDtypeStruct((3, full_len, width), bf16), jax.ShapeDtypeStruct((8, width), f32)],
        scratch=[pltpu.VMEM((full_len, LANES), f32), pltpu.VMEM((full_len, LANES), f32)],
        name="attention_grad",
    )


def act_kernel(n_ref, up_ref, bias_ref, act_ref, slope_ref):
    rows = n_ref.shape[0]
    step = min(256, rows)
    k0 = 0.7978845608028654
    k1 = k0 * 0.044715
    for i in range(rows // step):
        at = slice(i * step, (i + 1) * step)
        v = mm(n_ref[at], up_ref[...]) + bias_ref[...]
        v2 = v * v
        t = jnp.tanh(v * (k0 + k1 * v2))
        h = 0.5 * t + 0.5
        act_ref[at] = (v * h).astype(bf16)
        slope_ref[at] = (h + v * (1.0 - t * t) * (0.5 * k0 + 1.5 * k1 * v2)).astype(bf16)


def mlp_act(n, up, bias, deps=()):
    rows, depth = n.shape
    near, _, hidden = up.shape
    br, bh = min(1024, rows), min(512, hidden)
    per = hidden // bh
    out = pl.BlockSpec((br, bh), lambda j, i: (i, j))
    shape = jax.ShapeDtypeStruct((rows, near * hidden), bf16)
    return call(
        act_kernel,
        deps,
        (n, up, bias.reshape(1, -1)),
        grid=(near * per, rows // br),
        in_specs=[pl.BlockSpec((br, depth), lambda j, i: (i, 0)),
                  pl.BlockSpec((None, depth, bh), lambda j, i: (j // per, 0, j % per)),
                  pl.BlockSpec((1, bh), lambda j, i: (0, j))],
        out_specs=[out, out],
        out_shape=[shape, shape],
        name="mlp_act",
    )


def pre_kernel(c_ref, down_ref, slope_ref, pre_ref, sum_ref):
    rows = c_ref.shape[0]
    step = min(256, rows)
    total = None
    for i in range(rows // step):
        at = slice(i * step, (i + 1) * step)
        p = (mm(c_ref[at], down_ref[...]) * slope_ref[at].astype(f32)).astype(bf16)
        pre_ref[at] = p
        s = jnp.sum(p.astype(f32), 0, keepdims=True)
        total = s if total is None else total + s
    sum_ref[...] = jnp.broadcast_to(total, sum_ref.shape)


def mlp_pre(c, down_t, slope, deps=()):
    rows, depth = c.shape
    near, _, hidden = down_t.shape
    br, bh = min(1024, rows), min(512, hidden)
    per = hidden // bh
    out = pl.BlockSpec((br, bh), lambda j, i: (i, j))
    pre, sums = call(
        pre_kernel,
        deps,
        (c, down_t, slope),
        grid=(near * per, rows // br),
        in_specs=[pl.BlockSpec((br, depth), lambda j, i: (i, 0)),
                  pl.BlockSpec((None, depth, bh), lambda j, i: (j // per, 0, j % per)), out],
        out_specs=[out, pl.BlockSpec((8, bh), lambda j, i: (i, j))],
        out_shape=[
            jax.ShapeDtypeStruct((rows, near * hidden), bf16),
            jax.ShapeDtypeStruct((rows // br * 8, near * hidden), f32),
        ],
        name="mlp_pre",
    )
    return pre, jnp.sum(sums.reshape(-1, 8, near * hidden)[:, 0], 0)


def mixed_kernel(act_ref, attn_ref, down_ref, dense_ref, out_ref):
    rows = act_ref.shape[0]
    near, _, hidden = down_ref.shape
    step = min(512, rows)
    for i in range(rows // step):
        at = slice(i * step, (i + 1) * step)
        total = mm(attn_ref[at], dense_ref[...], NT)
        for r in range(near):
            total = total + mm(act_ref[at, r * hidden : (r + 1) * hidden], down_ref[r], NT)
        out_ref[at] = total.astype(bf16)


def mixed_part(act, attn, down_t, dense_t, deps=()):
    rows = act.shape[0]
    width = attn.shape[1]
    near, depth, hidden = down_t.shape
    br, bn = min(1024, rows), min(512, depth)
    return call(
        mixed_kernel,
        deps,
        (act, attn, down_t, dense_t),
        grid=(depth // bn, rows // br),
        in_specs=[pl.BlockSpec((br, near * hidden), lambda j, i: (i, 0)), pl.BlockSpec((br, width), lambda j, i: (i, 0)),
                  pl.BlockSpec((near, bn, hidden), lambda j, i: (0, j, 0)), pl.BlockSpec((bn, width), lambda j, i: (j, 0))],
        out_specs=pl.BlockSpec((br, bn), lambda j, i: (i, j)),
        out_shape=jax.ShapeDtypeStruct((rows, depth), bf16),
        name="mixed_part",
    )


def back_kernel(pre_ref, dp_ref, up_ref, qkv_ref, n_ref, out_ref, sum_ref):
    rows = pre_ref.shape[0]
    near, _, hidden = up_ref.shape
    parts, _, width = dp_ref.shape
    step = min(512, rows)
    plain = scaled = None
    for i in range(rows // step):
        at = slice(i * step, (i + 1) * step)
        total = None
        for r in range(near):
            t = mm(pre_ref[at, r * hidden : (r + 1) * hidden], up_ref[r], NT)
            total = t if total is None else total + t
        for c in range(parts):
            total = total + mm(dp_ref[c, at], qkv_ref[:, c * width : (c + 1) * width], NT)
        out_ref[at] = total.astype(bf16)
        a = jnp.sum(total, 0, keepdims=True)
        b = jnp.sum(total * n_ref[at].astype(f32), 0, keepdims=True)
        plain = a if plain is None else plain + a
        scaled = b if scaled is None else scaled + b
    sum_ref[0:1] = plain
    sum_ref[1:2] = scaled


def back_part(pre, dp, up, qkv, n, deps=()):
    rows = pre.shape[0]
    parts, _, width = dp.shape
    near, depth, hidden = up.shape
    br, bn = min(1024, rows), min(512, depth)
    out, sums = call(
        back_kernel,
        deps,
        (pre, dp, up, qkv, n),
        grid=(depth // bn, rows // br),
        in_specs=[pl.BlockSpec((br, near * hidden), lambda j, i: (i, 0)), pl.BlockSpec((parts, br, width), lambda j, i: (0, i, 0)),
                  pl.BlockSpec((near, bn, hidden), lambda j, i: (0, j, 0)), pl.BlockSpec((bn, parts * width), lambda j, i: (j, 0)),
                  pl.BlockSpec((br, bn), lambda j, i: (i, j))],
        out_specs=[pl.BlockSpec((br, bn), lambda j, i: (i, j)), pl.BlockSpec((8, bn), lambda j, i: (i, j))],
        out_shape=[jax.ShapeDtypeStruct((rows, depth), bf16), jax.ShapeDtypeStruct((rows // br * 8, depth), f32)],
        name="back_part",
    )
    return out, jnp.sum(sums.reshape(-1, 8, depth)[:, :2], 0)


def store_quarters(at_ref, total, held, keep_ref, send_ref):
    held[...] = total.astype(bf16)
    rows = held.shape[0] // 4
    y, core = at_ref[0], at_ref[1]
    for d in range(2):
        row = 2 * (1 - y if d else y)
        keep_ref[d] = held[pl.ds(pl.multiple_of((row + core) * rows, rows), rows)]
        send_ref[d] = held[pl.ds(pl.multiple_of((row + 1 - core) * rows, rows), rows)]


def weight_grad(at, xs, ys, deps=()):
    rows, m = xs[0].shape
    hidden = ys[0].shape[1] // 2
    tile = min(hidden, 512)
    per = hidden // tile
    count = len(xs)

    def kernel(at_ref, *refs):
        total = None
        for x, y in zip(refs[:count], refs[count : 2 * count], strict=True):
            t = mm(x[...], y[...], TN)
            total = t if total is None else total + t
        keep_ref, send_ref, held = refs[2 * count :]
        store_quarters(at_ref, total, held, keep_ref, send_ref)

    x_spec = pl.BlockSpec((rows, m), lambda j, at: (0, 0), pipeline_mode=pl.Buffered(1))
    y_spec = pl.BlockSpec((rows, tile), lambda j, at: (0, j))
    out = pl.BlockSpec((None, 2, m // 4, tile), lambda j, at: (j // per, 0, 0, j % per))
    shape = jax.ShapeDtypeStruct((2, 2, m // 4, hidden), bf16)
    return call(
        kernel,
        deps,
        (at, *xs, *ys),
        grid=(2 * per,),
        in_specs=[x_spec] * count + [y_spec] * count,
        out_specs=[out, out],
        out_shape=[shape, shape],
        scratch=[pltpu.VMEM((m, tile), bf16)],
        prefetch=1,
        name="weight_grad",
    )


def heads_grad(at, ns, dps, cs, attns, deps=()):
    parts, rows, wide = dps[0].shape
    m = ns[0].shape[1]
    width = wide // 2
    count = len(ns)
    out_cols = (parts + 1) * width
    if width % LANES:
        blocks = [sum(mm(n, dp[c], TN) for n, dp in zip(ns, dps, strict=True)) for c in range(parts)]
        blocks.append(sum(mm(c, a, TN) for c, a in zip(cs, attns, strict=True)))
        g = jnp.stack([jnp.concatenate([b[:, r * width : (r + 1) * width] for b in blocks], 1) for r in range(2)], 0)
        g = g.astype(bf16).reshape(2, 2, 2, m // 4, out_cols)
        g = jnp.where(at[0] == 0, g, g[:, ::-1])
        return jnp.where(at[1] == 0, g[:, :, 0], g[:, :, 1]), jnp.where(at[1] == 0, g[:, :, 1], g[:, :, 0])

    def kernel(at_ref, *refs):
        n_refs, dp_refs, c_refs, a_refs = (refs[i * count : (i + 1) * count] for i in range(4))
        keep_ref, send_ref, held = refs[4 * count :]
        part = pl.program_id(0)

        def store(total):
            for d in range(2):
                store_quarters(at_ref, total[:, d * width : (d + 1) * width], held, keep_ref.at[d], send_ref.at[d])

        @pl.when(part < parts)
        def _():
            store(sum(mm(n[...], d[...], TN) for n, d in zip(n_refs, dp_refs, strict=True)))

        @pl.when(part == parts)
        def _():
            store(sum(mm(c[...], a[...], TN) for c, a in zip(c_refs, a_refs, strict=True)))

    x_spec = pl.BlockSpec((rows, m), lambda p, at: (0, 0), pipeline_mode=pl.Buffered(1))
    dp_spec = pl.BlockSpec((None, rows, wide), lambda p, at: (jnp.minimum(p, parts - 1), 0, 0))
    a_spec = pl.BlockSpec((rows, wide), lambda p, at: (0, 0))
    out = pl.BlockSpec((2, 2, m // 4, width), lambda p, at: (0, 0, 0, p))
    shape = jax.ShapeDtypeStruct((2, 2, m // 4, out_cols), bf16)
    return call(
        kernel,
        deps,
        (at, *ns, *dps, *cs, *attns),
        grid=(parts + 1,),
        in_specs=[x_spec] * count + [dp_spec] * count + [x_spec] * count + [a_spec] * count,
        out_specs=[out, out],
        out_shape=[shape, shape],
        scratch=[pltpu.VMEM((m, width), bf16)],
        prefetch=1,
        name="heads_grad",
    )


SWAP = [(0, 1), (1, 0)]
FOLD = ("batch", "branch")


def flip(a, axis):
    return lax.ppermute(a, axis, SWAP)


def pick(a, index, axis=0):
    return lax.dynamic_index_in_dim(a, index, axis, keepdims=False)


def block_row(at_ref, k):
    y, core = at_ref[0], at_ref[1]
    chip, other = k // 2, k % 2
    return chip % 2, 2 * (1 - y if chip // 2 else y) + (1 - core if other else core)


def assemble(blocks, at, deps=()):
    rows, cols = blocks[0].shape
    tile = 256 if cols % 256 == 0 else cols

    def kernel(at_ref, *refs):
        for k in range(8):
            d, row = block_row(at_ref, k)
            refs[8][d, pl.ds(pl.multiple_of(row * rows, rows), rows)] = refs[k][...]

    return call(
        kernel,
        deps,
        (at, *blocks),
        grid=(cols // tile,),
        in_specs=[pl.BlockSpec((rows, tile), lambda j, at: (0, j))] * 8,
        out_specs=pl.BlockSpec((2, 4 * rows, tile), lambda j, at: (0, 0, j)),
        out_shape=jax.ShapeDtypeStruct((2, 4 * rows, cols), blocks[0].dtype),
        prefetch=1,
        name="assemble",
    )


def assemble_heads(blocks, at, parts, width, deps=()):
    rows, cols = blocks[0].shape
    hidden = cols - (parts + 1) * width
    if width % LANES:
        w = assemble(blocks, at)
        columns = [w[r, :, c * width : (c + 1) * width] for c in range(parts + 1) for r in range(2)]
        return jnp.concatenate(columns[: 2 * parts], 1), jnp.concatenate(columns[2 * parts :], 1), w[:, :, cols - hidden :]

    def kernel(at_ref, *refs):
        qkv_ref, dense_ref, up_ref = refs[8:]
        j = pl.program_id(0)
        for k in range(8):
            d, row = block_row(at_ref, k)
            at = pl.ds(pl.multiple_of(row * rows, rows), rows)
            for d_k in range(2):
                if d_k != d:
                    continue

                @pl.when(j < parts)
                def _():
                    qkv_ref[at, d_k * width : (d_k + 1) * width] = refs[k][...]

                @pl.when(j == parts)
                def _():
                    dense_ref[at, d_k * width : (d_k + 1) * width] = refs[k][...]

                @pl.when(j > parts)
                def _():
                    up_ref[d_k, at] = refs[k][...]

    depth = 4 * rows
    return call(
        kernel,
        deps,
        (at, *blocks),
        grid=(cols // width,),
        in_specs=[pl.BlockSpec((rows, width), lambda j, at: (0, j))] * 8,
        out_specs=[
            pl.BlockSpec((depth, 2 * width), lambda j, at: (0, jnp.minimum(j, parts - 1))),
            pl.BlockSpec((depth, 2 * width), lambda j, at: (0, 0)),
            pl.BlockSpec((2, depth, width), lambda j, at: (0, 0, jnp.maximum(j - parts - 1, 0))),
        ],
        out_shape=[
            jax.ShapeDtypeStruct((depth, 2 * parts * width), bf16),
            jax.ShapeDtypeStruct((depth, 2 * width), bf16),
            jax.ShapeDtypeStruct((2, depth, hidden), bf16),
        ],
        prefetch=1,
        name="assemble_heads",
    )


class Gather:
    def __init__(self, w):
        self.w = w
        self.half = w.shape[0] // 2
        self.blocks = [w, flip(w, "branch")]

    def first(self, *deps):
        w = tie(self.w, *deps) if deps else self.w
        self.x, self.y = flip(w, "near"), flip(w, "batch")

    def second(self, *deps):
        if deps:
            self.x, self.y = (tie(a, *deps) for a in (self.x, self.y))
        self.halves = self.y[: self.half], self.x[self.half :]
        self.corner = flip(self.halves[0], "near"), flip(self.halves[1], "batch")

    def third(self):
        for b in (self.x, self.y, jnp.concatenate(self.corner, 0)):
            self.blocks += [b, flip(b, "branch")]
        return self.blocks


class Scatter:
    def __init__(self, keep, send):
        self.keep, self.got = keep, flip(send, "branch")
        self.half = keep.shape[2] // 2

    def first(self, *deps):
        core = tie(self.got, *deps) if deps else self.got
        own, to_y, to_x, corner = ((self.keep[i, j], core[i, j]) for i, j in ((0, 0), (0, 1), (1, 0), (1, 1)))
        self.own, self.to_y, self.to_x = own, to_y, to_x
        corner = corner[0] + corner[1]
        self.got = flip(corner[: self.half], "near"), flip(corner[self.half :], "batch")
        return (corner,)

    def second(self, *deps):
        h = self.half
        got = tuple(tie(a, *deps) for a in self.got) if deps else self.got
        to_y, to_x = self.to_y[0] + self.to_y[1], self.to_x[0] + self.to_x[1]
        to_y = jnp.concatenate([to_y[:h] + got[0], to_y[h:]], 0)
        to_x = jnp.concatenate([to_x[:h], to_x[h:] + got[1]], 0)
        self.got = flip(to_x, "near"), flip(to_y, "batch")
        return to_x, to_y

    def result(self, *deps):
        got = tuple(tie(a, *deps) for a in self.got) if deps else self.got
        return sum(a.astype(f32) for a in (*self.own, *got))


def norm_grad(at, tokens, cotangent, kept, got, gain, s, into=None):
    shard, depth = tokens.shape[2:]
    both = kept is not None and got is not None
    at = jnp.concatenate([at, at if got is None else 1 - at])
    kept, got = (got if kept is None else kept), (kept if got is None else got)
    tile = min(32, shard)

    def kernel(at_ref, x_ref, c_ref, kept_ref, got_ref, gain_ref, *refs):
        x = x_ref[...].astype(f32)
        centered = x - jnp.mean(x, -1, keepdims=True)
        scale = lax.rsqrt(jnp.mean(centered * centered, -1, keepdims=True) + eps_norm)
        unit = centered * scale
        grad = kept_ref[...].astype(f32)
        if both:
            grad = jnp.where(pl.program_id(0) == at_ref[0], grad, got_ref[...].astype(f32))
        w = grad * gain_ref[...]
        refs[-1][...] = c_ref[...].astype(f32) + scale * (
            w - jnp.mean(w, -1, keepdims=True) - unit * jnp.mean(w * unit, -1, keepdims=True)
        )

    block = pl.BlockSpec((None, None, tile, depth), lambda m, i, at: (m if both else at[1], s, i, 0))
    rows = pl.BlockSpec((tile, depth), lambda m, i, at: (i, 0))
    extra = [] if into is None else [into]
    return pl.pallas_call(
        kernel,
        grid_spec=pltpu.PrefetchScalarGridSpec(
            num_scalar_prefetch=1,
            grid=(2 if both else 1, shard // tile),
            in_specs=[block, block, rows, rows, pl.BlockSpec((1, depth), lambda m, i, at: (0, 0))]
            + [pl.BlockSpec(memory_space=pl.ANY)] * len(extra),
            out_specs=block,
        ),
        out_shape=jax.ShapeDtypeStruct(tokens.shape, f32),
        input_output_aliases={6: 0} if extra else {},
        compiler_params=pltpu.CompilerParams(vmem_limit_bytes=VMEM),
        cost_estimate=cost(3),
        name="norm_grad",
    )(at, tokens, cotangent, kept, got, gain.reshape(1, -1), *extra)


def body(
    line_size,
    tokens,
    cotangent,
    segments,
    positions,
    ln_gain,
    ln_bias,
    qkv_weight,
    qkv_bias,
    dense_weight,
    dense_bias,
    up_weight,
    up_bias,
    down_weight,
    down_bias,
):
    micros, seqs, shard, depth = tokens.shape
    full_len = segments.shape[2]
    quarter, parts, width = qkv_weight.shape
    hidden = up_weight.shape[1]
    x, y, core, z = (lax.axis_index(a) for a in ("near", "batch", "branch", "line"))
    first = x == 0

    def to_group(a, start=(), end=()):
        send = jnp.where(first, a[1], a[0])
        got = flip(tie(send, *start) if start else send, "near")
        kept = jnp.where(first, a[0], a[1])
        got = tie(got, *end) if end else got
        return jnp.concatenate([jnp.where(first, kept, got), jnp.where(first, got, kept)], 0)

    def from_group(a):
        lo, hi = a[:shard], a[shard:]
        send = jnp.where(first, hi, lo)
        got = flip(send, "near")

        def finish(*deps, by_micro=True):
            other = tie(got, *deps) if deps else got
            kept = jnp.where(first, lo, hi)
            if not by_micro:
                return kept, other
            return jnp.where(first, kept, other), jnp.where(first, other, kept)

        return send, finish

    at = jnp.stack([y, core]).astype(jnp.int32)

    units, scales, groups_n, groups_c = [], [], [], []
    for s in range(seqs):
        r = tokens[:, s].astype(f32)
        centered = r - jnp.mean(r, -1, keepdims=True)
        scales.append(lax.rsqrt(jnp.mean(centered * centered, -1, keepdims=True) + eps_norm))
        units.append(centered * scales[s])

    def normed(s):
        return (units[s] * ln_gain + ln_bias).astype(bf16)

    def gather_rows(group):
        return lax.all_gather(group, "line", axis=0, tiled=True)

    segment = jnp.where(first, segments[0], segments[1])
    place = jnp.where(first, positions[0], positions[1])
    tables = [rope_tables(place[s]) for s in range(seqs)]
    n_0 = to_group(normed(0))
    c_0 = to_group(cotangent[:, 0], (n_0,))
    rows_n, rows_c = [gather_rows(n_0)], [gather_rows(c_0)]
    early = Gather(jnp.concatenate([qkv_weight.reshape(quarter, parts * width), dense_weight.T, up_weight], 1))
    late = Gather(down_weight.T)
    early.first(c_0)
    early.second(*tables[0], *tables[1])
    late.first(*early.corner)
    qkv, dense_t, up = assemble_heads(early.third(), at, parts, width)
    bias_qkv = jnp.concatenate([qkv_bias, flip(qkv_bias, "near")], 1)
    bias_up = jnp.concatenate([up_bias, flip(up_bias, "near")], 0)

    def scatter_rows(part):
        return lax.psum_scatter(part, "line", scatter_dimension=0, tiled=True)

    proj = project(rows_n[0], qkv, f32)
    n_1 = to_group(normed(1), early.corner, (dense_t,))
    late.second(proj)
    attn_0, keep, log = attention(proj, bias_qkv, tables[0], segment[0], (n_1, *late.halves))
    rows_n.append(gather_rows(n_1))
    act_0, slope = mlp_act(rows_n[0], up, bias_up, (attn_0, *late.corner))
    down_t = assemble(late.third(), at, (act_0,))
    part = mixed_part(act_0, attn_0, down_t, dense_t)
    both = [part]
    c_1 = to_group(cotangent[:, 1], (act_0,), (part,))
    rows_c.append(gather_rows(c_1))
    grad_attn = project(rows_c[0], dense_t, bf16, (part, c_1))
    dp_0, db_0 = attention_grad(keep, log, attn_0, grad_attn, tables[0], segment[0])
    pre_0, up_0 = mlp_pre(rows_c[0], down_t, slope, (dp_0,))
    part, back_0 = back_part(pre_0, dp_0, up, qkv, rows_n[0])
    both = jnp.stack([a.reshape(line_size, 2 * shard, depth) for a in (*both, part)], 1)
    mixed_0, back_sum_0 = lax.psum_scatter(both, "line", scatter_dimension=0, tiled=False)
    proj = project(rows_n[1], qkv, f32, (part,))
    attn_1, keep, log = attention(proj, bias_qkv, tables[1], segment[1])
    act_1, slope = mlp_act(rows_n[1], up, bias_up, (attn_1,))
    pre_1, up_1 = mlp_pre(rows_c[1], down_t, slope)
    grad_up = Scatter(*weight_grad(at, rows_n, (pre_0, pre_1)))
    grad_down = Scatter(*weight_grad(at, rows_c, (act_0, act_1), (grad_up.keep,)))
    sends = grad_up.first(grad_down.keep)
    part = mixed_part(act_1, attn_1, down_t, dense_t, sends)
    mixed_1 = scatter_rows(part)
    grad_attn = project(rows_c[1], dense_t, bf16, (part,))
    dp_1, db_1 = attention_grad(keep, log, attn_1, grad_attn, tables[1], segment[1])
    sends = (*grad_up.second(dp_1), *grad_down.first(dp_1))
    part, back_1 = back_part(pre_1, dp_1, up, qkv, rows_n[1], sends)
    back_sum_1 = scatter_rows(part)
    sends = grad_down.second(part)
    grad_up = grad_up.result()
    grad_heads = Scatter(*heads_grad(at, rows_n, (dp_0, dp_1), rows_c, (attn_0, attn_1), (*sends, grad_up)))
    grad_down = grad_down.result(grad_heads.keep)
    sum_qkv = (db_0 + db_1)[:parts].reshape(parts, 2, width)
    sum_up = (up_0 + up_1).reshape(2, hidden)
    out_bias = jnp.sum(cotangent, (0, 1, 2), dtype=f32)
    own, other = (jnp.concatenate([sum_qkv[:, d].reshape(-1), sum_up[d]]) for d in range(2))
    rest = jnp.concatenate([(back_0 + back_1).reshape(-1), out_bias])
    size = own.shape[0]
    sums = jnp.concatenate([own, rest]) + tie(flip(jnp.concatenate([other, rest]), "near"), grad_heads.keep)
    got = flip(sums, "batch")
    own_heads = grad_heads.first(tie(grad_down[:8, :LANES], sums, units=200))
    sums = sums + tie(got, *own_heads)
    _, finish_m = from_group(tie(mixed_0, *own_heads))
    _, finish = from_group(tie(back_sum_0, *own_heads))
    sums = sums + flip(sums, "branch")
    sends = grad_heads.second(sums)
    mixed_0 = finish_m(*sends)
    back_sum_0 = finish(*sends, by_micro=False)
    mixed_1 = from_group(tie(mixed_1, *back_sum_0))[1]()
    bias_sums, rest = sums[:size], tie(sums[size:], *sends)
    reach = 1
    while reach < line_size:
        rest = rest + lax.ppermute(rest, "line", [(i, i ^ reach) for i in range(line_size)])
        reach *= 2
    grad_down = grad_down.T
    grad_heads = grad_heads.result()
    grad_qkv = grad_heads[:, : parts * width].reshape(quarter, parts, width)
    grad_dense = grad_heads[:, parts * width :].T
    rest = rest.reshape(3, depth)
    shift_grad = rest[0]
    gain_grad = (rest[1] - ln_bias * shift_grad) / ln_gain

    near_at = x.astype(jnp.int32).reshape(1)
    tokens_grad = norm_grad(near_at, tokens, cotangent, *back_sum_0, ln_gain, 0)
    back_sum_1 = from_group(tie(back_sum_1, *mixed_1, rest))[1](by_micro=False)
    tokens_grad = norm_grad(near_at, tokens, cotangent, back_sum_1[0], None, ln_gain, 1, tokens_grad)
    tokens_grad = norm_grad(near_at, tokens, cotangent, None, back_sum_1[1], ln_gain, 1, tokens_grad)
    mixed = [
        (tokens[:, s].astype(f32) + jnp.stack(m, 0).astype(f32) + dense_bias + down_bias).astype(bf16)
        for s, m in enumerate((mixed_0, mixed_1))
    ]

    return (
        jnp.stack(mixed, 1),
        tokens_grad,
        gain_grad,
        shift_grad,
        grad_qkv,
        bias_sums[: parts * width].reshape(parts, width),
        grad_dense,
        rest[2],
        grad_up,
        bias_sums[parts * width :],
        grad_down,
        rest[2],
    )


def solution(mesh):
    batch, branch, tensor = (mesh.shape[a] for a in ("batch", "branch", "tensor"))
    inner = Mesh(mesh.devices.reshape(batch, branch, tensor // 2, 2), ("batch", "branch", "line", "near"))
    tensor = ("line", "near")
    rows = P(None, FOLD, tensor, None)
    first = P(FOLD, None, tensor)
    weights = (first, P(None, tensor), P(tensor, FOLD), P(), P(FOLD, tensor), P(tensor), P(tensor, FOLD), P())
    return jax.shard_map(
        partial(body, inner.shape["line"]),
        mesh=inner,
        in_specs=(rows, rows, P(None, FOLD, None), P(None, FOLD, None), P(), P(), *weights),
        out_specs=(rows, rows, P(), P(), *weights),
        check_vma=False,
    )
```
